128 devices in a mesh: gx: 4 (over y), gy: 4 (over z), gz: 8 (over x, core).
Axes of the slice: x: 4, y: 4, z: 4, core: 2. Of those that a mesh axis runs over, the one named last changes fastest.
Arguments:
- latent: bfloat16 [262144, 256], P(('gx', 'gy', 'gz')), may hold values from -6 to 6
- live_count: int32 [128], P(('gx', 'gy', 'gz')), may hold values from 640 to 2048, as said below
- leave_rows: int32 [16384], P(('gx', 'gy', 'gz')), may hold values from 0 to 2047, as said below
- leave_target: int32 [16384, 1], P(('gx', 'gy', 'gz')), may hold values from 0 to 127, as said below
- halo_rows: int32 [65536], P(('gx', 'gy', 'gz')), may hold values from 0 to 2303, as said below
- neighbours: int32 [294912, 24], P(('gx', 'gy', 'gz')), may hold values from -1 to 16127, as said below
- edge_in: bfloat16 [2, 2, 256, 256], replicated, may hold values from -0.25 to 0.25
- edge_bias: float32 [2, 256], replicated, may hold values from -3 to 3
- edge_out: bfloat16 [2, 256, 256], replicated, may hold values from -0.375 to 0.375
- edge_shift: float32 [2, 256], replicated, may hold values from -3 to 3
- edge_gain: float32 [2, 256], replicated, may hold values from 0.1 to 1.9
- node_in: bfloat16 [2, 2, 256, 256], replicated, may hold values from -0.25 to 0.25
- node_bias: float32 [2, 256], replicated, may hold values from -3 to 3
- node_out: bfloat16 [2, 256, 256], replicated, may hold values from -0.375 to 0.375
- node_shift: float32 [2, 256], replicated, may hold values from -3 to 3
- node_gain: float32 [2, 256], replicated, may hold values from 0.1 to 1.9
Outputs:
- updated: bfloat16 [294912, 256], P(('gx', 'gy', 'gz'))
The draws below stay inside these ranges and needn't reach their ends.
Inputs may be any that keep to these rules, and one draw needn't show every extreme that they name: `live_count`: every domain has at least 640 live slots; some domain has all 2048. `leave_rows`: the 128 entries of a domain are distinct slots below its live_count. `leave_target`: A domain number; one source sends at most 2 rows to one domain, and every source sends exactly 2 rows to some domain. A target may be the source itself. `halo_rows`: the 512 entries of a domain are distinct rows of its table that hold a particle. `neighbours`: -1 marks an empty slot. An index below 2304 is a row of the same table that holds a particle; 2304 + q * 512 + j is entry j of the boundary list of the domain at grid offset q (as in the reference program), never 13 and always inside the grid. Rows that hold no particle have only empty slots.
All inputs are finite; a program needn't handle non-finite values.
Results may differ from the reference program's by a relative error of at most 0.01.
Values may be sent and summed in bfloat16 or wider, within the bound.
A program may use at most 64 MiB of HBM per device.

```python
import jax
import jax.numpy as jnp
from jax import lax

D = 256
H = 256
P_SIZE = 2048
K = 24
STEPS = 2
CAP = 2
MIG = 128
B = 512
R = 2304
N_GX = 4
N_GY = 4
N_GZ = 8
DEVICES = 128


def domain_plan(key):
    key_list = jax.random.split(key, 12)
    devices = N_GX * N_GY * N_GZ
    lowest = MIG + B
    cube_base = jax.random.randint(key_list[0], (devices,), 0, 33)
    live_count = lowest + (P_SIZE - lowest) * cube_base * cube_base * cube_base // 32768
    fullest = jax.random.randint(key_list[1], (), 0, devices)
    live_count = live_count.at[fullest].set(P_SIZE).astype(jnp.int32)
    slot_index = jnp.arange(P_SIZE, dtype=jnp.int32)[None, :]
    scores = jax.random.randint(key_list[2], (devices, P_SIZE), 0, 1 << 20)
    scores = jnp.where(slot_index < live_count[:, None], scores, (1 << 20) + slot_index)
    leave_rows = jnp.argsort(scores, axis=1, stable=True)[:, :MIG].astype(jnp.int32)
    slots = devices * CAP
    slot_ids = jnp.arange(slots, dtype=jnp.int32)[None, :]
    slot_keys = jax.random.randint(key_list[3], (devices, slots), 0, 1 << 20)
    full_target = jax.random.randint(key_list[4], (devices, 1), 0, devices)
    slot_keys = jnp.where(slot_ids // CAP == full_target, slot_ids % CAP - CAP, slot_keys)
    chosen = jnp.argsort(slot_keys, axis=1, stable=True)[:, :MIG]
    shuffle = jnp.argsort(jax.random.randint(key_list[5], (devices, MIG), 0, 1 << 20), axis=1, stable=True)
    leave_target = (jnp.take_along_axis(chosen, shuffle, axis=1) // CAP).astype(jnp.int32)
    domain_ids = jnp.arange(devices, dtype=jnp.int32)
    per_pair = jnp.sum((leave_target[:, :, None] == domain_ids[None, None, :]).astype(jnp.int32), axis=1)
    arrivals = per_pair.T
    slot_rank = jnp.arange(CAP, dtype=jnp.int32)
    filled = (slot_rank[None, None, :] < arrivals[:, :, None]).reshape(devices, slots)
    departed = jnp.zeros((devices, P_SIZE), bool).at[domain_ids[:, None], leave_rows].set(True)
    local_live = jnp.logical_and(slot_index < live_count[:, None], jnp.logical_not(departed))
    occupied = jnp.concatenate([local_live, filled], axis=1)
    table_ids = jnp.arange(R, dtype=jnp.int32)[None, :]
    halo_keys = jax.random.randint(key_list[6], (devices, R), 0, 1 << 20)
    halo_keys = jnp.where(occupied, halo_keys, (1 << 20) + table_ids)
    halo_rows = jnp.argsort(halo_keys, axis=1, stable=True)[:, :B].astype(jnp.int32)
    live_order = jnp.argsort(jnp.where(local_live, 0, 1), axis=1, stable=True).astype(jnp.int32)
    live_total = live_count - MIG
    arrive_order = jnp.argsort(jnp.where(filled, 0, 1), axis=1, stable=True).astype(jnp.int32)
    arrive_total = jnp.sum(filled.astype(jnp.int32), axis=1)
    edge_shape = (devices, R, K)
    category = jax.random.randint(key_list[7], edge_shape, 0, 20)
    pick_local = jax.random.randint(key_list[8], edge_shape, 0, 1 << 20) % live_total[:, None, None]
    local_choice = jnp.take_along_axis(live_order, pick_local.reshape(devices, -1), axis=1).reshape(edge_shape)
    pick_arrive = jax.random.randint(key_list[9], edge_shape, 0, 1 << 20) % jnp.maximum(arrive_total, 1)[:, None, None]
    arrive_choice = P_SIZE + jnp.take_along_axis(arrive_order, pick_arrive.reshape(devices, -1), axis=1).reshape(edge_shape)
    direction = jax.random.randint(key_list[10], edge_shape, 0, 26)
    direction = direction + (direction >= 13).astype(jnp.int32)
    step_x = direction // 9 - 1
    step_y = direction // 3 % 3 - 1
    step_z = direction % 3 - 1
    place_x = (domain_ids // (N_GY * N_GZ))[:, None, None] + step_x
    place_y = (domain_ids // N_GZ % N_GY)[:, None, None] + step_y
    place_z = (domain_ids % N_GZ)[:, None, None] + step_z
    inside = (place_x >= 0) & (place_x < N_GX) & (place_y >= 0) & (place_y < N_GY) & (place_z >= 0) & (place_z < N_GZ)
    slot_pick = jax.random.randint(key_list[11], edge_shape, 0, B)
    ghost_choice = R + direction * B + slot_pick
    arrive_safe = jnp.where((arrive_total > 0)[:, None, None], arrive_choice, local_choice)
    ghost_safe = jnp.where(inside, ghost_choice, local_choice)
    picked = jnp.where(category < 10, local_choice, jnp.where(category < 12, arrive_safe, jnp.where(category < 18, ghost_safe, -1)))
    picked = jnp.where(occupied[:, :, None], picked, -1).astype(jnp.int32)
    return (live_count, leave_rows, leave_target, halo_rows, picked)


def draw_live_count(key, part):
    return domain_plan(key)[0]


def draw_leave_rows(key, part):
    return domain_plan(key)[1].reshape(-1)


def draw_leave_target(key, part):
    return domain_plan(key)[2].reshape(-1, 1)


def draw_halo_rows(key, part):
    return domain_plan(key)[3].reshape(-1)


def draw_neighbours(key, part):
    return domain_plan(key)[4].reshape(-1, K)


def steps_of(stream_key, extent, cuts, low, largest):
    gain = 1.0
    for dim, blocks in cuts:
        steps = jax.random.uniform(jax.random.fold_in(jax.random.fold_in(stream_key, 6), dim), (blocks,), jnp.float32, low / len(cuts), largest / len(cuts))
        gain = gain * jnp.repeat(jnp.exp(steps), extent[dim] // blocks).reshape((-1,) + (1,) * (len(extent) - 1 - dim))
    return gain


def normal_values(own_key, shape, width, most, cuts=(), kind=jnp.bfloat16):
    gain = steps_of(own_key, shape, cuts, -0.22, 0.18) if cuts else 1.0
    entries = jax.random.normal(own_key, shape, jnp.float32) * width * gain
    return jnp.minimum(jnp.maximum(entries, -most), most).astype(kind)


def setup_inputs(seed: int = 0) -> dict:
    key_of = jax.random.split(jax.random.key(seed), 17)
    return {
        "latent": normal_values(key_of[0], (DEVICES * P_SIZE, D), 1.0, 6.0, ((0, 128),)),
        "live_count": draw_live_count(jax.random.fold_in(key_of[16], 71), 0),
        "leave_rows": draw_leave_rows(jax.random.fold_in(key_of[16], 71), 0),
        "leave_target": draw_leave_target(jax.random.fold_in(key_of[16], 71), 0),
        "halo_rows": draw_halo_rows(jax.random.fold_in(key_of[16], 71), 0),
        "neighbours": draw_neighbours(jax.random.fold_in(key_of[16], 71), 0),
        "edge_in": normal_values(key_of[6], (STEPS, 2, D, H), (2 * D) ** -0.5, 0.25),
        "edge_bias": normal_values(key_of[7], (STEPS, H), 0.5, 3.0, (), jnp.float32),
        "edge_out": normal_values(key_of[8], (STEPS, H, D), H ** -0.5, 0.375),
        "edge_shift": normal_values(key_of[9], (STEPS, D), 0.5, 3.0, (), jnp.float32),
        "edge_gain": jnp.clip(1.0 + 0.18 * jax.random.normal(key_of[10], (STEPS, D), jnp.float32), 0.1, 1.9),
        "node_in": normal_values(key_of[11], (STEPS, 2, D, H), (2 * D) ** -0.5, 0.25),
        "node_bias": normal_values(key_of[12], (STEPS, H), 0.5, 3.0, (), jnp.float32),
        "node_out": normal_values(key_of[13], (STEPS, H, D), H ** -0.5, 0.375),
        "node_shift": normal_values(key_of[14], (STEPS, D), 0.5, 3.0, (), jnp.float32),
        "node_gain": jnp.clip(1.0 + 0.18 * jax.random.normal(key_of[15], (STEPS, D), jnp.float32), 0.1, 1.9),
    }


eps = 1e-05

def layer_norm(values, feature_gain):
    average = lax.optimization_barrier(jnp.mean(values, axis=-1, keepdims=True))
    centred = values - average
    spread = lax.optimization_barrier(jnp.mean(centred * centred, axis=-1, keepdims=True))
    return centred * lax.rsqrt(spread + eps) * feature_gain

def message_rows(node_table, senders, neighbour_ids, living, receive_weight, edge_bias, edge_out, edge_shift, edge_gain, node_self, node_message, node_bias, node_out, node_shift, node_gain):
    table_rows = node_table.shape[0]
    slot_count = neighbour_ids.shape[1]
    receive = jnp.dot(node_table, receive_weight, preferred_element_type=jnp.float32)
    present = neighbour_ids >= 0
    picked = jnp.take(senders, jnp.where(present, neighbour_ids, 0), axis=0)
    edge_input = receive[:, None, :] + picked.astype(jnp.float32) + edge_bias
    active = jnp.maximum(edge_input, 0.0).astype(jnp.bfloat16).reshape(table_rows * slot_count, -1)
    edge_raw = jnp.dot(active, edge_out, preferred_element_type=jnp.float32) + edge_shift
    message = layer_norm(edge_raw, edge_gain).reshape(table_rows, slot_count, -1)
    summed = lax.optimization_barrier(jnp.sum(message * present[:, :, None].astype(jnp.float32), axis=1)).astype(jnp.bfloat16)
    hidden = jnp.dot(node_table, node_self, preferred_element_type=jnp.float32) + jnp.dot(summed, node_message, preferred_element_type=jnp.float32) + node_bias
    hidden = jnp.maximum(hidden, 0.0).astype(jnp.bfloat16)
    node_raw = jnp.dot(hidden, node_out, preferred_element_type=jnp.float32) + node_shift
    renewed = (node_table.astype(jnp.float32) + layer_norm(node_raw, node_gain)) * living[:, None]
    return renewed.astype(jnp.bfloat16)

def reference(latent, live_count, leave_rows, leave_target, halo_rows, neighbours, edge_in, edge_bias, edge_out, edge_shift, edge_gain, node_in, node_bias, node_out, node_shift, node_gain):
    devices = N_GX * N_GY * N_GZ
    feature_width = latent.shape[1]
    local = latent.reshape(devices, P_SIZE, feature_width)
    leaving = leave_rows.reshape(devices, MIG).astype(jnp.int32)
    target = leave_target.reshape(devices, MIG).astype(jnp.int32)
    order_rows = jnp.arange(MIG, dtype=jnp.int32)
    earlier = order_rows[None, :] < order_rows[:, None]
    same_target = target[:, :, None] == target[:, None, :]
    row_rank = lax.optimization_barrier(jnp.sum(jnp.logical_and(same_target, earlier[None]).astype(jnp.int32), axis=2))
    sources = jnp.arange(devices, dtype=jnp.int32)[:, None]
    placed = target * (devices * CAP) + sources * CAP + row_rank
    moving = jnp.take_along_axis(local, leaving[:, :, None], axis=1)
    arrived = jnp.zeros((devices * devices * CAP, feature_width), jnp.bfloat16).at[placed.reshape(-1)].set(moving.reshape(-1, feature_width))
    filled = jnp.zeros((devices * devices * CAP,), jnp.float32).at[placed.reshape(-1)].set(1.0)
    node_table = jnp.concatenate([local, arrived.reshape(devices, devices * CAP, feature_width)], axis=1)
    departed = jnp.zeros((devices, P_SIZE), jnp.float32).at[sources, leaving].set(1.0)
    slot_index = jnp.arange(P_SIZE, dtype=jnp.int32)[None, :]
    local_live = jnp.where(slot_index < live_count[:, None], 1.0 - departed, 0.0)
    living = jnp.concatenate([local_live, filled.reshape(devices, devices * CAP)], axis=1).astype(jnp.float32)
    coords = jnp.arange(devices, dtype=jnp.int32)
    place_x = coords // (N_GY * N_GZ)
    place_y = coords // N_GZ % N_GY
    place_z = coords % N_GZ
    zero_index = jnp.zeros((), jnp.int32)
    halo_index = halo_rows.reshape(devices, B).astype(jnp.int32)
    edge_lists = neighbours.reshape(devices, R, K)
    for step_index in range(STEPS):
        send_weight = edge_in[step_index, 1]

        def project(own_rows):
            return jnp.dot(own_rows, send_weight, preferred_element_type=jnp.float32).astype(jnp.bfloat16)
        projected = lax.map(project, node_table)
        boundary = jnp.take_along_axis(projected, halo_index[:, :, None], axis=1)
        padded_grid = jnp.pad(boundary.reshape(N_GX, N_GY, N_GZ, B, H), ((1, 1), (1, 1), (1, 1), (0, 0), (0, 0)))

        def per_domain(pieces):
            own_rows, own_projection, edge_ids, own_live, domain = pieces
            corner = (place_x[domain], place_y[domain], place_z[domain], zero_index, zero_index)
            beside_all = lax.dynamic_slice(padded_grid, corner, (3, 3, 3, B, H))
            senders = jnp.concatenate([own_projection, beside_all.reshape(27 * B, H)], axis=0)
            return message_rows(own_rows, senders, edge_ids, own_live, edge_in[step_index, 0], edge_bias[step_index], edge_out[step_index], edge_shift[step_index], edge_gain[step_index], node_in[step_index, 0], node_in[step_index, 1], node_bias[step_index], node_out[step_index], node_shift[step_index], node_gain[step_index])
        node_table = lax.map(per_domain, (node_table, projected, edge_lists, living, coords))
    return node_table.reshape(devices * R, feature_width)
```

```python
import functools

import jax
import jax.numpy as jnp
from jax import lax
from jax.experimental import pallas as pl
from jax.experimental.pallas import tpu as pltpu
from jax.sharding import PartitionSpec as P

EPS = 1e-05
F32 = jnp.float32
BF16 = jnp.bfloat16
HALF = 128
ROWS = 32
CHUNK = 256
GROUP = 8
NODE_ROWS = 256
VMEM_BYTES = 56 * 2**20


def layer_norm(values, feature_gain):
    average = jnp.mean(values, axis=-1, keepdims=True)
    centred = values - average
    spread = jnp.mean(centred * centred, axis=-1, keepdims=True)
    return centred * lax.rsqrt(spread + EPS) * feature_gain


def store_split(pairs, first_row, values):
    count = values.shape[0]
    pairs[pl.ds(2 * first_row, count, stride=2), :] = values[:, :HALF]
    pairs[pl.ds(2 * first_row + 1, count, stride=2), :] = values[:, HALF:]


def project_rows(pairs, first_row, rows, weight):
    projected = jnp.dot(rows, weight, preferred_element_type=F32).astype(BF16)
    store_split(pairs, first_row, projected.astype(F32))
    return projected


def pick_boundary(pairs, halo_ids, picked, boundary_ref):
    count = boundary_ref.shape[0]

    @pl.loop(0, count // 64)
    def _(block):
        for g in range(64 // GROUP):
            ids = halo_ids.at[pl.ds(block * 64 + g * GROUP, GROUP)]
            for e in range(GROUP):
                row = pl.multiple_of(ids[e], 2)
                picked[pl.ds(2 * (g * GROUP + e), 2), :] = pairs[pl.ds(row, 2), :]
        here = pl.ds(pl.multiple_of(block * 64, 64), 64)
        boundary_ref[here, :HALF] = picked[pl.ds(0, 64, stride=2), :].astype(BF16)
        boundary_ref[here, HALF:] = picked[pl.ds(1, 64, stride=2), :].astype(BF16)


def open_kernel(latent_ref, arrived_ref, halo_ids, weight_ref, table_ref, projected_ref, boundary_ref, pairs, picked):
    local_rows = latent_ref.shape[0]
    arrivals = arrived_ref.shape[0]

    @pl.loop(0, local_rows // NODE_ROWS)
    def _(i):
        first = pl.multiple_of(i * NODE_ROWS, NODE_ROWS)
        rows = latent_ref[pl.ds(first, NODE_ROWS), :]
        table_ref[pl.ds(first, NODE_ROWS), :] = rows
        projected_ref[pl.ds(first, NODE_ROWS), :] = project_rows(pairs, first, rows, weight_ref[...])

    rows = arrived_ref[...]
    table_ref[pl.ds(local_rows, arrivals), :] = rows
    projected_ref[pl.ds(local_rows, arrivals), :] = project_rows(pairs, local_rows, rows, weight_ref[...])
    pick_boundary(pairs, halo_ids, picked, boundary_ref)


def open_table(latent, arrived, halo_ids, weight):
    rows = latent.shape[0] + arrived.shape[0]
    width = latent.shape[1]
    count = halo_ids.shape[0]
    vmem = pl.BlockSpec(memory_space=pltpu.VMEM)
    return pl.pallas_call(
        open_kernel,
        out_shape=(
            jax.ShapeDtypeStruct((rows, width), BF16),
            jax.ShapeDtypeStruct((rows, width), BF16),
            jax.ShapeDtypeStruct((count, width), BF16),
        ),
        in_specs=[vmem, vmem, pl.BlockSpec(memory_space=pltpu.SMEM), vmem],
        out_specs=(vmem, vmem, vmem),
        scratch_shapes=[pltpu.VMEM((2 * rows, HALF), F32), pltpu.VMEM((2 * 64, HALF), F32)],
        compiler_params=pltpu.CompilerParams(vmem_limit_bytes=VMEM_BYTES),
        name="open_table",
    )(latent, arrived, halo_ids, weight)


def step_kernel(slots, last, *refs):
    (
        block_total,
        edge_ids,
        ghosts,
        table_ref,
        projected_ref,
        floor_ref,
        living_ref,
        receive_weight,
        edge_bias,
        edge_out,
        edge_shift,
        edge_gain,
        node_self,
        node_message,
        node_bias,
        node_out,
        node_shift,
        node_gain,
    ) = refs[:18]
    if last:
        (renewed_ref,) = refs[18:19]
        rest = refs[19:]
    else:
        halo_ids, next_weight, renewed_ref, next_projected, boundary_ref = refs[18:23]
        rest = refs[23:]
    pairs, even, odd, receive, summed, raw, square, weight, staged, picked, sems = rest
    rows = table_ref.shape[0]
    width = table_ref.shape[1]
    edges = slots * ROWS
    blocks = rows // ROWS
    gathered = (even, odd)
    ghost_blocks, ghost_rows = ghosts.shape[0], ghosts.shape[1]

    def fetch(block, slot):
        return pltpu.make_async_copy(ghosts.at[block], staged.at[slot], sems.at[slot])

    fetch(0, 0).start()

    @pl.loop(0, rows // NODE_ROWS)
    def _(i):
        first = pl.multiple_of(i * NODE_ROWS, NODE_ROWS)
        here = pl.ds(first, NODE_ROWS)
        store_split(pairs, first, projected_ref[here, :].astype(F32))
        receive[here, :] = (
            jnp.dot(table_ref[here, :], receive_weight[...], preferred_element_type=F32) + edge_bias[...]
        )

    wide = edge_out[...].astype(F32)
    weight[...] = (wide - jnp.mean(wide, axis=1, keepdims=True)).astype(BF16)
    shift = edge_shift[...] - jnp.mean(edge_shift[...], axis=1, keepdims=True)

    @pl.loop(0, ghost_blocks)
    def _(block):
        slot = lax.rem(block, 2)
        fetch(block, slot).wait()

        @pl.when(block + 1 < ghost_blocks)
        def _():
            fetch(block + 1, 1 - slot).start()

        for piece in range(ghost_rows // NODE_ROWS):
            values = staged[slot, pl.ds(piece * NODE_ROWS, NODE_ROWS), :].astype(F32)
            store_split(pairs, pl.multiple_of(rows + block * ghost_rows + piece * NODE_ROWS, NODE_ROWS), values)

    def gather(into, block, start, stop):
        base = pl.multiple_of(block * edges, HALF)
        for e in range(start, stop):
            if e % GROUP == 0:
                ids = edge_ids.at[pl.ds(base + e, GROUP)]
            row = pl.multiple_of(ids[e % GROUP], 2)
            into[pl.ds(2 * e, 2), :] = pairs[pl.ds(row, 2), :]

    per_chunk = CHUNK // ROWS

    def first_half(source, first, chunk):
        own = receive[pl.ds(first, ROWS), :]
        left = source[pl.ds(2 * chunk * CHUNK, CHUNK, stride=2), :].reshape(per_chunk, ROWS, HALF)
        right = source[pl.ds(2 * chunk * CHUNK + 1, CHUNK, stride=2), :].reshape(per_chunk, ROWS, HALF)
        left = jnp.maximum(left + own[:, :HALF][None], 0.0).reshape(CHUNK, HALF).astype(BF16)
        right = jnp.maximum(right + own[:, HALF:][None], 0.0).reshape(CHUNK, HALF).astype(BF16)
        active = jnp.concatenate([left, right], axis=1)
        centred = jnp.dot(active, weight[...], preferred_element_type=F32) + shift
        total = jnp.sum(
            centred[:, :HALF] * centred[:, :HALF] + centred[:, HALF:] * centred[:, HALF:], axis=1, keepdims=True
        )
        here = pl.ds(chunk * CHUNK, CHUNK)
        raw[here, :] = centred
        square[here, :] = jnp.broadcast_to(total, (CHUNK, HALF))

    def second_half(floor, chunk, sums):
        left, right = sums
        for k in range(chunk * per_chunk, (chunk + 1) * per_chunk):
            here = pl.ds(k * ROWS, ROWS)
            scale = lax.rsqrt(square[here, :] * (1.0 / width) + floor[:, k : k + 1])
            left = left + raw[here, :HALF] * scale
            right = right + raw[here, HALF:] * scale
        return left, right

    chunks = edges // CHUNK
    gather(even, 0, 0, edges)

    @pl.loop(0, blocks // 2)
    def _(pair):
        for parity in range(2):
            block = 2 * pair + parity

            @pl.when(block < block_total[0])
            def _():
                first = pl.multiple_of(block * ROWS, ROWS)
                following = jnp.minimum(block + 1, blocks - 1)
                floor = floor_ref[pl.ds(first, ROWS), :]
                sums = (jnp.zeros((ROWS, HALF), F32), jnp.zeros((ROWS, HALF), F32))
                for chunk in range(chunks + 1):
                    if chunk < chunks:
                        gather(gathered[1 - parity], following, chunk * CHUNK, (chunk + 1) * CHUNK)
                        first_half(gathered[parity], first, chunk)
                    if chunk > 0:
                        sums = second_half(floor, chunk - 1, sums)
                summed[pl.ds(first, ROWS), :HALF] = sums[0]
                summed[pl.ds(first, ROWS), HALF:] = sums[1]

    @pl.loop(0, rows // NODE_ROWS)
    def _(i):
        first = pl.multiple_of(i * NODE_ROWS, NODE_ROWS)
        here = pl.ds(first, NODE_ROWS)
        own = table_ref[here, :]
        message = (summed[here, :] * edge_gain[...]).astype(BF16)
        hidden = (
            jnp.dot(own, node_self[...], preferred_element_type=F32)
            + jnp.dot(message, node_message[...], preferred_element_type=F32)
            + node_bias[...]
        )
        hidden = jnp.maximum(hidden, 0.0).astype(BF16)
        node_raw = jnp.dot(hidden, node_out[...], preferred_element_type=F32) + node_shift[...]
        renewed = (own.astype(F32) + layer_norm(node_raw, node_gain[...])) * living_ref[here, :]
        renewed = renewed.astype(BF16)
        renewed_ref[here, :] = renewed
        if not last:
            next_projected[here, :] = project_rows(pairs, first, renewed, next_weight[...])

    if not last:
        pick_boundary(pairs, halo_ids, picked, boundary_ref)


def message_step(block_total, edge_ids, ghosts, table, projected, floor, living, weights, halo_ids=None, next_weight=None):
    last = halo_ids is None
    rows, width = table.shape
    slots = floor.shape[1]
    edges = slots * ROWS
    ghost_total = ghosts.shape[0] * ghosts.shape[1]
    vmem = pl.BlockSpec(memory_space=pltpu.VMEM)
    smem = pl.BlockSpec(memory_space=pltpu.SMEM)
    out_shape = [jax.ShapeDtypeStruct((rows, width), BF16)]
    extra, extra_specs = [], []
    if not last:
        count = halo_ids.shape[0]
        out_shape += [jax.ShapeDtypeStruct((rows, width), BF16), jax.ShapeDtypeStruct((count, width), BF16)]
        extra, extra_specs = [halo_ids, next_weight], [smem, vmem]
    return pl.pallas_call(
        functools.partial(step_kernel, slots, last),
        out_shape=tuple(out_shape),
        in_specs=[smem, smem, pl.BlockSpec(memory_space=pl.ANY)] + [vmem] * (4 + len(weights)) + extra_specs,
        out_specs=tuple([vmem] * len(out_shape)),
        scratch_shapes=[
            pltpu.VMEM((2 * (rows + ghost_total), HALF), F32),
            pltpu.VMEM((2 * edges, HALF), F32),
            pltpu.VMEM((2 * edges, HALF), F32),
            pltpu.VMEM((rows, width), F32),
            pltpu.VMEM((rows, width), F32),
            pltpu.VMEM((edges, width), F32),
            pltpu.VMEM((edges, HALF), F32),
            pltpu.VMEM((width, width), BF16),
            pltpu.VMEM((2, ghosts.shape[1], width), BF16),
            pltpu.VMEM((2 * 64, HALF), F32),
            pltpu.SemaphoreType.DMA((2,)),
        ],
        compiler_params=pltpu.CompilerParams(vmem_limit_bytes=VMEM_BYTES),
        name="message_step",
    )(block_total, edge_ids, ghosts, table, projected, floor, living, *weights, *extra)


def with_halo(x, sides, width):
    for axis, dim in sides:
        devices, length = (lax.axis_size(axis), x.shape[dim])
        up = [(i, i + 1) for i in range(devices - 1)]
        down = [(j, i) for i, j in up]
        last = lax.slice_in_dim(x, length - width, length, axis=dim)
        first = lax.slice_in_dim(x, 0, width, axis=dim)
        before = lax.ppermute(last, axis, up)
        after = lax.ppermute(first, axis, down)
        x = jnp.concatenate([before, x, after], axis=dim)
    return x


def exchange(boundary):
    count, width = boundary.shape
    spread = with_halo(boundary.reshape(1, 1, 1, count, width), (("gx", 0), ("gy", 1), ("gz", 2)), 1)
    return spread.reshape(-1, count, width)


def pick_rows(source_rows, row_ids):
    selector = (
        row_ids[:, None] == jnp.arange(source_rows.shape[0], dtype=jnp.int32)[None, :]
    ).astype(source_rows.dtype)
    return jnp.dot(selector, source_rows, preferred_element_type=F32).astype(source_rows.dtype)


def local(
    latent,
    live_count,
    leave_rows,
    leave_target,
    halo_rows,
    neighbours,
    edge_in,
    edge_bias,
    edge_out,
    edge_shift,
    edge_gain,
    node_in,
    node_bias,
    node_out,
    node_shift,
    node_gain,
):
    axes = ("gx", "gy", "gz")
    devices = lax.axis_size(axes)
    local_rows, width = latent.shape
    table_rows, slots = neighbours.shape
    slots_total = table_rows - local_rows
    capacity = slots_total // devices
    leaving = leave_rows.shape[0]
    target_domain = leave_target[:, 0]
    order_rows = jnp.arange(leaving, dtype=jnp.int32)
    earlier = order_rows[None, :] < order_rows[:, None]
    same_target = target_domain[:, None] == target_domain[None, :]
    row_rank = jnp.sum(jnp.logical_and(same_target, earlier).astype(jnp.int32), axis=1)
    position = target_domain * capacity + row_rank
    moving = pick_rows(latent, leave_rows)
    moving = jnp.concatenate([moving, jnp.ones((leaving, HALF), BF16)], axis=1)
    placement = jnp.arange(slots_total, dtype=jnp.int32)[:, None] == position[None, :]
    outgoing = jnp.dot(placement.astype(BF16), moving, preferred_element_type=F32).astype(BF16)
    arrived = lax.all_to_all(
        outgoing.reshape(devices, capacity, width + HALF), axes, split_axis=0, concat_axis=0, tiled=True
    ).reshape(slots_total, width + HALF)
    local_index = jnp.arange(local_rows, dtype=jnp.int32)
    departed = jnp.any(local_index[:, None] == leave_rows[None, :], axis=1)
    local_live = jnp.logical_and(local_index < live_count[0], jnp.logical_not(departed)).astype(F32)
    living = jnp.concatenate([local_live[:, None], arrived[:, width : width + 1].astype(F32)], axis=0)

    blocks = table_rows // ROWS
    edge_ids = 2 * jnp.maximum(neighbours, 0)
    edge_ids = edge_ids.reshape(blocks, ROWS, slots).transpose(0, 2, 1).reshape(-1)
    floor = jnp.where(neighbours >= 0, EPS, jnp.inf).astype(F32)
    block_total = jnp.full((1,), blocks, jnp.int32)
    halo_ids = 2 * halo_rows

    table, projected, boundary = open_table(latent, arrived[:, :width], halo_ids, edge_in[0, 1])
    steps = edge_in.shape[0]
    for t in range(steps):
        ghosts = exchange(boundary)
        weights = (
            edge_in[t, 0],
            edge_bias[t][None],
            edge_out[t],
            edge_shift[t][None],
            edge_gain[t][None],
            node_in[t, 0],
            node_in[t, 1],
            node_bias[t][None],
            node_out[t],
            node_shift[t][None],
            node_gain[t][None],
        )
        if t < steps - 1:
            table, projected, boundary = message_step(
                block_total, edge_ids, ghosts, table, projected, floor, living, weights, halo_ids, edge_in[t + 1, 1]
            )
        else:
            (table,) = message_step(block_total, edge_ids, ghosts, table, projected, floor, living, weights)
    return table


def solution(mesh):
    rows = P(("gx", "gy", "gz"))
    in_specs = (rows,) * 6 + (P(),) * 10
    return jax.shard_map(local, mesh=mesh, in_specs=in_specs, out_specs=rows, check_vma=False)
```

```python
import functools

import jax
import jax.numpy as jnp
from jax import lax
from jax.experimental import pallas as pl
from jax.experimental.pallas import tpu as pltpu
from jax.sharding import PartitionSpec as P

EPS = 1e-05
F32 = jnp.float32
BF16 = jnp.bfloat16
HALF = 128
ROWS = 32
CHUNK = 256
GROUP = 8
NODE_ROWS = 256
VMEM_BYTES = 56 * 2**20


def layer_norm(values, feature_gain):
    average = jnp.mean(values, axis=-1, keepdims=True)
    centred = values - average
    spread = jnp.mean(centred * centred, axis=-1, keepdims=True)
    return centred * lax.rsqrt(spread + EPS) * feature_gain


def store_split(pairs, first_row, values):
    count = values.shape[0]
    pairs[pl.ds(2 * first_row, count, stride=2), :] = values[:, :HALF]
    pairs[pl.ds(2 * first_row + 1, count, stride=2), :] = values[:, HALF:]


def project_rows(pairs, first_row, rows, weight):
    projected = jnp.dot(rows, weight, preferred_element_type=F32).astype(BF16)
    store_split(pairs, first_row, projected.astype(F32))
    return projected


def pick_boundary(pairs, halo_ids, picked, boundary_ref):
    count = boundary_ref.shape[0]

    @pl.loop(0, count // 64)
    def _(block):
        for g in range(64 // GROUP):
            ids = halo_ids.at[pl.ds(block * 64 + g * GROUP, GROUP)]
            for e in range(GROUP):
                row = pl.multiple_of(ids[e], 2)
                picked[pl.ds(2 * (g * GROUP + e), 2), :] = pairs[pl.ds(row, 2), :]
        here = pl.ds(pl.multiple_of(block * 64, 64), 64)
        boundary_ref[here, :HALF] = picked[pl.ds(0, 64, stride=2), :].astype(BF16)
        boundary_ref[here, HALF:] = picked[pl.ds(1, 64, stride=2), :].astype(BF16)


def open_kernel(latent_ref, arrived_ref, halo_ids, weight_ref, table_ref, projected_ref, boundary_ref, pairs, picked):
    local_rows = latent_ref.shape[0]
    arrivals = arrived_ref.shape[0]

    @pl.loop(0, local_rows // NODE_ROWS)
    def _(i):
        first = pl.multiple_of(i * NODE_ROWS, NODE_ROWS)
        rows = latent_ref[pl.ds(first, NODE_ROWS), :]
        table_ref[pl.ds(first, NODE_ROWS), :] = rows
        projected_ref[pl.ds(first, NODE_ROWS), :] = project_rows(pairs, first, rows, weight_ref[...])

    rows = arrived_ref[...]
    table_ref[pl.ds(local_rows, arrivals), :] = rows
    projected_ref[pl.ds(local_rows, arrivals), :] = project_rows(pairs, local_rows, rows, weight_ref[...])
    pick_boundary(pairs, halo_ids, picked, boundary_ref)


def open_table(latent, arrived, halo_ids, weight):
    rows = latent.shape[0] + arrived.shape[0]
    width = latent.shape[1]
    count = halo_ids.shape[0]
    vmem = pl.BlockSpec(memory_space=pltpu.VMEM)
    return pl.pallas_call(
        open_kernel,
        out_shape=(
            jax.ShapeDtypeStruct((rows, width), BF16),
            jax.ShapeDtypeStruct((rows, width), BF16),
            jax.ShapeDtypeStruct((count, width), BF16),
        ),
        in_specs=[vmem, vmem, pl.BlockSpec(memory_space=pltpu.SMEM), vmem],
        out_specs=(vmem, vmem, vmem),
        scratch_shapes=[pltpu.VMEM((2 * rows, HALF), F32), pltpu.VMEM((2 * 64, HALF), F32)],
        compiler_params=pltpu.CompilerParams(vmem_limit_bytes=VMEM_BYTES),
        name="open_table",
    )(latent, arrived, halo_ids, weight)


def step_kernel(slots, last, *refs):
    (
        block_total,
        edge_ids,
        ghosts,
        table_ref,
        projected_ref,
        floor_ref,
        living_ref,
        receive_weight,
        edge_bias,
        edge_out,
        edge_shift,
        edge_gain,
        node_self,
        node_message,
        node_bias,
        node_out,
        node_shift,
        node_gain,
    ) = refs[:18]
    if last:
        (renewed_ref,) = refs[18:19]
        rest = refs[19:]
    else:
        halo_ids, next_weight, renewed_ref, next_projected, boundary_ref = refs[18:23]
        rest = refs[23:]
    pairs, even, odd, receive, summed, raw, square, weight, staged, picked, sems = rest
    rows = table_ref.shape[0]
    width = table_ref.shape[1]
    edges = slots * ROWS
    blocks = rows // ROWS
    gathered = (even, odd)
    ghost_blocks, ghost_rows = ghosts.shape[0], ghosts.shape[1]

    centre = ghost_blocks // 2

    def fetch(block):
        return pltpu.make_async_copy(ghosts.at[block], staged.at[block], sems.at[block])

    for block in range(ghost_blocks):
        if block != centre:
            fetch(block).start()

    @pl.loop(0, rows // NODE_ROWS)
    def _(i):
        first = pl.multiple_of(i * NODE_ROWS, NODE_ROWS)
        here = pl.ds(first, NODE_ROWS)
        store_split(pairs, first, projected_ref[here, :].astype(F32))
        receive[here, :] = (
            jnp.dot(table_ref[here, :], receive_weight[...], preferred_element_type=F32) + edge_bias[...]
        )

    wide = edge_out[...].astype(F32)
    weight[...] = (wide - jnp.mean(wide, axis=1, keepdims=True)).astype(BF16)
    shift = edge_shift[...] - jnp.mean(edge_shift[...], axis=1, keepdims=True)

    @pl.loop(0, ghost_blocks)
    def _(block):
        @pl.when(block != centre)
        def _():
            fetch(block).wait()
            for piece in range(ghost_rows // NODE_ROWS):
                values = staged[block, pl.ds(piece * NODE_ROWS, NODE_ROWS), :].astype(F32)
                store_split(pairs, pl.multiple_of(rows + block * ghost_rows + piece * NODE_ROWS, NODE_ROWS), values)

    def gather(into, block, start, stop):
        base = pl.multiple_of(block * edges, HALF)
        for e in range(start, stop):
            if e % GROUP == 0:
                ids = edge_ids.at[pl.ds(base + e, GROUP)]
            row = pl.multiple_of(ids[e % GROUP], 2)
            into[pl.ds(2 * e, 2), :] = pairs[pl.ds(row, 2), :]

    per_chunk = CHUNK // ROWS

    def first_half(source, first, chunk):
        own = receive[pl.ds(first, ROWS), :]
        left = source[pl.ds(2 * chunk * CHUNK, CHUNK, stride=2), :].reshape(per_chunk, ROWS, HALF)
        right = source[pl.ds(2 * chunk * CHUNK + 1, CHUNK, stride=2), :].reshape(per_chunk, ROWS, HALF)
        left = jnp.maximum(left + own[:, :HALF][None], 0.0).reshape(CHUNK, HALF).astype(BF16)
        right = jnp.maximum(right + own[:, HALF:][None], 0.0).reshape(CHUNK, HALF).astype(BF16)
        active = jnp.concatenate([left, right], axis=1)
        centred = jnp.dot(active, weight[...], preferred_element_type=F32) + shift
        total = jnp.sum(
            centred[:, :HALF] * centred[:, :HALF] + centred[:, HALF:] * centred[:, HALF:], axis=1, keepdims=True
        )
        here = pl.ds(chunk * CHUNK, CHUNK)
        raw[here, :] = centred
        square[here, :] = jnp.broadcast_to(total, (CHUNK, HALF))

    def second_half(floor, chunk, sums):
        left, right = sums
        for k in range(chunk * per_chunk, (chunk + 1) * per_chunk):
            here = pl.ds(k * ROWS, ROWS)
            scale = lax.rsqrt(square[here, :] * (1.0 / width) + floor[:, k : k + 1])
            left = left + raw[here, :HALF] * scale
            right = right + raw[here, HALF:] * scale
        return left, right

    chunks = edges // CHUNK
    gather(even, 0, 0, edges)

    @pl.loop(0, blocks // 2)
    def _(pair):
        for parity in range(2):
            block = 2 * pair + parity

            @pl.when(block < block_total[0])
            def _():
                first = pl.multiple_of(block * ROWS, ROWS)
                following = jnp.minimum(block + 1, blocks - 1)
                floor = floor_ref[pl.ds(first, ROWS), :]
                sums = (jnp.zeros((ROWS, HALF), F32), jnp.zeros((ROWS, HALF), F32))
                for chunk in range(chunks + 1):
                    if chunk < chunks:
                        gather(gathered[1 - parity], following, chunk * CHUNK, (chunk + 1) * CHUNK)
                        first_half(gathered[parity], first, chunk)
                    if chunk > 0:
                        sums = second_half(floor, chunk - 1, sums)
                summed[pl.ds(first, ROWS), :HALF] = sums[0]
                summed[pl.ds(first, ROWS), HALF:] = sums[1]

    @pl.loop(0, rows // NODE_ROWS)
    def _(i):
        first = pl.multiple_of(i * NODE_ROWS, NODE_ROWS)
        here = pl.ds(first, NODE_ROWS)
        own = table_ref[here, :]
        message = (summed[here, :] * edge_gain[...]).astype(BF16)
        hidden = (
            jnp.dot(own, node_self[...], preferred_element_type=F32)
            + jnp.dot(message, node_message[...], preferred_element_type=F32)
            + node_bias[...]
        )
        hidden = jnp.maximum(hidden, 0.0).astype(BF16)
        node_raw = jnp.dot(hidden, node_out[...], preferred_element_type=F32) + node_shift[...]
        renewed = (own.astype(F32) + layer_norm(node_raw, node_gain[...])) * living_ref[here, :]
        renewed = renewed.astype(BF16)
        renewed_ref[here, :] = renewed
        if not last:
            next_projected[here, :] = project_rows(pairs, first, renewed, next_weight[...])

    if not last:
        pick_boundary(pairs, halo_ids, picked, boundary_ref)


def message_step(block_total, edge_ids, ghosts, table, projected, floor, living, weights, halo_ids=None, next_weight=None):
    last = halo_ids is None
    rows, width = table.shape
    slots = floor.shape[1]
    edges = slots * ROWS
    ghost_total = ghosts.shape[0] * ghosts.shape[1]
    vmem = pl.BlockSpec(memory_space=pltpu.VMEM)
    smem = pl.BlockSpec(memory_space=pltpu.SMEM)
    out_shape = [jax.ShapeDtypeStruct((rows, width), BF16)]
    extra, extra_specs = [], []
    if not last:
        count = halo_ids.shape[0]
        out_shape += [jax.ShapeDtypeStruct((rows, width), BF16), jax.ShapeDtypeStruct((count, width), BF16)]
        extra, extra_specs = [halo_ids, next_weight], [smem, vmem]
    return pl.pallas_call(
        functools.partial(step_kernel, slots, last),
        out_shape=tuple(out_shape),
        in_specs=[smem, smem, pl.BlockSpec(memory_space=pl.ANY)] + [vmem] * (4 + len(weights)) + extra_specs,
        out_specs=tuple([vmem] * len(out_shape)),
        scratch_shapes=[
            pltpu.VMEM((2 * (rows + ghost_total), HALF), F32),
            pltpu.VMEM((2 * edges, HALF), F32),
            pltpu.VMEM((2 * edges, HALF), F32),
            pltpu.VMEM((rows, width), F32),
            pltpu.VMEM((rows, width), F32),
            pltpu.VMEM((edges, width), F32),
            pltpu.VMEM((edges, HALF), F32),
            pltpu.VMEM((width, width), BF16),
            pltpu.VMEM(ghosts.shape, BF16),
            pltpu.VMEM((2 * 64, HALF), F32),
            pltpu.SemaphoreType.DMA((ghosts.shape[0],)),
        ],
        compiler_params=pltpu.CompilerParams(vmem_limit_bytes=VMEM_BYTES),
        name="message_step",
    )(block_total, edge_ids, ghosts, table, projected, floor, living, *weights, *extra)


def exchange_kernel(axes, boundary, ghosts, send_sems, recv_sems):
    place = [lax.axis_index(a) for a in axes]
    sizes = [lax.axis_size(a) for a in axes]

    def inside(axis, step):
        return jnp.logical_and(place[axis] + step >= 0, place[axis] + step < sizes[axis])

    def target(axis, step):
        return tuple(place[a] + (step if a == axis else 0) for a in range(3))

    barrier = pltpu.get_barrier_semaphore()
    friends = jnp.int32(0)
    for axis in range(3):
        for step in (-1, 1):
            friends = friends + inside(axis, step).astype(jnp.int32)

            @pl.when(inside(axis, step))
            def _():
                pl.semaphore_signal(
                    barrier, inc=1, device_id=target(axis, step), device_id_type=pl.DeviceIdType.MESH
                )

    pl.semaphore_wait(barrier, friends)

    def number(offset):
        return 9 * (offset[0] + 1) + 3 * (offset[1] + 1) + offset[2] + 1

    def moved(offset, axis, step):
        return tuple(offset[a] + (step if a == axis else 0) for a in range(3))

    def send(offset, axis, step):
        slot = number(moved(offset, axis, -step))
        source = boundary if offset == (0, 0, 0) else ghosts.at[number(offset)]
        return pltpu.make_async_remote_copy(
            src_ref=source,
            dst_ref=ghosts.at[slot],
            send_sem=send_sems.at[slot],
            recv_sem=recv_sems.at[slot],
            device_id=target(axis, step),
            device_id_type=pl.DeviceIdType.MESH,
        )

    def present(offset):
        found = None
        for a in range(3):
            if offset[a] != 0:
                here = inside(a, offset[a])
                found = here if found is None else jnp.logical_and(found, here)
        return found

    def forward(offset, first_axis):
        for axis in range(first_axis, 3):
            for step in (-1, 1):

                @pl.when(inside(axis, step))
                def _():
                    send(offset, axis, step).start()

    def arrive(offset):
        axis = max(a for a in range(3) if offset[a] != 0)
        send(moved(offset, axis, -offset[axis]), axis, -offset[axis]).wait_recv()

    middle = [(dx, 0, 0) for dx in (-1, 1)]
    sides = [(dx, dy, 0) for dx in (0, -1, 1) for dy in (-1, 1)]
    ends = [(dx, dy, dz) for dx in (0, -1, 1) for dy in (0, -1, 1) for dz in (-1, 1)]
    forward((0, 0, 0), 0)
    for offset in middle + sides:

        @pl.when(present(offset))
        def _():
            arrive(offset)
            forward(offset, 1 if offset in middle else 2)

    for offset in ends:

        @pl.when(present(offset))
        def _():
            arrive(offset)

    for offset, first_axis in [((0, 0, 0), 0)] + [(o, 1) for o in middle] + [(o, 2) for o in sides]:
        for axis in range(first_axis, 3):
            for step in (-1, 1):
                there = inside(axis, step)
                if offset != (0, 0, 0):
                    there = jnp.logical_and(there, present(offset))

                @pl.when(there)
                def _():
                    send(offset, axis, step).wait_send()


def exchange(boundary):
    axes = ("gx", "gy", "gz")
    anywhere = pl.BlockSpec(memory_space=pl.ANY)
    return pl.pallas_call(
        functools.partial(exchange_kernel, axes),
        out_shape=jax.ShapeDtypeStruct((27,) + boundary.shape, boundary.dtype),
        in_specs=[anywhere],
        out_specs=anywhere,
        scratch_shapes=[pltpu.SemaphoreType.DMA((27,)), pltpu.SemaphoreType.DMA((27,))],
        compiler_params=pltpu.CompilerParams(collective_id=0, has_side_effects=True),
        name="exchange",
    )(boundary)


def pick_rows(source_rows, row_ids):
    selector = (
        row_ids[:, None] == jnp.arange(source_rows.shape[0], dtype=jnp.int32)[None, :]
    ).astype(source_rows.dtype)
    return jnp.dot(selector, source_rows, preferred_element_type=F32).astype(source_rows.dtype)


def local(
    latent,
    live_count,
    leave_rows,
    leave_target,
    halo_rows,
    neighbours,
    edge_in,
    edge_bias,
    edge_out,
    edge_shift,
    edge_gain,
    node_in,
    node_bias,
    node_out,
    node_shift,
    node_gain,
):
    axes = ("gx", "gy", "gz")
    devices = lax.axis_size(axes)
    local_rows, width = latent.shape
    table_rows, slots = neighbours.shape
    slots_total = table_rows - local_rows
    capacity = slots_total // devices
    leaving = leave_rows.shape[0]
    target_domain = leave_target[:, 0]
    order_rows = jnp.arange(leaving, dtype=jnp.int32)
    earlier = order_rows[None, :] < order_rows[:, None]
    same_target = target_domain[:, None] == target_domain[None, :]
    row_rank = jnp.sum(jnp.logical_and(same_target, earlier).astype(jnp.int32), axis=1)
    position = target_domain * capacity + row_rank
    moving = pick_rows(latent, leave_rows)
    moving = jnp.concatenate([moving, jnp.ones((leaving, HALF), BF16)], axis=1)
    placement = jnp.arange(slots_total, dtype=jnp.int32)[:, None] == position[None, :]
    outgoing = jnp.dot(placement.astype(BF16), moving, preferred_element_type=F32).astype(BF16)
    arrived = lax.all_to_all(
        outgoing.reshape(devices, capacity, width + HALF), axes, split_axis=0, concat_axis=0, tiled=True
    ).reshape(slots_total, width + HALF)
    local_index = jnp.arange(local_rows, dtype=jnp.int32)
    departed = jnp.any(local_index[:, None] == leave_rows[None, :], axis=1)
    local_live = jnp.logical_and(local_index < live_count[0], jnp.logical_not(departed)).astype(F32)
    living = jnp.concatenate([local_live[:, None], arrived[:, width : width + 1].astype(F32)], axis=0)

    blocks = table_rows // ROWS
    edge_ids = 2 * jnp.maximum(neighbours, 0)
    edge_ids = edge_ids.reshape(blocks, ROWS, slots).transpose(0, 2, 1).reshape(-1)
    floor = jnp.where(neighbours >= 0, EPS, jnp.inf).astype(F32)
    block_total = jnp.full((1,), blocks, jnp.int32)
    halo_ids = 2 * halo_rows

    table, projected, boundary = open_table(latent, arrived[:, :width], halo_ids, edge_in[0, 1])
    steps = edge_in.shape[0]
    for t in range(steps):
        ghosts = exchange(boundary)
        weights = (
            edge_in[t, 0],
            edge_bias[t][None],
            edge_out[t],
            edge_shift[t][None],
            edge_gain[t][None],
            node_in[t, 0],
            node_in[t, 1],
            node_bias[t][None],
            node_out[t],
            node_shift[t][None],
            node_gain[t][None],
        )
        if t < steps - 1:
            table, projected, boundary = message_step(
                block_total, edge_ids, ghosts, table, projected, floor, living, weights, halo_ids, edge_in[t + 1, 1]
            )
        else:
            (table,) = message_step(block_total, edge_ids, ghosts, table, projected, floor, living, weights)
    return table


def solution(mesh):
    rows = P(("gx", "gy", "gz"))
    in_specs = (rows,) * 6 + (P(),) * 10
    return jax.shard_map(local, mesh=mesh, in_specs=in_specs, out_specs=rows, check_vma=False)
```

```python
import functools

import jax
import jax.numpy as jnp
from jax import lax
from jax.experimental import pallas as pl
from jax.experimental.pallas import tpu as pltpu
from jax.sharding import PartitionSpec as P

EPS = 1e-05
F32 = jnp.float32
BF16 = jnp.bfloat16
HALF = 128
ROWS = 32
CHUNK = 256
GROUP = 8
NODE_ROWS = 256
AXES = ("gx", "gy", "gz")
MESH = pl.DeviceIdType.MESH
VMEM_BYTES = 58 * 2**20
VMEM = pl.BlockSpec(memory_space=pltpu.VMEM)
SMEM = pl.BlockSpec(memory_space=pltpu.SMEM)
ANYWHERE = pl.BlockSpec(memory_space=pl.ANY)


def layer_norm(values, feature_gain):
    average = jnp.mean(values, axis=-1, keepdims=True)
    centred = values - average
    spread = jnp.mean(centred * centred, axis=-1, keepdims=True)
    return centred * lax.rsqrt(spread + EPS) * feature_gain


def store_split(pairs, first_row, values):
    count = values.shape[0]
    pairs[pl.ds(2 * first_row, count, stride=2), :] = values[:, :HALF]
    pairs[pl.ds(2 * first_row + 1, count, stride=2), :] = values[:, HALF:]


def load_split(pairs, first_row, count):
    left = pairs[pl.ds(2 * first_row, count, stride=2), :]
    right = pairs[pl.ds(2 * first_row + 1, count, stride=2), :]
    return jnp.concatenate([left, right], axis=1)


def project(rows, weight):
    return jnp.dot(rows, weight, preferred_element_type=F32).astype(BF16)


def copy_rows(source, ids, into, count):
    @pl.loop(0, count // 64)
    def _(block):
        for g in range(64 // GROUP):
            some = ids.at[pl.ds(block * 64 + g * GROUP, GROUP)]
            for e in range(GROUP):
                row = pl.multiple_of(some[e], 2)
                place = pl.multiple_of(2 * (block * 64 + g * GROUP + e), 2)
                into[pl.ds(place, 2), :] = source[pl.ds(row, 2), :]


def order_kernel(neighbours, digits, halo_lanes, edge_ids, floor_ref, order_ref, place_ref, count_ref, places):
    rows, slots = neighbours.shape
    boundary = halo_lanes.shape[1]
    n = NODE_ROWS
    lower = (
        lax.broadcasted_iota(jnp.int32, (n, n), 0) > lax.broadcasted_iota(jnp.int32, (n, n), 1)
    ).astype(BF16)
    lane = lax.broadcasted_iota(jnp.int32, (n, boundary), 1).astype(F32)

    def one_chunk(c, carry):
        used, spare = carry
        first = pl.multiple_of(c * n, n)
        active = jnp.max(neighbours[pl.ds(first, n), :], axis=1, keepdims=True) >= 0
        row_ids = lax.broadcasted_iota(jnp.int32, (n, boundary), 0) + first
        same = (row_ids == halo_lanes[...]).astype(F32)
        listed = jnp.sum(same, axis=1, keepdims=True) > 0.0
        position = jnp.sum(same * lane, axis=1, keepdims=True)
        others = jnp.where(listed, 0.0, jnp.where(active, 1.0, 0.0))
        idle = jnp.where(listed, 0.0, jnp.where(active, 0.0, 1.0))
        others = jnp.broadcast_to(others, (n, HALF))
        idle = jnp.broadcast_to(idle, (n, HALF))
        before = jnp.dot(lower, others.astype(BF16), preferred_element_type=F32) + used
        behind = jnp.dot(lower, idle.astype(BF16), preferred_element_type=F32) + spare
        place = jnp.where(others > 0.0, boundary + before, rows - 1 - behind)
        place = jnp.where(listed, position, place)
        places[pl.ds(first, n), :] = place
        place_ref[pl.ds(first, n), :] = (2.0 * place[:, :1]).astype(jnp.int32)
        return used + jnp.sum(others[:, :1]), spare + jnp.sum(idle[:, :1])

    used, _ = lax.fori_loop(0, rows // n, one_chunk, (jnp.float32(0.0), jnp.float32(0.0)))
    count_ref[0] = used.astype(jnp.int32) + boundary

    @pl.loop(0, rows // n)
    def _(c):
        first = pl.multiple_of(c * n, n)
        halves = []
        for half in range(n // HALF):
            lanes = lax.broadcasted_iota(jnp.int32, (rows, HALF), 1).astype(F32)
            wanted = lanes + (first + half * HALF).astype(F32)
            halves.append(jnp.where(places[...] == wanted, 1.0, 0.0).astype(BF16))
        chosen = jnp.concatenate(halves, axis=1)
        picked = jnp.dot(digits[...], chosen, preferred_element_type=F32)
        half_rows = digits.shape[0] // 2
        value = picked[:half_rows] * 128.0 + picked[half_rows:]
        here = pl.ds(first, n)
        edge_ids[:, here] = (2.0 * jnp.maximum(value[:slots] - 1.0, 0.0)).astype(jnp.int32)
        order_ref[:, here] = (2.0 * value[slots : slots + 1]).astype(jnp.int32)
        floor = jnp.where(value > 0.5, EPS, jnp.inf).astype(F32)
        floor_ref[here, :] = jnp.transpose(jnp.concatenate([floor] * (HALF // half_rows), axis=0))


def order_rows(neighbours, halo_rows):
    rows, slots = neighbours.shape
    half_rows = 32
    ids = neighbours.T + 1
    ids = jnp.concatenate(
        [ids, jnp.arange(rows, dtype=jnp.int32)[None], jnp.zeros((half_rows - slots - 1, rows), jnp.int32)]
    )
    digits = jnp.concatenate([ids // 128, ids % 128]).astype(BF16)
    return pl.pallas_call(
        order_kernel,
        out_shape=(
            jax.ShapeDtypeStruct((slots, rows), jnp.int32),
            jax.ShapeDtypeStruct((rows, HALF), F32),
            jax.ShapeDtypeStruct((1, rows), jnp.int32),
            jax.ShapeDtypeStruct((rows, 1), jnp.int32),
            jax.ShapeDtypeStruct((1,), jnp.int32),
        ),
        in_specs=[VMEM, VMEM, VMEM],
        out_specs=(VMEM, VMEM, VMEM, VMEM, SMEM),
        scratch_shapes=[pltpu.VMEM((rows, HALF), F32)],
        compiler_params=pltpu.CompilerParams(vmem_limit_bytes=VMEM_BYTES),
        name="order_rows",
    )(neighbours, digits, halo_rows[None, :])


def open_kernel(latent_ref, arrived_ref, halo_ids, order, weight_ref, ordered_ref, projected_ref, boundary_ref, pairs, picked):
    local_rows = latent_ref.shape[0]
    arrivals = arrived_ref.shape[0]
    rows = local_rows + arrivals

    def sources(take):
        @pl.loop(0, local_rows // NODE_ROWS)
        def _(i):
            first = pl.multiple_of(i * NODE_ROWS, NODE_ROWS)
            take(first, latent_ref[pl.ds(first, NODE_ROWS), :])

        take(local_rows, arrived_ref[...])

    def projection(first, values):
        projected = project(values, weight_ref[...])
        projected_ref[pl.ds(first, NODE_ROWS), :] = projected
        store_split(pairs, first, projected.astype(F32))

    sources(projection)
    count = boundary_ref.shape[0]
    copy_rows(pairs, halo_ids, picked, count)
    boundary_ref[...] = load_split(picked, 0, count).astype(BF16)
    sources(lambda first, values: store_split(pairs, first, values.astype(F32)))
    copy_rows(pairs, order, picked, rows)

    @pl.loop(0, rows // NODE_ROWS)
    def _(i):
        first = pl.multiple_of(i * NODE_ROWS, NODE_ROWS)
        ordered_ref[pl.ds(first, NODE_ROWS), :] = load_split(picked, first, NODE_ROWS).astype(BF16)


def open_table(latent, arrived, halo_ids, order, weight):
    rows = latent.shape[0] + arrived.shape[0]
    width = latent.shape[1]
    count = halo_ids.shape[0]
    return pl.pallas_call(
        open_kernel,
        out_shape=(
            jax.ShapeDtypeStruct((rows, width), BF16),
            jax.ShapeDtypeStruct((rows, width), BF16),
            jax.ShapeDtypeStruct((count, width), BF16),
        ),
        in_specs=[VMEM, VMEM, SMEM, SMEM, VMEM],
        out_specs=(VMEM, VMEM, VMEM),
        scratch_shapes=[pltpu.VMEM((2 * rows, HALF), F32), pltpu.VMEM((2 * rows, HALF), F32)],
        compiler_params=pltpu.CompilerParams(vmem_limit_bytes=VMEM_BYTES),
        name="open_table",
    )(latent, arrived, halo_ids, order, weight)


class Grid:
    def __init__(self):
        self.place = [lax.axis_index(a) for a in AXES]
        self.sizes = [lax.axis_size(a) for a in AXES]

    def inside(self, axis, step):
        return jnp.logical_and(self.place[axis] + step >= 0, self.place[axis] + step < self.sizes[axis])

    def target(self, axis, step):
        return tuple(self.place[a] + (step if a == axis else 0) for a in range(3))

    def present(self, offset):
        found = None
        for a in range(3):
            if offset[a] != 0:
                here = self.inside(a, offset[a])
                found = here if found is None else jnp.logical_and(found, here)
        return found

    def greet(self):
        barrier = pltpu.get_barrier_semaphore()
        friends = jnp.int32(0)
        for axis in range(3):
            for step in (-1, 1):
                friends = friends + self.inside(axis, step).astype(jnp.int32)

                @pl.when(self.inside(axis, step))
                def _():
                    pl.semaphore_signal(barrier, inc=1, device_id=self.target(axis, step), device_id_type=MESH)

        pl.semaphore_wait(barrier, friends)


def number(offset):
    return 9 * (offset[0] + 1) + 3 * (offset[1] + 1) + offset[2] + 1


def moved(offset, axis, step):
    return tuple(offset[a] + (step if a == axis else 0) for a in range(3))


CENTRE = (0, 0, 0)
MIDDLE = [(dx, 0, 0) for dx in (-1, 1)]
SIDES = [(dx, dy, 0) for dx in (0, -1, 1) for dy in (-1, 1)]
ENDS = [(dx, dy, dz) for dx in (0, -1, 1) for dy in (0, -1, 1) for dz in (-1, 1)]


class Exchange:
    def __init__(self, grid, boundary, ghosts, send_sems, recv_sems):
        self.grid, self.boundary, self.ghosts = grid, boundary, ghosts
        self.send_sems, self.recv_sems = send_sems, recv_sems

    def copy(self, offset, axis, step):
        slot = number(moved(offset, axis, -step))
        return pltpu.make_async_remote_copy(
            src_ref=self.boundary if offset == CENTRE else self.ghosts.at[number(offset)],
            dst_ref=self.ghosts.at[slot],
            send_sem=self.send_sems.at[slot],
            recv_sem=self.recv_sems.at[slot],
            device_id=self.grid.target(axis, step),
            device_id_type=MESH,
        )

    def first_axis(self, offset):
        return 0 if offset == CENTRE else 1 if offset in MIDDLE else 2

    def forward(self, offset):
        for axis in range(self.first_axis(offset), 3):
            for step in (-1, 1):

                @pl.when(self.grid.inside(axis, step))
                def _():
                    self.copy(offset, axis, step).start()

    def arrive(self, offset):
        axis = max(a for a in range(3) if offset[a] != 0)
        self.copy(moved(offset, axis, -offset[axis]), axis, -offset[axis]).wait_recv()

    def relay(self, offsets):
        for offset in offsets:

            @pl.when(self.grid.present(offset))
            def _():
                self.arrive(offset)
                self.forward(offset)

    def finish_sends(self):
        for offset in [CENTRE] + MIDDLE + SIDES:
            for axis in range(self.first_axis(offset), 3):
                for step in (-1, 1):
                    there = self.grid.inside(axis, step)
                    if offset != CENTRE:
                        there = jnp.logical_and(there, self.grid.present(offset))

                    @pl.when(there)
                    def _():
                        self.copy(offset, axis, step).wait_send()


class EdgeLayers:
    def __init__(self, rows, slots, refs, scratch):
        self.edge_ids, self.floor = refs["edge_ids"], refs["floor"]
        self.refs = refs
        self.rows, self.slots = rows, slots
        self.edges = slots * ROWS
        self.pairs, self.buffers, self.receive, self.summed, self.raw, self.square, self.weight = scratch
        self.width = self.receive.shape[1]

    def prepare(self, table_ref):
        refs = self.refs
        wide = refs["edge_out"][...].astype(F32)
        self.weight[...] = (wide - jnp.mean(wide, axis=1, keepdims=True)).astype(BF16)

        @pl.loop(0, self.rows // NODE_ROWS)
        def _(i):
            here = pl.ds(pl.multiple_of(i * NODE_ROWS, NODE_ROWS), NODE_ROWS)
            self.summed[here, :] = jnp.zeros((NODE_ROWS, self.width), F32)
            self.receive[here, :] = (
                jnp.dot(table_ref[here, :], refs["receive_weight"][...], preferred_element_type=F32)
                + refs["edge_bias"][...]
            )

    def gather(self, into, block, start, stop):
        first = pl.multiple_of(block * ROWS, ROWS)
        for e in range(start, stop):
            k, r = divmod(e, ROWS)
            if r % GROUP == 0:
                ids = self.edge_ids.at[k, pl.ds(first + r, GROUP)]
            into[pl.ds(2 * e, 2), :] = self.pairs[pl.ds(ids[r % GROUP], 2), :]

    def first_half(self, source, first, chunk, shift):
        per_chunk = CHUNK // ROWS
        own = self.receive[pl.ds(first, ROWS), :]
        left = source[pl.ds(2 * chunk * CHUNK, CHUNK, stride=2), :].reshape(per_chunk, ROWS, HALF)
        right = source[pl.ds(2 * chunk * CHUNK + 1, CHUNK, stride=2), :].reshape(per_chunk, ROWS, HALF)
        left = jnp.maximum(left + own[:, :HALF][None], 0.0).reshape(CHUNK, HALF).astype(BF16)
        right = jnp.maximum(right + own[:, HALF:][None], 0.0).reshape(CHUNK, HALF).astype(BF16)
        active = jnp.concatenate([left, right], axis=1)
        centred = jnp.dot(active, self.weight[...], preferred_element_type=F32) + shift
        total = jnp.sum(
            centred[:, :HALF] * centred[:, :HALF] + centred[:, HALF:] * centred[:, HALF:], axis=1, keepdims=True
        )
        here = pl.ds(chunk * CHUNK, CHUNK)
        self.raw[here, :] = centred
        self.square[here, :] = jnp.broadcast_to(total, (CHUNK, HALF))

    def second_half(self, floor, chunk, sums):
        left, right = sums
        per_chunk = CHUNK // ROWS
        for k in range(chunk * per_chunk, (chunk + 1) * per_chunk):
            here = pl.ds(k * ROWS, ROWS)
            scale = lax.rsqrt(self.square[here, :] * (1.0 / self.width) + floor[:, k : k + 1])
            left = left + self.raw[here, :HALF] * scale
            right = right + self.raw[here, HALF:] * scale
        return left, right

    def one_block(self, block, parity, last_block):
        chunks = self.edges // CHUNK
        first = pl.multiple_of(block * ROWS, ROWS)
        following = jnp.minimum(block + 1, last_block)
        edge_shift = self.refs["edge_shift"]
        shift = edge_shift[...] - jnp.mean(edge_shift[...], axis=1, keepdims=True)
        floor = self.floor[pl.ds(first, ROWS), :]
        sums = (jnp.zeros((ROWS, HALF), F32), jnp.zeros((ROWS, HALF), F32))
        for chunk in range(chunks + 1):
            if chunk < chunks:
                self.gather(self.buffers[1 - parity], following, chunk * CHUNK, (chunk + 1) * CHUNK)
                self.first_half(self.buffers[parity], first, chunk, shift)
            if chunk > 0:
                sums = self.second_half(floor, chunk - 1, sums)
        self.summed[pl.ds(first, ROWS), :HALF] = sums[0]
        self.summed[pl.ds(first, ROWS), HALF:] = sums[1]


def node_layers(refs, table_ref, summed, here):
    own = table_ref[here, :]
    message = (summed[here, :] * refs["edge_gain"][...]).astype(BF16)
    hidden = (
        jnp.dot(own, refs["node_self"][...], preferred_element_type=F32)
        + jnp.dot(message, refs["node_message"][...], preferred_element_type=F32)
        + refs["node_bias"][...]
    )
    hidden = jnp.maximum(hidden, 0.0).astype(BF16)
    node_raw = jnp.dot(hidden, refs["node_out"][...], preferred_element_type=F32) + refs["node_shift"][...]
    return own.astype(F32) + layer_norm(node_raw, refs["node_gain"][...])


NAMES = (
    "edge_ids",
    "floor",
    "receive_weight",
    "edge_bias",
    "edge_out",
    "edge_shift",
    "edge_gain",
    "node_self",
    "node_message",
    "node_bias",
    "node_out",
    "node_shift",
    "node_gain",
)


def edge_scratch(rows, slots, senders, width):
    edges = slots * ROWS
    return [
        pltpu.VMEM((2 * senders, HALF), F32),
        pltpu.VMEM((2 * edges, HALF), F32),
        pltpu.VMEM((2 * edges, HALF), F32),
        pltpu.VMEM((rows, width), F32),
        pltpu.VMEM((rows, width), F32),
        pltpu.VMEM((edges, width), F32),
        pltpu.VMEM((edges, HALF), F32),
        pltpu.VMEM((width, width), BF16),
    ]


def unpack_scratch(scratch):
    pairs, even, odd, receive, summed, raw, square, weight = scratch
    return pairs, (even, odd), receive, summed, raw, square, weight


def spread_block(pairs, first_row, block_ref):
    @pl.loop(0, block_ref.shape[0] // 128)
    def _(piece):
        start = pl.multiple_of(piece * 128, 128)
        store_split(pairs, first_row + start, block_ref[pl.ds(start, 128), :].astype(F32))


def first_step_kernel(slots, blocks, marks, *args):
    refs = dict(zip(NAMES, args))
    table_ref, projected_ref, boundary_ref, next_weight = args[13:17]
    renewed_ref, next_projected, next_ghosts = args[17:20]
    scratch = unpack_scratch(args[20:28])
    ghosts, next_boundary, send_a, recv_a, send_b, recv_b = args[28:]
    pairs, summed = scratch[0], scratch[3]
    rows = table_ref.shape[0]
    boundary_rows = boundary_ref.shape[0]
    grid = Grid()
    now = Exchange(grid, boundary_ref, ghosts, send_a, recv_a)
    later = Exchange(grid, next_boundary, next_ghosts, send_b, recv_b)
    layers = EdgeLayers(rows, slots, refs, scratch)
    grid.greet()
    now.forward(CENTRE)
    layers.prepare(table_ref)

    @pl.loop(0, rows // NODE_ROWS)
    def _(i):
        first = pl.multiple_of(i * NODE_ROWS, NODE_ROWS)
        store_split(pairs, first, projected_ref[pl.ds(first, NODE_ROWS), :].astype(F32))

    def spread(offset):
        spread_block(pairs, rows + number(offset) * boundary_rows, ghosts.at[number(offset)])

    def spread_all(offsets):
        for offset in offsets:

            @pl.when(grid.present(offset))
            def _():
                spread(offset)

    now.relay(MIDDLE)
    now.relay(SIDES[:2])
    spread_all(MIDDLE)
    spread_all(SIDES[:2])
    now.relay(SIDES[2:])
    spread_all(SIDES[2:])
    for offset in ENDS:

        @pl.when(grid.present(offset))
        def _():
            now.arrive(offset)
            spread(offset)

    layers.gather(layers.buffers[0], 0, 0, layers.edges)

    def renew(first):
        here = pl.ds(first, NODE_ROWS)
        renewed = node_layers(refs, table_ref, summed, here).astype(BF16)
        renewed_ref[here, :] = renewed
        projected = project(renewed, next_weight[...])
        next_projected[here, :] = projected
        return projected

    @pl.loop(0, blocks // 2)
    def _(pair):
        @pl.when(pair == marks[0])
        def _():
            for first in range(0, boundary_rows, NODE_ROWS):
                next_boundary[pl.ds(first, NODE_ROWS), :] = renew(first)
            later.forward(CENTRE)

        for mark, offsets in zip(marks[1:], (MIDDLE, SIDES[:2], SIDES[2:])):

            @pl.when(pair == mark)
            def _():
                later.relay(offsets)

        for parity in range(2):
            block = 2 * pair + parity

            @pl.when(block < blocks + grid.place[0])
            def _():
                layers.one_block(block, parity, blocks - 1)

    @pl.loop(boundary_rows // NODE_ROWS, rows // NODE_ROWS)
    def _(i):
        renew(pl.multiple_of(i * NODE_ROWS, NODE_ROWS))

    for offset in ENDS:

        @pl.when(grid.present(offset))
        def _():
            later.arrive(offset)

    now.finish_sends()
    later.finish_sends()


def first_step(blocks, layer_args, table, projected, boundary, next_weight):
    rows, width = table.shape
    slots = layer_args[0].shape[0]
    count = boundary.shape[0]
    first_pair = count // ROWS // 2
    rest = blocks // 2 - first_pair
    marks = (first_pair, first_pair + rest * 5 // 26, first_pair + rest * 7 // 26, first_pair + rest * 14 // 26)
    return pl.pallas_call(
        functools.partial(first_step_kernel, slots, blocks, marks),
        out_shape=(
            jax.ShapeDtypeStruct((rows, width), BF16),
            jax.ShapeDtypeStruct((rows, width), BF16),
            jax.ShapeDtypeStruct((27, count, width), BF16),
        ),
        in_specs=[SMEM] + [VMEM] * 16,
        out_specs=(VMEM, VMEM, ANYWHERE),
        scratch_shapes=edge_scratch(rows, slots, rows + 27 * count, width)
        + [pltpu.VMEM((27, count, width), BF16), pltpu.VMEM((count, width), BF16)]
        + [pltpu.SemaphoreType.DMA((27,))] * 4,
        compiler_params=pltpu.CompilerParams(
            collective_id=0, has_side_effects=True, vmem_limit_bytes=VMEM_BYTES
        ),
        name="first_step",
    )(*layer_args, table, projected, boundary, next_weight)


def last_step_kernel(slots, *args):
    refs = dict(zip(NAMES, args))
    table_ref, projected_ref, ghosts, living_ref, place_ids, count_ref = args[13:19]
    updated_ref = args[19]
    scratch = unpack_scratch(args[20:28])
    staged, ordered, sems = args[28:]
    pairs, summed = scratch[0], scratch[3]
    rows = table_ref.shape[0]
    ghost_blocks, ghost_rows = ghosts.shape[0], ghosts.shape[1]
    centre = ghost_blocks // 2
    layers = EdgeLayers(rows, slots, refs, scratch)

    def fetch(block):
        return pltpu.make_async_copy(ghosts.at[block], staged.at[block], sems.at[block])

    for block in range(ghost_blocks):
        if block != centre:
            fetch(block).start()
    layers.prepare(table_ref)

    @pl.loop(0, rows // NODE_ROWS)
    def _(i):
        first = pl.multiple_of(i * NODE_ROWS, NODE_ROWS)
        store_split(ordered, first, projected_ref[pl.ds(first, NODE_ROWS), :].astype(F32))

    copy_rows(ordered, place_ids, pairs, rows)

    @pl.loop(0, ghost_blocks)
    def _(block):
        @pl.when(block != centre)
        def _():
            fetch(block).wait()
            spread_block(pairs, pl.multiple_of(rows + block * ghost_rows, ghost_rows), staged.at[block])

    blocks = (count_ref[0] + ROWS - 1) // ROWS
    layers.gather(layers.buffers[0], 0, 0, layers.edges)

    @pl.loop(0, (blocks + 1) // 2)
    def _(pair):
        for parity in range(2):
            block = 2 * pair + parity

            @pl.when(block < blocks)
            def _():
                layers.one_block(block, parity, rows // ROWS - 1)

    @pl.loop(0, rows // NODE_ROWS)
    def _(i):
        first = pl.multiple_of(i * NODE_ROWS, NODE_ROWS)
        renewed = node_layers(refs, table_ref, summed, pl.ds(first, NODE_ROWS))
        store_split(ordered, first, renewed)

    copy_rows(ordered, place_ids, pairs, rows)

    @pl.loop(0, rows // NODE_ROWS)
    def _(i):
        first = pl.multiple_of(i * NODE_ROWS, NODE_ROWS)
        here = pl.ds(first, NODE_ROWS)
        updated_ref[here, :] = (load_split(pairs, first, NODE_ROWS) * living_ref[here, :]).astype(BF16)


def last_step(layer_args, table, projected, ghosts, living, place_ids, count):
    rows, width = table.shape
    slots = layer_args[0].shape[0]
    return pl.pallas_call(
        functools.partial(last_step_kernel, slots),
        out_shape=jax.ShapeDtypeStruct((rows, width), BF16),
        in_specs=[SMEM] + [VMEM] * 12 + [VMEM, VMEM, ANYWHERE, VMEM, SMEM, SMEM],
        out_specs=VMEM,
        scratch_shapes=edge_scratch(rows, slots, rows + ghosts.shape[0] * ghosts.shape[1], width)
        + [
            pltpu.VMEM(ghosts.shape, BF16),
            pltpu.VMEM((2 * rows, HALF), F32),
            pltpu.SemaphoreType.DMA((ghosts.shape[0],)),
        ],
        compiler_params=pltpu.CompilerParams(vmem_limit_bytes=VMEM_BYTES),
        name="last_step",
    )(*layer_args, table, projected, ghosts, living, place_ids, count)


def pick_rows(source_rows, row_ids):
    selector = (
        row_ids[:, None] == jnp.arange(source_rows.shape[0], dtype=jnp.int32)[None, :]
    ).astype(source_rows.dtype)
    return jnp.dot(selector, source_rows, preferred_element_type=F32).astype(source_rows.dtype)


def local(
    latent,
    live_count,
    leave_rows,
    leave_target,
    halo_rows,
    neighbours,
    edge_in,
    edge_bias,
    edge_out,
    edge_shift,
    edge_gain,
    node_in,
    node_bias,
    node_out,
    node_shift,
    node_gain,
):
    axes = ("gx", "gy", "gz")
    devices = lax.axis_size(axes)
    local_rows, width = latent.shape
    table_rows, slots = neighbours.shape
    slots_total = table_rows - local_rows
    capacity = slots_total // devices
    leaving = leave_rows.shape[0]
    target_domain = leave_target[:, 0]
    entry = jnp.arange(leaving, dtype=jnp.int32)
    earlier = entry[None, :] < entry[:, None]
    same_target = target_domain[:, None] == target_domain[None, :]
    row_rank = jnp.sum(jnp.logical_and(same_target, earlier).astype(jnp.int32), axis=1)
    position = target_domain * capacity + row_rank
    moving = pick_rows(latent, leave_rows)
    moving = jnp.concatenate([moving, jnp.ones((leaving, HALF), BF16)], axis=1)
    placement = jnp.arange(slots_total, dtype=jnp.int32)[:, None] == position[None, :]
    outgoing = jnp.dot(placement.astype(BF16), moving, preferred_element_type=F32).astype(BF16)
    arrived = lax.all_to_all(
        outgoing.reshape(devices, capacity, width + HALF), axes, split_axis=0, concat_axis=0, tiled=True
    ).reshape(slots_total, width + HALF)
    local_index = jnp.arange(local_rows, dtype=jnp.int32)
    departed = jnp.any(local_index[:, None] == leave_rows[None, :], axis=1)
    local_live = jnp.logical_and(local_index < live_count[0], jnp.logical_not(departed)).astype(F32)
    living = jnp.concatenate([local_live[:, None], arrived[:, width : width + 1].astype(F32)], axis=0)

    edge_ids, floor, order, place_ids, count = order_rows(neighbours, halo_rows)
    place_ids = place_ids.reshape(-1)
    order = order.reshape(-1)
    table, projected, boundary = open_table(latent, arrived[:, :width], 2 * halo_rows, order, edge_in[0, 1])
    blocks = (local_rows - leaving + slots_total) // ROWS

    def layer_args(t):
        return (
            edge_ids,
            floor,
            edge_in[t, 0],
            edge_bias[t][None],
            edge_out[t],
            edge_shift[t][None],
            edge_gain[t][None],
            node_in[t, 0],
            node_in[t, 1],
            node_bias[t][None],
            node_out[t],
            node_shift[t][None],
            node_gain[t][None],
        )

    table, projected, ghosts = first_step(blocks, layer_args(0), table, projected, boundary, edge_in[1, 1])
    return last_step(layer_args(1), table, projected, ghosts, living, place_ids, count)


def solution(mesh):
    rows = P(("gx", "gy", "gz"))
    in_specs = (rows,) * 6 + (P(),) * 10
    return jax.shard_map(local, mesh=mesh, in_specs=in_specs, out_specs=rows, check_vma=False)
```

```python
import functools

import jax
import jax.numpy as jnp
from jax import lax
from jax.experimental import pallas as pl
from jax.experimental.pallas import tpu as pltpu
from jax.sharding import PartitionSpec as P

EPS = 1e-05
F32 = jnp.float32
BF16 = jnp.bfloat16
HALF = 128
ROWS = 32
CHUNK = 256
LAG = 2
GROUP = 8
NODE_ROWS = 256
SPARE = 8
AXES = ("gx", "gy", "gz")
MESH = pl.DeviceIdType.MESH
VMEM_BYTES = 58 * 2**20
VMEM = pl.BlockSpec(memory_space=pltpu.VMEM)
SMEM = pl.BlockSpec(memory_space=pltpu.SMEM)
ANYWHERE = pl.BlockSpec(memory_space=pl.ANY)


def layer_norm(values, feature_gain):
    average = jnp.mean(values, axis=-1, keepdims=True)
    centred = values - average
    spread = jnp.mean(centred * centred, axis=-1, keepdims=True)
    return centred * lax.rsqrt(spread + EPS) * feature_gain


def store_split(pairs, first_row, values):
    count = values.shape[0]
    pairs[pl.ds(2 * first_row, count, stride=2), :] = values[:, :HALF]
    pairs[pl.ds(2 * first_row + 1, count, stride=2), :] = values[:, HALF:]


def load_split(pairs, first_row, count):
    left = pairs[pl.ds(2 * first_row, count, stride=2), :]
    right = pairs[pl.ds(2 * first_row + 1, count, stride=2), :]
    return jnp.concatenate([left, right], axis=1)


def project(rows, weight):
    return jnp.dot(rows, weight, preferred_element_type=F32).astype(BF16)


def copy_rows(source, ids, into, count):
    @pl.loop(0, count // 64)
    def _(block):
        for g in range(64 // GROUP):
            some = ids.at[pl.ds(block * 64 + g * GROUP, GROUP)]
            for e in range(GROUP):
                place = pl.multiple_of(2 * (block * 64 + g * GROUP + e), 2)
                into[pl.ds(place, 2), :] = source[pl.ds(2 * some[e], 2), :]


def find_places(digits, halo_lanes, places, place_ref, count_ref):
    rows = digits.shape[1]
    half_rows = digits.shape[0] // 2
    slots = half_rows - SPARE
    boundary = halo_lanes.shape[1]
    n = NODE_ROWS
    lower = (
        lax.broadcasted_iota(jnp.int32, (n, n), 0) > lax.broadcasted_iota(jnp.int32, (n, n), 1)
    ).astype(BF16)
    lane = lax.broadcasted_iota(jnp.int32, (n, boundary), 1).astype(F32)

    def one_chunk(c, carry):
        used, spare = carry
        first = pl.multiple_of(c * n, n)
        here = pl.ds(first, n)
        largest = jnp.max(
            digits[pl.ds(0, slots), here].astype(F32) + digits[pl.ds(half_rows, slots), here].astype(F32),
            axis=0,
            keepdims=True,
        )
        active = jnp.transpose(jnp.broadcast_to(largest, (HALF, n))) > 0.0
        row_ids = lax.broadcasted_iota(jnp.int32, (n, boundary), 0) + first
        same = (row_ids == halo_lanes[...]).astype(F32)
        listed = jnp.sum(same, axis=1, keepdims=True) > 0.0
        position = jnp.sum(same * lane, axis=1, keepdims=True)
        others = jnp.where(listed, 0.0, jnp.where(active, 1.0, 0.0))
        idle = jnp.where(listed, 0.0, jnp.where(active, 0.0, 1.0))
        before = jnp.dot(lower, others.astype(BF16), preferred_element_type=F32) + used
        behind = jnp.dot(lower, idle.astype(BF16), preferred_element_type=F32) + spare
        place = jnp.where(others > 0.0, boundary + before, rows - 1 - behind)
        place = jnp.where(listed, position, place)
        places[here, :] = place
        place_ref[:, here] = jnp.transpose(place)[:1].astype(jnp.int32)
        return used + jnp.sum(others[:, :1]), spare + jnp.sum(idle[:, :1])

    used, _ = lax.fori_loop(0, rows // n, one_chunk, (jnp.float32(0.0), jnp.float32(0.0)))
    count_ref[0] = used.astype(jnp.int32) + boundary


def apply_places(senders, digits, places, edge_ids, floor_ref, order_ref):
    rows = digits.shape[1]
    half_rows = digits.shape[0] // 2
    slots = half_rows - SPARE
    n = NODE_ROWS

    @pl.loop(0, rows // n)
    def _(c):
        first = pl.multiple_of(c * n, n)
        lanes = lax.broadcasted_iota(jnp.int32, (n, HALF), 1).astype(F32)
        picked = jnp.zeros((2 * half_rows, n), F32)
        for part in range(rows // n):
            here = places[pl.ds(part * n, n), :]
            halves = [
                jnp.where(here == lanes + (first + half * HALF).astype(F32), 1.0, 0.0).astype(BF16)
                for half in range(n // HALF)
            ]
            chosen = jnp.concatenate(halves, axis=1)
            picked = picked + jnp.dot(digits[:, pl.ds(part * n, n)], chosen, preferred_element_type=F32)
        value = picked[:half_rows] * 128.0 + picked[half_rows:]
        here = pl.ds(first, n)
        edge_ids[:, here] = 2 * jnp.clip((value[:slots] - 1.0).astype(jnp.int32), 0, senders - 1)
        order_ref[:, here] = jnp.clip(value[slots : slots + 1].astype(jnp.int32), 0, rows - 1)
        floor = jnp.where(value > 0.5, EPS, jnp.inf).astype(F32)
        floor_ref[here, :] = jnp.transpose(jnp.concatenate([floor] * (HALF // half_rows), axis=0))


def digits_of(neighbours):
    rows, slots = neighbours.shape
    ids = jnp.concatenate(
        [neighbours.T + 1, jnp.arange(rows, dtype=jnp.int32)[None], jnp.zeros((SPARE - 1, rows), jnp.int32)]
    )
    return jnp.concatenate([ids // 128, ids % 128]).astype(BF16)


class Grid:
    def __init__(self):
        self.place = [lax.axis_index(a) for a in AXES]
        self.sizes = [lax.axis_size(a) for a in AXES]

    def inside(self, axis, step):
        return jnp.logical_and(self.place[axis] + step >= 0, self.place[axis] + step < self.sizes[axis])

    def target(self, axis, step):
        return tuple(self.place[a] + (step if a == axis else 0) for a in range(3))

    def present(self, offset):
        found = None
        for a in range(3):
            if offset[a] != 0:
                here = self.inside(a, offset[a])
                found = here if found is None else jnp.logical_and(found, here)
        return found

    def greet(self):
        barrier = pltpu.get_barrier_semaphore()
        friends = jnp.int32(0)
        for axis in range(3):
            for step in (-1, 1):
                friends = friends + self.inside(axis, step).astype(jnp.int32)

                @pl.when(self.inside(axis, step))
                def _():
                    pl.semaphore_signal(barrier, inc=1, device_id=self.target(axis, step), device_id_type=MESH)

        pl.semaphore_wait(barrier, friends)


def number(offset):
    return 9 * (offset[0] + 1) + 3 * (offset[1] + 1) + offset[2] + 1


def moved(offset, axis, step):
    return tuple(offset[a] + (step if a == axis else 0) for a in range(3))


CENTRE = (0, 0, 0)
MIDDLE = [(dx, 0, 0) for dx in (-1, 1)]
SIDES = [(dx, dy, 0) for dx in (0, -1, 1) for dy in (-1, 1)]
ENDS = [(dx, dy, dz) for dx in (0, -1, 1) for dy in (0, -1, 1) for dz in (-1, 1)]


class Exchange:
    def __init__(self, grid, boundary, ghosts, send_sems, recv_sems):
        self.grid, self.boundary, self.ghosts = grid, boundary, ghosts
        self.send_sems, self.recv_sems = send_sems, recv_sems

    def copy(self, offset, axis, step):
        slot = number(moved(offset, axis, -step))
        return pltpu.make_async_remote_copy(
            src_ref=self.boundary if offset == CENTRE else self.ghosts.at[number(offset)],
            dst_ref=self.ghosts.at[slot],
            send_sem=self.send_sems.at[slot],
            recv_sem=self.recv_sems.at[slot],
            device_id=self.grid.target(axis, step),
            device_id_type=MESH,
        )

    def first_axis(self, offset):
        return 0 if offset == CENTRE else 1 if offset in MIDDLE else 2

    def forward(self, offset):
        for axis in range(self.first_axis(offset), 3):
            for step in (-1, 1):

                @pl.when(self.grid.inside(axis, step))
                def _():
                    self.copy(offset, axis, step).start()

    def arrive(self, offset):
        axis = max(a for a in range(3) if offset[a] != 0)
        self.copy(moved(offset, axis, -offset[axis]), axis, -offset[axis]).wait_recv()

    def relay(self, offsets):
        for offset in offsets:

            @pl.when(self.grid.present(offset))
            def _():
                self.arrive(offset)
                self.forward(offset)

    def finish_sends(self):
        for offset in [CENTRE] + MIDDLE + SIDES:
            for axis in range(self.first_axis(offset), 3):
                for step in (-1, 1):
                    there = self.grid.inside(axis, step)
                    if offset != CENTRE:
                        there = jnp.logical_and(there, self.grid.present(offset))

                    @pl.when(there)
                    def _():
                        self.copy(offset, axis, step).wait_send()


class EdgeLayers:
    def __init__(self, rows, slots, refs, scratch):
        self.edge_ids, self.floor = refs["edge_ids"], refs["floor"]
        self.refs = refs
        self.rows, self.slots = rows, slots
        self.edges = slots * ROWS
        self.pairs, self.buffers, self.receive, self.summed, self.raw, self.square, self.weight = scratch
        self.width = self.receive.shape[1]

    def prepare(self, table_ref):
        refs = self.refs
        wide = refs["edge_out"][...].astype(F32)
        self.weight[...] = (wide - jnp.mean(wide, axis=1, keepdims=True)).astype(BF16)

        @pl.loop(0, self.rows // NODE_ROWS)
        def _(i):
            here = pl.ds(pl.multiple_of(i * NODE_ROWS, NODE_ROWS), NODE_ROWS)
            self.summed[here, :] = jnp.zeros((NODE_ROWS, self.width), F32)
            self.receive[here, :] = (
                jnp.dot(table_ref[here, :], refs["receive_weight"][...], preferred_element_type=F32)
                + refs["edge_bias"][...]
            )

    def gather(self, into, block, start, stop):
        first = pl.multiple_of(block * ROWS, ROWS)
        for e in range(start, stop):
            k, r = divmod(e, ROWS)
            if r % GROUP == 0:
                ids = self.edge_ids.at[k, pl.ds(first + r, GROUP)]
            into[pl.ds(2 * e, 2), :] = self.pairs[pl.ds(ids[r % GROUP], 2), :]

    def first_half(self, source, first, chunk, shift):
        per_chunk = CHUNK // ROWS
        own = self.receive[pl.ds(first, ROWS), :]
        left = source[pl.ds(2 * chunk * CHUNK, CHUNK, stride=2), :].reshape(per_chunk, ROWS, HALF)
        right = source[pl.ds(2 * chunk * CHUNK + 1, CHUNK, stride=2), :].reshape(per_chunk, ROWS, HALF)
        left = jnp.maximum(left + own[:, :HALF][None], 0.0).reshape(CHUNK, HALF).astype(BF16)
        right = jnp.maximum(right + own[:, HALF:][None], 0.0).reshape(CHUNK, HALF).astype(BF16)
        active = jnp.concatenate([left, right], axis=1)
        centred = jnp.dot(active, self.weight[...], preferred_element_type=F32) + shift
        total = jnp.sum(
            centred[:, :HALF] * centred[:, :HALF] + centred[:, HALF:] * centred[:, HALF:], axis=1, keepdims=True
        )
        here = pl.ds(chunk * CHUNK, CHUNK)
        self.raw[here, :] = centred
        self.square[here, :] = jnp.broadcast_to(total, (CHUNK, HALF))

    def second_half(self, floor, chunk, sums):
        left, right = sums
        per_chunk = CHUNK // ROWS
        for k in range(chunk * per_chunk, (chunk + 1) * per_chunk):
            here = pl.ds(k * ROWS, ROWS)
            scale = lax.rsqrt(self.square[here, :] * (1.0 / self.width) + floor[:, k : k + 1])
            left = left + self.raw[here, :HALF] * scale
            right = right + self.raw[here, HALF:] * scale
        return left, right

    def one_block(self, block, parity, last_block):
        chunks = self.edges // CHUNK
        first = pl.multiple_of(block * ROWS, ROWS)
        following = jnp.minimum(block + 1, last_block)
        edge_shift = self.refs["edge_shift"]
        shift = edge_shift[...] - jnp.mean(edge_shift[...], axis=1, keepdims=True)
        floor = self.floor[pl.ds(first, ROWS), :]
        sums = (jnp.zeros((ROWS, HALF), F32), jnp.zeros((ROWS, HALF), F32))
        for chunk in range(chunks + LAG):
            if chunk < chunks:
                self.gather(self.buffers[1 - parity], following, chunk * CHUNK, (chunk + 1) * CHUNK)
                self.first_half(self.buffers[parity], first, chunk, shift)
            if chunk >= LAG:
                sums = self.second_half(floor, chunk - LAG, sums)
        self.summed[pl.ds(first, ROWS), :HALF] = sums[0]
        self.summed[pl.ds(first, ROWS), HALF:] = sums[1]


def node_layers(refs, table_ref, summed, here):
    own = table_ref[here, :]
    message = (summed[here, :] * refs["edge_gain"][...]).astype(BF16)
    hidden = (
        jnp.dot(own, refs["node_self"][...], preferred_element_type=F32)
        + jnp.dot(message, refs["node_message"][...], preferred_element_type=F32)
        + refs["node_bias"][...]
    )
    hidden = jnp.maximum(hidden, 0.0).astype(BF16)
    node_raw = jnp.dot(hidden, refs["node_out"][...], preferred_element_type=F32) + refs["node_shift"][...]
    return own.astype(F32) + layer_norm(node_raw, refs["node_gain"][...])


def step_refs(t, edge_ids, floor, weights):
    edge_in, edge_bias, edge_out, edge_shift, edge_gain, node_in, node_bias, node_out, node_shift, node_gain = weights
    row = pl.ds(t, 1)
    return {
        "edge_ids": edge_ids,
        "floor": floor,
        "receive_weight": edge_in.at[t, 0],
        "edge_bias": edge_bias.at[row],
        "edge_out": edge_out.at[t],
        "edge_shift": edge_shift.at[row],
        "edge_gain": edge_gain.at[row],
        "node_self": node_in.at[t, 0],
        "node_message": node_in.at[t, 1],
        "node_bias": node_bias.at[row],
        "node_out": node_out.at[t],
        "node_shift": node_shift.at[row],
        "node_gain": node_gain.at[row],
    }


def edge_scratch(rows, slots, senders, width):
    edges = slots * ROWS
    return [
        pltpu.VMEM((2 * senders, HALF), F32),
        pltpu.VMEM((2 * edges, HALF), F32),
        pltpu.VMEM((2 * edges, HALF), F32),
        pltpu.VMEM((rows, width), F32),
        pltpu.VMEM((rows, width), F32),
        pltpu.VMEM((edges, width), F32),
        pltpu.VMEM((edges, HALF), F32),
        pltpu.VMEM((width, width), BF16),
    ]


def unpack_scratch(scratch):
    pairs, even, odd, receive, summed, raw, square, weight = scratch
    return pairs, (even, odd), receive, summed, raw, square, weight


def spread_block(pairs, first_row, block_ref):
    @pl.loop(0, block_ref.shape[0] // 128)
    def _(piece):
        start = pl.multiple_of(piece * 128, 128)
        store_split(pairs, first_row + start, block_ref[pl.ds(start, 128), :].astype(F32))


def first_step_kernel(slots, blocks, marks, *args):
    latent_ref, arrived_ref, digits, halo_lanes, halo_ids = args[:5]
    weights = args[5:15]
    renewed_ref, next_projected, next_ghosts, edge_lanes, floor_ref, place_ref, count_ref = args[15:22]
    scratch = unpack_scratch(args[22:30])
    (
        ghosts,
        boundary_ref,
        next_boundary,
        original,
        ordered,
        places,
        table_ref,
        order_lanes,
        edge_ids,
        order_ids,
        send_a,
        recv_a,
        send_b,
        recv_b,
        id_sems,
    ) = args[30:]
    pairs, summed = scratch[0], scratch[3]
    local_rows, width = latent_ref.shape
    arrivals = arrived_ref.shape[0]
    rows = local_rows + arrivals
    boundary_rows = boundary_ref.shape[0]
    refs = step_refs(0, edge_ids, floor_ref, weights)
    send_weight, next_weight = weights[0].at[0, 1], weights[0].at[1, 1]
    grid = Grid()
    now = Exchange(grid, boundary_ref, ghosts, send_a, recv_a)
    later = Exchange(grid, next_boundary, next_ghosts, send_b, recv_b)
    layers = EdgeLayers(rows, slots, refs, scratch)
    grid.greet()

    def take(first, values):
        store_split(original, first, values.astype(F32))
        store_split(pairs, first, project(values, send_weight[...]).astype(F32))

    @pl.loop(0, local_rows // NODE_ROWS)
    def _(i):
        first = pl.multiple_of(i * NODE_ROWS, NODE_ROWS)
        take(first, latent_ref[pl.ds(first, NODE_ROWS), :])

    for first in range(0, arrivals, NODE_ROWS):
        take(local_rows + first, arrived_ref[pl.ds(first, NODE_ROWS), :width])
    copy_rows(pairs, halo_ids, ordered, boundary_rows)
    boundary_ref[...] = load_split(ordered, 0, boundary_rows).astype(BF16)
    now.forward(CENTRE)
    find_places(digits, halo_lanes, places, place_ref, count_ref)

    def spread(offset):
        spread_block(pairs, rows + number(offset) * boundary_rows, ghosts.at[number(offset)])

    def spread_all(offsets):
        for offset in offsets:

            @pl.when(grid.present(offset))
            def _():
                spread(offset)

    now.relay(MIDDLE)
    now.relay(SIDES[:2])
    apply_places(pairs.shape[0] // 2, digits, places, edge_lanes, floor_ref, order_lanes)
    fetch_edges = pltpu.make_async_copy(edge_lanes, edge_ids, id_sems.at[0])
    fetch_order = pltpu.make_async_copy(order_lanes, order_ids, id_sems.at[1])
    fetch_edges.start()
    fetch_order.start()
    spread_all(MIDDLE)
    spread_all(SIDES[:2])
    now.relay(SIDES[2:])
    fetch_edges.wait()
    fetch_order.wait()
    copy_rows(original, order_ids.at[0], ordered, rows)

    @pl.loop(0, rows // NODE_ROWS)
    def _(i):
        first = pl.multiple_of(i * NODE_ROWS, NODE_ROWS)
        table_ref[pl.ds(first, NODE_ROWS), :] = load_split(ordered, first, NODE_ROWS).astype(BF16)

    layers.prepare(table_ref)
    spread_all(SIDES[2:])
    for offset in ENDS:

        @pl.when(grid.present(offset))
        def _():
            now.arrive(offset)
            spread(offset)

    layers.gather(layers.buffers[0], 0, 0, layers.edges)

    def renew(first):
        here = pl.ds(first, NODE_ROWS)
        renewed = node_layers(refs, table_ref, summed, here).astype(BF16)
        renewed_ref[here, :] = renewed
        projected = project(renewed, next_weight[...])
        next_projected[here, :] = projected
        return projected

    @pl.loop(0, blocks // 2)
    def _(pair):
        @pl.when(pair == marks[0])
        def _():
            for first in range(0, boundary_rows, NODE_ROWS):
                next_boundary[pl.ds(first, NODE_ROWS), :] = renew(first)
            later.forward(CENTRE)

        for mark, offsets in zip(marks[1:], (MIDDLE, SIDES[:2], SIDES[2:])):

            @pl.when(pair == mark)
            def _():
                later.relay(offsets)

        for parity in range(2):
            block = 2 * pair + parity

            @pl.when(block < blocks + grid.place[0])
            def _():
                layers.one_block(block, parity, blocks - 1)

    @pl.loop(boundary_rows // NODE_ROWS, rows // NODE_ROWS)
    def _(i):
        renew(pl.multiple_of(i * NODE_ROWS, NODE_ROWS))

    for offset in ENDS:

        @pl.when(grid.present(offset))
        def _():
            later.arrive(offset)

    now.finish_sends()
    later.finish_sends()


def first_step(blocks, latent, arrived, digits, halo_rows, weights):
    local_rows, width = latent.shape
    rows = local_rows + arrived.shape[0]
    slots = digits.shape[0] // 2 - SPARE
    count = halo_rows.shape[0]
    first_pair = count // ROWS // 2
    rest = blocks // 2 - first_pair
    marks = (first_pair, first_pair + rest * 5 // 26, first_pair + rest * 7 // 26, first_pair + rest * 14 // 26)
    return pl.pallas_call(
        functools.partial(first_step_kernel, slots, blocks, marks),
        out_shape=(
            jax.ShapeDtypeStruct((rows, width), BF16),
            jax.ShapeDtypeStruct((rows, width), BF16),
            jax.ShapeDtypeStruct((27, count, width), BF16),
            jax.ShapeDtypeStruct((slots, rows), jnp.int32),
            jax.ShapeDtypeStruct((rows, HALF), F32),
            jax.ShapeDtypeStruct((1, rows), jnp.int32),
            jax.ShapeDtypeStruct((1,), jnp.int32),
        ),
        in_specs=[VMEM] * 4 + [SMEM] + [VMEM] * 10,
        out_specs=(VMEM, VMEM, ANYWHERE, VMEM, VMEM, VMEM, SMEM),
        scratch_shapes=edge_scratch(rows, slots, rows + 27 * count, width)
        + [
            pltpu.VMEM((27, count, width), BF16),
            pltpu.VMEM((count, width), BF16),
            pltpu.VMEM((count, width), BF16),
            pltpu.VMEM((2 * rows, HALF), F32),
            pltpu.VMEM((2 * rows, HALF), F32),
            pltpu.VMEM((rows, HALF), F32),
            pltpu.VMEM((rows, width), BF16),
            pltpu.VMEM((1, rows), jnp.int32),
            pltpu.SMEM((slots, rows), jnp.int32),
            pltpu.SMEM((1, rows), jnp.int32),
        ]
        + [pltpu.SemaphoreType.DMA((27,))] * 4
        + [pltpu.SemaphoreType.DMA((2,))],
        compiler_params=pltpu.CompilerParams(
            collective_id=0, has_side_effects=True, vmem_limit_bytes=VMEM_BYTES
        ),
        name="first_step",
    )(latent, arrived, digits, halo_rows[None, :], halo_rows, *weights)


def last_step_kernel(slots, *args):
    edge_ids, floor_ref, table_ref, projected_ref, ghosts = args[:5]
    place_ids, count_ref, live_count, leave_lanes, arrived_ref = args[5:10]
    weights = args[10:20]
    updated_ref = args[20]
    scratch = unpack_scratch(args[21:29])
    staged, ordered, sems = args[29:]
    refs = step_refs(1, edge_ids, floor_ref, weights)
    pairs, summed = scratch[0], scratch[3]
    rows, width = table_ref.shape
    local_rows = rows - arrived_ref.shape[0]
    ghost_blocks, ghost_rows = ghosts.shape[0], ghosts.shape[1]
    centre = ghost_blocks // 2
    layers = EdgeLayers(rows, slots, refs, scratch)

    def fetch(block):
        return pltpu.make_async_copy(ghosts.at[block], staged.at[block], sems.at[block])

    for block in range(ghost_blocks):
        if block != centre:
            fetch(block).start()
    layers.prepare(table_ref)

    @pl.loop(0, rows // NODE_ROWS)
    def _(i):
        first = pl.multiple_of(i * NODE_ROWS, NODE_ROWS)
        store_split(ordered, first, projected_ref[pl.ds(first, NODE_ROWS), :].astype(F32))

    copy_rows(ordered, place_ids.at[0], pairs, rows)

    @pl.loop(0, ghost_blocks)
    def _(block):
        @pl.when(block != centre)
        def _():
            fetch(block).wait()
            spread_block(pairs, pl.multiple_of(rows + block * ghost_rows, ghost_rows), staged.at[block])

    blocks = (count_ref[0] + ROWS - 1) // ROWS
    layers.gather(layers.buffers[0], 0, 0, layers.edges)

    @pl.loop(0, (blocks + 1) // 2)
    def _(pair):
        for parity in range(2):
            block = 2 * pair + parity

            @pl.when(block < blocks)
            def _():
                layers.one_block(block, parity, rows // ROWS - 1)

    @pl.loop(0, rows // NODE_ROWS)
    def _(i):
        first = pl.multiple_of(i * NODE_ROWS, NODE_ROWS)
        renewed = node_layers(refs, table_ref, summed, pl.ds(first, NODE_ROWS))
        store_split(ordered, first, renewed)

    copy_rows(ordered, place_ids.at[0], pairs, rows)

    @pl.loop(0, local_rows // NODE_ROWS)
    def _(i):
        first = pl.multiple_of(i * NODE_ROWS, NODE_ROWS)
        row_ids = lax.broadcasted_iota(jnp.int32, (NODE_ROWS, leave_lanes.shape[1]), 0) + first
        leaves = jnp.max((row_ids == leave_lanes[...]).astype(F32), axis=1, keepdims=True)
        living = jnp.where(row_ids[:, :1] < live_count[0], 1.0 - leaves, 0.0)
        updated_ref[pl.ds(first, NODE_ROWS), :] = (load_split(pairs, first, NODE_ROWS) * living).astype(BF16)

    for first in range(0, rows - local_rows, NODE_ROWS):
        living = arrived_ref[pl.ds(first, NODE_ROWS), width : width + 1].astype(F32)
        updated_ref[pl.ds(local_rows + first, NODE_ROWS), :] = (
            load_split(pairs, local_rows + first, NODE_ROWS) * living
        ).astype(BF16)


def last_step(edge_ids, floor, table, projected, ghosts, place_ids, count, live_count, leave_rows, arrived, weights):
    rows, width = table.shape
    slots = edge_ids.shape[0]
    return pl.pallas_call(
        functools.partial(last_step_kernel, slots),
        out_shape=jax.ShapeDtypeStruct((rows, width), BF16),
        in_specs=[SMEM, VMEM, VMEM, VMEM, ANYWHERE, SMEM, SMEM, SMEM] + [VMEM] * 12,
        out_specs=VMEM,
        scratch_shapes=edge_scratch(rows, slots, rows + ghosts.shape[0] * ghosts.shape[1], width)
        + [
            pltpu.VMEM(ghosts.shape, BF16),
            pltpu.VMEM((2 * rows, HALF), F32),
            pltpu.SemaphoreType.DMA((ghosts.shape[0],)),
        ],
        compiler_params=pltpu.CompilerParams(vmem_limit_bytes=VMEM_BYTES),
        name="last_step",
    )(
        edge_ids,
        floor,
        table,
        projected,
        ghosts,
        place_ids,
        count,
        live_count,
        leave_rows[None, :],
        arrived,
        *weights,
    )


def pick_rows(source_rows, row_ids):
    selector = (
        row_ids[:, None] == jnp.arange(source_rows.shape[0], dtype=jnp.int32)[None, :]
    ).astype(source_rows.dtype)
    return jnp.dot(selector, source_rows, preferred_element_type=F32).astype(source_rows.dtype)


def local(
    latent,
    live_count,
    leave_rows,
    leave_target,
    halo_rows,
    neighbours,
    edge_in,
    edge_bias,
    edge_out,
    edge_shift,
    edge_gain,
    node_in,
    node_bias,
    node_out,
    node_shift,
    node_gain,
):
    axes = ("gx", "gy", "gz")
    devices = lax.axis_size(axes)
    local_rows, width = latent.shape
    table_rows, slots = neighbours.shape
    slots_total = table_rows - local_rows
    capacity = slots_total // devices
    leaving = leave_rows.shape[0]
    target_domain = leave_target[:, 0]
    entry = jnp.arange(leaving, dtype=jnp.int32)
    earlier = entry[None, :] < entry[:, None]
    same_target = target_domain[:, None] == target_domain[None, :]
    row_rank = jnp.sum(jnp.logical_and(same_target, earlier).astype(jnp.int32), axis=1)
    position = target_domain * capacity + row_rank
    moving = pick_rows(latent, leave_rows)
    moving = jnp.concatenate([moving, jnp.ones((leaving, HALF), BF16)], axis=1)
    placement = jnp.arange(slots_total, dtype=jnp.int32)[:, None] == position[None, :]
    outgoing = jnp.dot(placement.astype(BF16), moving, preferred_element_type=F32).astype(BF16)
    arrived = lax.all_to_all(
        outgoing.reshape(devices, capacity, width + HALF), axes, split_axis=0, concat_axis=0, tiled=True
    ).reshape(slots_total, width + HALF)
    weights = (
        edge_in,
        edge_bias,
        edge_out,
        edge_shift,
        edge_gain,
        node_in,
        node_bias,
        node_out,
        node_shift,
        node_gain,
    )
    blocks = (local_rows - leaving + slots_total) // ROWS
    table, projected, ghosts, edge_ids, floor, place_ids, count = first_step(
        blocks, latent, arrived, digits_of(neighbours), halo_rows, weights
    )
    return last_step(
        edge_ids, floor, table, projected, ghosts, place_ids, count, live_count, leave_rows, arrived, weights
    )


def solution(mesh):
    rows = P(("gx", "gy", "gz"))
    in_specs = (rows,) * 6 + (P(),) * 10
    return jax.shard_map(local, mesh=mesh, in_specs=in_specs, out_specs=rows, check_vma=False)
```

```python
import functools

import jax
import jax.numpy as jnp
from jax import lax
from jax.experimental import pallas as pl
from jax.experimental.pallas import tpu as pltpu
from jax.sharding import PartitionSpec as P

EPS = 1e-05
F32 = jnp.float32
BF16 = jnp.bfloat16
HALF = 128
ROWS = 32
CHUNK = 256
LAG = 2
GROUP = 8
NODE_ROWS = 256
SPARE = 8
AXES = ("gx", "gy", "gz")
MESH = pl.DeviceIdType.MESH
VMEM_BYTES = 58 * 2**20
VMEM = pl.BlockSpec(memory_space=pltpu.VMEM)
SMEM = pl.BlockSpec(memory_space=pltpu.SMEM)
ANYWHERE = pl.BlockSpec(memory_space=pl.ANY)


def layer_norm(values, feature_gain):
    average = jnp.mean(values, axis=-1, keepdims=True)
    centred = values - average
    spread = jnp.mean(centred * centred, axis=-1, keepdims=True)
    return centred * lax.rsqrt(spread + EPS) * feature_gain


def store_split(pairs, first_row, values):
    count = values.shape[0]
    pairs[pl.ds(2 * first_row, count, stride=2), :] = values[:, :HALF]
    pairs[pl.ds(2 * first_row + 1, count, stride=2), :] = values[:, HALF:]


def load_split(pairs, first_row, count):
    left = pairs[pl.ds(2 * first_row, count, stride=2), :]
    right = pairs[pl.ds(2 * first_row + 1, count, stride=2), :]
    return jnp.concatenate([left, right], axis=1)


def project(rows, weight):
    return jnp.dot(rows, weight, preferred_element_type=F32).astype(BF16)


def copy_rows(source, ids, into, count):
    @pl.loop(0, count // 64)
    def _(block):
        for g in range(64 // GROUP):
            some = ids.at[pl.ds(block * 64 + g * GROUP, GROUP)]
            for e in range(GROUP):
                place = pl.multiple_of(2 * (block * 64 + g * GROUP + e), 2)
                into[pl.ds(place, 2), :] = source[pl.ds(2 * some[e], 2), :]


def find_places(digits, halo_lanes, places, place_ref, count_ref):
    rows = digits.shape[1]
    half_rows = digits.shape[0] // 2
    slots = half_rows - SPARE
    boundary = halo_lanes.shape[1]
    n = NODE_ROWS
    lower = (
        lax.broadcasted_iota(jnp.int32, (n, n), 0) > lax.broadcasted_iota(jnp.int32, (n, n), 1)
    ).astype(BF16)
    lane = lax.broadcasted_iota(jnp.int32, (n, boundary), 1).astype(F32)

    def one_chunk(c, carry):
        used, spare = carry
        first = pl.multiple_of(c * n, n)
        here = pl.ds(first, n)
        largest = jnp.max(
            digits[pl.ds(0, slots), here].astype(F32) + digits[pl.ds(half_rows, slots), here].astype(F32),
            axis=0,
            keepdims=True,
        )
        active = jnp.transpose(jnp.broadcast_to(largest, (HALF, n))) > 0.0
        row_ids = lax.broadcasted_iota(jnp.int32, (n, boundary), 0) + first
        same = (row_ids == halo_lanes[...]).astype(F32)
        listed = jnp.sum(same, axis=1, keepdims=True) > 0.0
        position = jnp.sum(same * lane, axis=1, keepdims=True)
        others = jnp.where(listed, 0.0, jnp.where(active, 1.0, 0.0))
        idle = jnp.where(listed, 0.0, jnp.where(active, 0.0, 1.0))
        before = jnp.dot(lower, others.astype(BF16), preferred_element_type=F32) + used
        behind = jnp.dot(lower, idle.astype(BF16), preferred_element_type=F32) + spare
        place = jnp.where(others > 0.0, boundary + before, rows - 1 - behind)
        place = jnp.where(listed, position, place)
        places[here, :] = place
        place_ref[:, here] = jnp.transpose(place)[:1].astype(jnp.int32)
        return used + jnp.sum(others[:, :1]), spare + jnp.sum(idle[:, :1])

    used, _ = lax.fori_loop(0, rows // n, one_chunk, (jnp.float32(0.0), jnp.float32(0.0)))
    count_ref[0] = used.astype(jnp.int32) + boundary


def apply_places(senders, digits, places, edge_ids, floor_ref, order_ref):
    rows = digits.shape[1]
    half_rows = digits.shape[0] // 2
    slots = half_rows - SPARE
    n = NODE_ROWS

    @pl.loop(0, rows // n)
    def _(c):
        first = pl.multiple_of(c * n, n)
        lanes = lax.broadcasted_iota(jnp.int32, (n, HALF), 1).astype(F32)
        picked = jnp.zeros((2 * half_rows, n), F32)
        for part in range(rows // n):
            here = places[pl.ds(part * n, n), :]
            halves = [
                jnp.where(here == lanes + (first + half * HALF).astype(F32), 1.0, 0.0).astype(BF16)
                for half in range(n // HALF)
            ]
            chosen = jnp.concatenate(halves, axis=1)
            picked = picked + jnp.dot(digits[:, pl.ds(part * n, n)], chosen, preferred_element_type=F32)
        value = picked[:half_rows] * 128.0 + picked[half_rows:]
        here = pl.ds(first, n)
        edge_ids[:, here] = 2 * jnp.clip((value[:slots] - 1.0).astype(jnp.int32), 0, senders - 1)
        order_ref[:, here] = jnp.clip(value[slots : slots + 1].astype(jnp.int32), 0, rows - 1)
        floor = jnp.where(value > 0.5, EPS, jnp.inf).astype(F32)
        floor_ref[here, :] = jnp.transpose(jnp.concatenate([floor] * (HALF // half_rows), axis=0))


def digits_of(neighbours):
    rows, slots = neighbours.shape
    ids = jnp.concatenate(
        [neighbours.T + 1, jnp.arange(rows, dtype=jnp.int32)[None], jnp.zeros((SPARE - 1, rows), jnp.int32)]
    )
    return jnp.concatenate([ids // 128, ids % 128]).astype(BF16)


class Grid:
    def __init__(self):
        self.place = [lax.axis_index(a) for a in AXES]
        self.sizes = [lax.axis_size(a) for a in AXES]

    def inside(self, axis, step):
        return jnp.logical_and(self.place[axis] + step >= 0, self.place[axis] + step < self.sizes[axis])

    def target(self, axis, step):
        return tuple(self.place[a] + (step if a == axis else 0) for a in range(3))

    def present(self, offset):
        found = None
        for a in range(3):
            if offset[a] != 0:
                here = self.inside(a, offset[a])
                found = here if found is None else jnp.logical_and(found, here)
        return found

    def greet(self):
        barrier = pltpu.get_barrier_semaphore()
        friends = jnp.int32(0)
        for axis in range(3):
            for step in (-1, 1):
                friends = friends + self.inside(axis, step).astype(jnp.int32)

                @pl.when(self.inside(axis, step))
                def _():
                    pl.semaphore_signal(barrier, inc=1, device_id=self.target(axis, step), device_id_type=MESH)

        pl.semaphore_wait(barrier, friends)


def number(offset):
    return 9 * (offset[0] + 1) + 3 * (offset[1] + 1) + offset[2] + 1


def moved(offset, axis, step):
    return tuple(offset[a] + (step if a == axis else 0) for a in range(3))


CENTRE = (0, 0, 0)
OFFSETS = [(dx, dy, dz) for dx in (-1, 0, 1) for dy in (-1, 0, 1) for dz in (-1, 0, 1)]
ALONG = [o for o in OFFSETS if o[:2] == (0, 0) and o[2] != 0]
FACES = [o for o in OFFSETS if o[2] == 0 and abs(o[0]) + abs(o[1]) == 1]
CORNERS = [o for o in OFFSETS if o[2] == 0 and o[0] != 0 and o[1] != 0]
ENDS = [o for o in OFFSETS if o[2] != 0 and o[:2] != (0, 0)]


class Exchange:
    def __init__(self, grid, boundary, ghosts, send_sems, recv_sems):
        self.grid, self.boundary, self.ghosts = grid, boundary, ghosts
        self.send_sems, self.recv_sems = send_sems, recv_sems

    def copy(self, offset, axis, step):
        slot = number(moved(offset, axis, -step))
        return pltpu.make_async_remote_copy(
            src_ref=self.boundary if offset == CENTRE else self.ghosts.at[number(offset)],
            dst_ref=self.ghosts.at[slot],
            send_sem=self.send_sems.at[slot],
            recv_sem=self.recv_sems.at[slot],
            device_id=self.grid.target(axis, step),
            device_id_type=MESH,
        )

    def on_chip(self, step):
        return lax.rem(self.grid.place[2], 2) == (0 if step == 1 else 1)

    def last_hops(self, offset):
        dx, dy, dz = offset
        if dz == 0:
            if dx != 0 and dy != 0:
                return [(1 if dx == dy else 0, None)]
            return [(0 if dx != 0 else 1, None)]
        if (dx != 0) == (dy != 0):
            return [(2, None)]
        near = self.on_chip(dz)
        return [(2, near), (0 if dx != 0 else 1, jnp.logical_not(near))]

    def hops_from(self, offset):
        found = []
        for axis in range(3):
            if offset[axis] != 0:
                continue
            for step in (-1, 1):
                dx, dy, dz = reached = moved(offset, axis, -step)
                there = self.grid.inside(axis, step)
                if offset != CENTRE:
                    there = jnp.logical_and(there, self.grid.present(offset))
                if dz != 0 and (dx != 0) != (dy != 0):
                    near = self.on_chip(step if axis == 2 else dz)
                    there = jnp.logical_and(there, near if axis == 2 else jnp.logical_not(near))
                elif axis not in [a for a, _ in self.last_hops(reached)]:
                    continue
                found.append((axis, step, there))
        return found

    def forward(self, offset):
        for axis, step, there in self.hops_from(offset):

            @pl.when(there)
            def _():
                self.copy(offset, axis, step).start()

    def arrive(self, offset):
        for axis, condition in self.last_hops(offset):
            there = self.grid.present(offset)
            if condition is not None:
                there = jnp.logical_and(there, condition)

            @pl.when(there)
            def _():
                self.copy(moved(offset, axis, -offset[axis]), axis, -offset[axis]).wait_recv()

    def relay(self, offsets):
        for offset in offsets:
            self.arrive(offset)
            self.forward(offset)

    def finish_sends(self):
        for offset in [CENTRE] + ALONG + FACES + CORNERS:
            for axis, step, there in self.hops_from(offset):

                @pl.when(there)
                def _():
                    self.copy(offset, axis, step).wait_send()


class EdgeLayers:
    def __init__(self, rows, slots, refs, scratch):
        self.edge_ids, self.floor = refs["edge_ids"], refs["floor"]
        self.refs = refs
        self.rows, self.slots = rows, slots
        self.edges = slots * ROWS
        self.pairs, self.buffers, self.receive, self.summed, self.raw, self.square, self.weight = scratch
        self.width = self.receive.shape[1]

    def prepare(self, table_ref):
        refs = self.refs
        wide = refs["edge_out"][...].astype(F32)
        self.weight[...] = (wide - jnp.mean(wide, axis=1, keepdims=True)).astype(BF16)

        @pl.loop(0, self.rows // NODE_ROWS)
        def _(i):
            here = pl.ds(pl.multiple_of(i * NODE_ROWS, NODE_ROWS), NODE_ROWS)
            self.summed[here, :] = jnp.zeros((NODE_ROWS, self.width), F32)
            self.receive[here, :] = (
                jnp.dot(table_ref[here, :], refs["receive_weight"][...], preferred_element_type=F32)
                + refs["edge_bias"][...]
            )

    def gather(self, into, block, start, stop):
        first = pl.multiple_of(block * ROWS, ROWS)
        for e in range(start, stop):
            k, r = divmod(e, ROWS)
            if r % GROUP == 0:
                ids = self.edge_ids.at[k, pl.ds(first + r, GROUP)]
            into[pl.ds(2 * e, 2), :] = self.pairs[pl.ds(ids[r % GROUP], 2), :]

    def first_half(self, source, first, chunk, shift):
        per_chunk = CHUNK // ROWS
        own = self.receive[pl.ds(first, ROWS), :]
        left = source[pl.ds(2 * chunk * CHUNK, CHUNK, stride=2), :].reshape(per_chunk, ROWS, HALF)
        right = source[pl.ds(2 * chunk * CHUNK + 1, CHUNK, stride=2), :].reshape(per_chunk, ROWS, HALF)
        left = jnp.maximum(left + own[:, :HALF][None], 0.0).reshape(CHUNK, HALF).astype(BF16)
        right = jnp.maximum(right + own[:, HALF:][None], 0.0).reshape(CHUNK, HALF).astype(BF16)
        active = jnp.concatenate([left, right], axis=1)
        centred = jnp.dot(active, self.weight[...], preferred_element_type=F32) + shift
        total = jnp.sum(
            centred[:, :HALF] * centred[:, :HALF] + centred[:, HALF:] * centred[:, HALF:], axis=1, keepdims=True
        )
        here = pl.ds(chunk * CHUNK, CHUNK)
        self.raw[here, :] = centred
        self.square[here, :] = jnp.broadcast_to(total, (CHUNK, HALF))

    def second_half(self, floor, chunk, sums):
        left, right = sums
        per_chunk = CHUNK // ROWS
        for k in range(chunk * per_chunk, (chunk + 1) * per_chunk):
            here = pl.ds(k * ROWS, ROWS)
            scale = lax.rsqrt(self.square[here, :] * (1.0 / self.width) + floor[:, k : k + 1])
            left = left + self.raw[here, :HALF] * scale
            right = right + self.raw[here, HALF:] * scale
        return left, right

    def one_block(self, block, parity, last_block):
        chunks = self.edges // CHUNK
        first = pl.multiple_of(block * ROWS, ROWS)
        following = jnp.minimum(block + 1, last_block)
        edge_shift = self.refs["edge_shift"]
        shift = edge_shift[...] - jnp.mean(edge_shift[...], axis=1, keepdims=True)
        floor = self.floor[pl.ds(first, ROWS), :]
        sums = (jnp.zeros((ROWS, HALF), F32), jnp.zeros((ROWS, HALF), F32))
        for chunk in range(chunks + LAG):
            if chunk < chunks:
                self.gather(self.buffers[1 - parity], following, chunk * CHUNK, (chunk + 1) * CHUNK)
                self.first_half(self.buffers[parity], first, chunk, shift)
            if chunk >= LAG:
                sums = self.second_half(floor, chunk - LAG, sums)
        self.summed[pl.ds(first, ROWS), :HALF] = sums[0]
        self.summed[pl.ds(first, ROWS), HALF:] = sums[1]


def node_layers(refs, table_ref, summed, here):
    own = table_ref[here, :]
    message = (summed[here, :] * refs["edge_gain"][...]).astype(BF16)
    hidden = (
        jnp.dot(own, refs["node_self"][...], preferred_element_type=F32)
        + jnp.dot(message, refs["node_message"][...], preferred_element_type=F32)
        + refs["node_bias"][...]
    )
    hidden = jnp.maximum(hidden, 0.0).astype(BF16)
    node_raw = jnp.dot(hidden, refs["node_out"][...], preferred_element_type=F32) + refs["node_shift"][...]
    return own.astype(F32) + layer_norm(node_raw, refs["node_gain"][...])


def step_refs(t, edge_ids, floor, weights):
    edge_in, edge_bias, edge_out, edge_shift, edge_gain, node_in, node_bias, node_out, node_shift, node_gain = weights
    row = pl.ds(t, 1)
    return {
        "edge_ids": edge_ids,
        "floor": floor,
        "receive_weight": edge_in.at[t, 0],
        "edge_bias": edge_bias.at[row],
        "edge_out": edge_out.at[t],
        "edge_shift": edge_shift.at[row],
        "edge_gain": edge_gain.at[row],
        "node_self": node_in.at[t, 0],
        "node_message": node_in.at[t, 1],
        "node_bias": node_bias.at[row],
        "node_out": node_out.at[t],
        "node_shift": node_shift.at[row],
        "node_gain": node_gain.at[row],
    }


def edge_scratch(rows, slots, senders, width):
    edges = slots * ROWS
    return [
        pltpu.VMEM((2 * senders, HALF), F32),
        pltpu.VMEM((2 * edges, HALF), F32),
        pltpu.VMEM((2 * edges, HALF), F32),
        pltpu.VMEM((rows, width), F32),
        pltpu.VMEM((rows, width), F32),
        pltpu.VMEM((edges, width), F32),
        pltpu.VMEM((edges, HALF), F32),
        pltpu.VMEM((width, width), BF16),
    ]


def unpack_scratch(scratch):
    pairs, even, odd, receive, summed, raw, square, weight = scratch
    return pairs, (even, odd), receive, summed, raw, square, weight


def spread_block(pairs, first_row, block_ref):
    @pl.loop(0, block_ref.shape[0] // 128)
    def _(piece):
        start = pl.multiple_of(piece * 128, 128)
        store_split(pairs, first_row + start, block_ref[pl.ds(start, 128), :].astype(F32))


def first_step_kernel(slots, blocks, marks, *args):
    latent_ref, arrived_ref, digits, halo_lanes, halo_ids = args[:5]
    weights = args[5:15]
    renewed_ref, next_projected, next_ghosts, edge_lanes, floor_ref, place_ref, count_ref = args[15:22]
    scratch = unpack_scratch(args[22:30])
    (
        ghosts,
        boundary_ref,
        next_boundary,
        original,
        ordered,
        places,
        table_ref,
        order_lanes,
        edge_ids,
        order_ids,
        send_a,
        recv_a,
        send_b,
        recv_b,
        id_sems,
    ) = args[30:]
    pairs, summed = scratch[0], scratch[3]
    local_rows, width = latent_ref.shape
    arrivals = arrived_ref.shape[0]
    rows = local_rows + arrivals
    boundary_rows = boundary_ref.shape[0]
    refs = step_refs(0, edge_ids, floor_ref, weights)
    send_weight, next_weight = weights[0].at[0, 1], weights[0].at[1, 1]
    grid = Grid()
    now = Exchange(grid, boundary_ref, ghosts, send_a, recv_a)
    later = Exchange(grid, next_boundary, next_ghosts, send_b, recv_b)
    layers = EdgeLayers(rows, slots, refs, scratch)
    grid.greet()

    def sources(take):
        @pl.loop(0, local_rows // NODE_ROWS)
        def _(i):
            first = pl.multiple_of(i * NODE_ROWS, NODE_ROWS)
            take(first, latent_ref[pl.ds(first, NODE_ROWS), :])

        for first in range(0, arrivals, NODE_ROWS):
            take(local_rows + first, arrived_ref[pl.ds(first, NODE_ROWS), :width])

    sources(lambda first, values: store_split(original, first, values.astype(F32)))
    copy_rows(original, halo_ids, ordered, boundary_rows)
    for first in range(0, boundary_rows, NODE_ROWS):
        values = load_split(ordered, first, NODE_ROWS).astype(BF16)
        boundary_ref[pl.ds(first, NODE_ROWS), :] = project(values, send_weight[...])
    now.forward(CENTRE)
    sources(lambda first, values: store_split(pairs, first, project(values, send_weight[...]).astype(F32)))
    now.relay(ALONG)
    find_places(digits, halo_lanes, places, place_ref, count_ref)

    def spread(offset):
        spread_block(pairs, rows + number(offset) * boundary_rows, ghosts.at[number(offset)])

    def spread_all(offsets):
        for offset in offsets:

            @pl.when(grid.present(offset))
            def _():
                spread(offset)

    now.relay(FACES)
    apply_places(pairs.shape[0] // 2, digits, places, edge_lanes, floor_ref, order_lanes)
    fetch_edges = pltpu.make_async_copy(edge_lanes, edge_ids, id_sems.at[0])
    fetch_order = pltpu.make_async_copy(order_lanes, order_ids, id_sems.at[1])
    fetch_edges.start()
    fetch_order.start()
    now.relay(CORNERS)
    spread_all(ALONG)
    spread_all(FACES)
    fetch_edges.wait()
    fetch_order.wait()
    copy_rows(original, order_ids.at[0], ordered, rows)

    @pl.loop(0, rows // NODE_ROWS)
    def _(i):
        first = pl.multiple_of(i * NODE_ROWS, NODE_ROWS)
        table_ref[pl.ds(first, NODE_ROWS), :] = load_split(ordered, first, NODE_ROWS).astype(BF16)

    layers.prepare(table_ref)
    spread_all(CORNERS)
    for offset in ENDS:
        now.arrive(offset)
        spread_all([offset])

    layers.gather(layers.buffers[0], 0, 0, layers.edges)

    def renew(first):
        here = pl.ds(first, NODE_ROWS)
        renewed = node_layers(refs, table_ref, summed, here).astype(BF16)
        renewed_ref[here, :] = renewed
        projected = project(renewed, next_weight[...])
        next_projected[here, :] = projected
        return projected

    @pl.loop(0, blocks // 2)
    def _(pair):
        @pl.when(pair == marks[0])
        def _():
            for first in range(0, boundary_rows, NODE_ROWS):
                next_boundary[pl.ds(first, NODE_ROWS), :] = renew(first)
            later.forward(CENTRE)

        for mark, offsets in zip(marks[1:], (ALONG, FACES, CORNERS)):

            @pl.when(pair == mark)
            def _():
                later.relay(offsets)

        for parity in range(2):
            block = 2 * pair + parity

            @pl.when(block < blocks + grid.place[0])
            def _():
                layers.one_block(block, parity, blocks - 1)

    @pl.loop(boundary_rows // NODE_ROWS, rows // NODE_ROWS)
    def _(i):
        renew(pl.multiple_of(i * NODE_ROWS, NODE_ROWS))

    for offset in ENDS:
        later.arrive(offset)

    now.finish_sends()
    later.finish_sends()


def first_step(blocks, latent, arrived, digits, halo_rows, weights):
    local_rows, width = latent.shape
    rows = local_rows + arrived.shape[0]
    slots = digits.shape[0] // 2 - SPARE
    count = halo_rows.shape[0]
    first_pair = count // ROWS // 2
    rest = blocks // 2 - first_pair
    marks = (first_pair, first_pair + rest * 4 // 26, first_pair + rest * 6 // 26, first_pair + rest * 10 // 26)
    return pl.pallas_call(
        functools.partial(first_step_kernel, slots, blocks, marks),
        out_shape=(
            jax.ShapeDtypeStruct((rows, width), BF16),
            jax.ShapeDtypeStruct((rows, width), BF16),
            jax.ShapeDtypeStruct((27, count, width), BF16),
            jax.ShapeDtypeStruct((slots, rows), jnp.int32),
            jax.ShapeDtypeStruct((rows, HALF), F32),
            jax.ShapeDtypeStruct((1, rows), jnp.int32),
            jax.ShapeDtypeStruct((1,), jnp.int32),
        ),
        in_specs=[VMEM] * 4 + [SMEM] + [VMEM] * 10,
        out_specs=(VMEM, VMEM, ANYWHERE, VMEM, VMEM, VMEM, SMEM),
        scratch_shapes=edge_scratch(rows, slots, rows + 27 * count, width)
        + [
            pltpu.VMEM((27, count, width), BF16),
            pltpu.VMEM((count, width), BF16),
            pltpu.VMEM((count, width), BF16),
            pltpu.VMEM((2 * rows, HALF), F32),
            pltpu.VMEM((2 * rows, HALF), F32),
            pltpu.VMEM((rows, HALF), F32),
            pltpu.VMEM((rows, width), BF16),
            pltpu.VMEM((1, rows), jnp.int32),
            pltpu.SMEM((slots, rows), jnp.int32),
            pltpu.SMEM((1, rows), jnp.int32),
        ]
        + [pltpu.SemaphoreType.DMA((27,))] * 4
        + [pltpu.SemaphoreType.DMA((2,))],
        compiler_params=pltpu.CompilerParams(
            collective_id=0, has_side_effects=True, vmem_limit_bytes=VMEM_BYTES
        ),
        name="first_step",
    )(latent, arrived, digits, halo_rows[None, :], halo_rows, *weights)


def last_step_kernel(slots, *args):
    edge_ids, floor_ref, table_ref, projected_ref, ghosts = args[:5]
    place_ids, count_ref, live_count, leave_lanes, arrived_ref = args[5:10]
    weights = args[10:20]
    updated_ref = args[20]
    scratch = unpack_scratch(args[21:29])
    staged, ordered, sems = args[29:]
    refs = step_refs(1, edge_ids, floor_ref, weights)
    pairs, summed = scratch[0], scratch[3]
    rows, width = table_ref.shape
    local_rows = rows - arrived_ref.shape[0]
    ghost_blocks, ghost_rows = ghosts.shape[0], ghosts.shape[1]
    centre = ghost_blocks // 2
    layers = EdgeLayers(rows, slots, refs, scratch)

    def fetch(block):
        return pltpu.make_async_copy(ghosts.at[block], staged.at[block], sems.at[block])

    for block in range(ghost_blocks):
        if block != centre:
            fetch(block).start()
    layers.prepare(table_ref)

    @pl.loop(0, rows // NODE_ROWS)
    def _(i):
        first = pl.multiple_of(i * NODE_ROWS, NODE_ROWS)
        store_split(ordered, first, projected_ref[pl.ds(first, NODE_ROWS), :].astype(F32))

    copy_rows(ordered, place_ids.at[0], pairs, rows)

    @pl.loop(0, ghost_blocks)
    def _(block):
        @pl.when(block != centre)
        def _():
            fetch(block).wait()
            spread_block(pairs, pl.multiple_of(rows + block * ghost_rows, ghost_rows), staged.at[block])

    blocks = (count_ref[0] + ROWS - 1) // ROWS
    layers.gather(layers.buffers[0], 0, 0, layers.edges)

    @pl.loop(0, (blocks + 1) // 2)
    def _(pair):
        for parity in range(2):
            block = 2 * pair + parity

            @pl.when(block < blocks)
            def _():
                layers.one_block(block, parity, rows // ROWS - 1)

    @pl.loop(0, rows // NODE_ROWS)
    def _(i):
        first = pl.multiple_of(i * NODE_ROWS, NODE_ROWS)
        renewed = node_layers(refs, table_ref, summed, pl.ds(first, NODE_ROWS))
        store_split(ordered, first, renewed)

    copy_rows(ordered, place_ids.at[0], pairs, rows)

    @pl.loop(0, local_rows // NODE_ROWS)
    def _(i):
        first = pl.multiple_of(i * NODE_ROWS, NODE_ROWS)
        row_ids = lax.broadcasted_iota(jnp.int32, (NODE_ROWS, leave_lanes.shape[1]), 0) + first
        leaves = jnp.max((row_ids == leave_lanes[...]).astype(F32), axis=1, keepdims=True)
        living = jnp.where(row_ids[:, :1] < live_count[0], 1.0 - leaves, 0.0)
        updated_ref[pl.ds(first, NODE_ROWS), :] = (load_split(pairs, first, NODE_ROWS) * living).astype(BF16)

    for first in range(0, rows - local_rows, NODE_ROWS):
        living = arrived_ref[pl.ds(first, NODE_ROWS), width : width + 1].astype(F32)
        updated_ref[pl.ds(local_rows + first, NODE_ROWS), :] = (
            load_split(pairs, local_rows + first, NODE_ROWS) * living
        ).astype(BF16)


def last_step(edge_ids, floor, table, projected, ghosts, place_ids, count, live_count, leave_rows, arrived, weights):
    rows, width = table.shape
    slots = edge_ids.shape[0]
    return pl.pallas_call(
        functools.partial(last_step_kernel, slots),
        out_shape=jax.ShapeDtypeStruct((rows, width), BF16),
        in_specs=[SMEM, VMEM, VMEM, VMEM, ANYWHERE, SMEM, SMEM, SMEM] + [VMEM] * 12,
        out_specs=VMEM,
        scratch_shapes=edge_scratch(rows, slots, rows + ghosts.shape[0] * ghosts.shape[1], width)
        + [
            pltpu.VMEM(ghosts.shape, BF16),
            pltpu.VMEM((2 * rows, HALF), F32),
            pltpu.SemaphoreType.DMA((ghosts.shape[0],)),
        ],
        compiler_params=pltpu.CompilerParams(vmem_limit_bytes=VMEM_BYTES),
        name="last_step",
    )(
        edge_ids,
        floor,
        table,
        projected,
        ghosts,
        place_ids,
        count,
        live_count,
        leave_rows[None, :],
        arrived,
        *weights,
    )


def pick_rows(source_rows, row_ids):
    selector = (
        row_ids[:, None] == jnp.arange(source_rows.shape[0], dtype=jnp.int32)[None, :]
    ).astype(source_rows.dtype)
    return jnp.dot(selector, source_rows, preferred_element_type=F32).astype(source_rows.dtype)


def local(
    latent,
    live_count,
    leave_rows,
    leave_target,
    halo_rows,
    neighbours,
    edge_in,
    edge_bias,
    edge_out,
    edge_shift,
    edge_gain,
    node_in,
    node_bias,
    node_out,
    node_shift,
    node_gain,
):
    axes = ("gx", "gy", "gz")
    devices = lax.axis_size(axes)
    local_rows, width = latent.shape
    table_rows, slots = neighbours.shape
    slots_total = table_rows - local_rows
    capacity = slots_total // devices
    leaving = leave_rows.shape[0]
    target_domain = leave_target[:, 0]
    entry = jnp.arange(leaving, dtype=jnp.int32)
    earlier = entry[None, :] < entry[:, None]
    same_target = target_domain[:, None] == target_domain[None, :]
    row_rank = jnp.sum(jnp.logical_and(same_target, earlier).astype(jnp.int32), axis=1)
    position = target_domain * capacity + row_rank
    moving = pick_rows(latent, leave_rows)
    moving = jnp.concatenate([moving, jnp.ones((leaving, HALF), BF16)], axis=1)
    placement = jnp.arange(slots_total, dtype=jnp.int32)[:, None] == position[None, :]
    outgoing = jnp.dot(placement.astype(BF16), moving, preferred_element_type=F32).astype(BF16)
    arrived = lax.all_to_all(
        outgoing.reshape(devices, capacity, width + HALF), axes, split_axis=0, concat_axis=0, tiled=True
    ).reshape(slots_total, width + HALF)
    weights = (
        edge_in,
        edge_bias,
        edge_out,
        edge_shift,
        edge_gain,
        node_in,
        node_bias,
        node_out,
        node_shift,
        node_gain,
    )
    blocks = (local_rows - leaving + slots_total) // ROWS
    table, projected, ghosts, edge_ids, floor, place_ids, count = first_step(
        blocks, latent, arrived, digits_of(neighbours), halo_rows, weights
    )
    return last_step(
        edge_ids, floor, table, projected, ghosts, place_ids, count, live_count, leave_rows, arrived, weights
    )


def solution(mesh):
    rows = P(("gx", "gy", "gz"))
    in_specs = (rows,) * 6 + (P(),) * 10
    return jax.shard_map(local, mesh=mesh, in_specs=in_specs, out_specs=rows, check_vma=False)
```

```python
import functools

import jax
import jax.numpy as jnp
from jax import lax
from jax.experimental import pallas as pl
from jax.experimental.pallas import tpu as pltpu
from jax.sharding import PartitionSpec as P

EPS = 1e-05
F32 = jnp.float32
BF16 = jnp.bfloat16
HALF = 128
ROWS = 32
CHUNK = 256
LAG = 2
GROUP = 8
NODE_ROWS = 256
SPARE = 8
AXES = ("gx", "gy", "gz")
MESH = pl.DeviceIdType.MESH
VMEM_BYTES = 58 * 2**20
VMEM = pl.BlockSpec(memory_space=pltpu.VMEM)
SMEM = pl.BlockSpec(memory_space=pltpu.SMEM)
ANYWHERE = pl.BlockSpec(memory_space=pl.ANY)


def even_part(count, most=1024):
    parts = -(-count // most)
    while count % (parts * HALF):
        parts += 1
    return count // parts


def layer_norm(values, feature_gain):
    average = jnp.mean(values, axis=-1, keepdims=True)
    centred = values - average
    spread = jnp.mean(centred * centred, axis=-1, keepdims=True)
    return centred * lax.rsqrt(spread + EPS) * feature_gain


def store_split(pairs, first_row, values):
    count = values.shape[0]
    pairs[pl.ds(2 * first_row, count, stride=2), :] = values[:, :HALF]
    pairs[pl.ds(2 * first_row + 1, count, stride=2), :] = values[:, HALF:]


def load_split(pairs, first_row, count):
    left = pairs[pl.ds(2 * first_row, count, stride=2), :]
    right = pairs[pl.ds(2 * first_row + 1, count, stride=2), :]
    return jnp.concatenate([left, right], axis=1)


def project(rows, weight):
    return jnp.dot(rows, weight, preferred_element_type=F32).astype(BF16)


def copy_rows(source, ids, into, count):
    @pl.loop(0, count // 64)
    def _(block):
        for g in range(64 // GROUP):
            some = ids.at[pl.ds(block * 64 + g * GROUP, GROUP)]
            for e in range(GROUP):
                place = pl.multiple_of(2 * (block * 64 + g * GROUP + e), 2)
                into[pl.ds(place, 2), :] = source[pl.ds(2 * some[e], 2), :]


def find_places(digits, halo_lanes, places, place_ref, count_ref):
    rows = digits.shape[1]
    half_rows = digits.shape[0] // 2
    slots = half_rows - SPARE
    boundary = halo_lanes.shape[1]
    n = NODE_ROWS
    lower = (
        lax.broadcasted_iota(jnp.int32, (n, n), 0) > lax.broadcasted_iota(jnp.int32, (n, n), 1)
    ).astype(BF16)
    lane = lax.broadcasted_iota(jnp.int32, (n, boundary), 1).astype(F32)

    def one_chunk(c, carry):
        used, spare = carry
        first = pl.multiple_of(c * n, n)
        here = pl.ds(first, n)
        largest = jnp.max(
            digits[pl.ds(0, slots), here].astype(F32) + digits[pl.ds(half_rows, slots), here].astype(F32),
            axis=0,
            keepdims=True,
        )
        active = jnp.transpose(jnp.broadcast_to(largest, (HALF, n))) > 0.0
        row_ids = lax.broadcasted_iota(jnp.int32, (n, boundary), 0) + first
        same = (row_ids == halo_lanes[...]).astype(F32)
        listed = jnp.sum(same, axis=1, keepdims=True) > 0.0
        position = jnp.sum(same * lane, axis=1, keepdims=True)
        others = jnp.where(listed, 0.0, jnp.where(active, 1.0, 0.0))
        idle = jnp.where(listed, 0.0, jnp.where(active, 0.0, 1.0))
        before = jnp.dot(lower, others.astype(BF16), preferred_element_type=F32) + used
        behind = jnp.dot(lower, idle.astype(BF16), preferred_element_type=F32) + spare
        place = jnp.where(others > 0.0, boundary + before, rows - 1 - behind)
        place = jnp.where(listed, position, place)
        places[here, :] = place
        place_ref[:, here] = jnp.transpose(place)[:1].astype(jnp.int32)
        return used + jnp.sum(others[:, :1]), spare + jnp.sum(idle[:, :1])

    used, _ = lax.fori_loop(0, rows // n, one_chunk, (jnp.float32(0.0), jnp.float32(0.0)), unroll=3)
    count_ref[0] = used.astype(jnp.int32) + boundary


def apply_places(senders, digits, places, edge_ids, floor_ref, order_ref):
    rows = digits.shape[1]
    half_rows = digits.shape[0] // 2
    slots = half_rows - SPARE
    n = NODE_ROWS

    @pl.loop(0, rows // n, unroll=3)
    def _(c):
        first = pl.multiple_of(c * n, n)
        lanes = lax.broadcasted_iota(jnp.int32, (n, HALF), 1).astype(F32)
        picked = jnp.zeros((2 * half_rows, n), F32)
        for part in range(rows // n):
            here = places[pl.ds(part * n, n), :]
            halves = [
                jnp.where(here == lanes + (first + half * HALF).astype(F32), 1.0, 0.0).astype(BF16)
                for half in range(n // HALF)
            ]
            chosen = jnp.concatenate(halves, axis=1)
            picked = picked + jnp.dot(digits[:, pl.ds(part * n, n)], chosen, preferred_element_type=F32)
        value = picked[:half_rows] * 128.0 + picked[half_rows:]
        here = pl.ds(first, n)
        edge_ids[:, here] = 2 * jnp.clip((value[:slots] - 1.0).astype(jnp.int32), 0, senders - 1)
        order_ref[:, here] = jnp.clip(value[slots : slots + 1].astype(jnp.int32), 0, rows - 1)
        floor = jnp.where(value > 0.5, EPS, jnp.inf).astype(F32)
        floor_ref[here, :] = jnp.transpose(jnp.concatenate([floor] * (HALF // half_rows), axis=0))


def digits_of(neighbours):
    rows, slots = neighbours.shape
    ids = jnp.concatenate(
        [neighbours.T + 1, jnp.arange(rows, dtype=jnp.int32)[None], jnp.zeros((SPARE - 1, rows), jnp.int32)]
    )
    return jnp.concatenate([ids // 128, ids % 128]).astype(BF16)


class Grid:
    def __init__(self):
        self.place = [lax.axis_index(a) for a in AXES]
        self.sizes = [lax.axis_size(a) for a in AXES]

    def inside(self, axis, step):
        return jnp.logical_and(self.place[axis] + step >= 0, self.place[axis] + step < self.sizes[axis])

    def target(self, axis, step):
        return tuple(self.place[a] + (step if a == axis else 0) for a in range(3))

    def present(self, offset):
        found = None
        for a in range(3):
            if offset[a] != 0:
                here = self.inside(a, offset[a])
                found = here if found is None else jnp.logical_and(found, here)
        return found

    def greet(self):
        barrier = pltpu.get_barrier_semaphore()
        friends = jnp.int32(0)
        for axis in range(3):
            for step in (-1, 1):
                friends = friends + self.inside(axis, step).astype(jnp.int32)

                @pl.when(self.inside(axis, step))
                def _():
                    pl.semaphore_signal(barrier, inc=1, device_id=self.target(axis, step), device_id_type=MESH)

        pl.semaphore_wait(barrier, friends)


def number(offset):
    return 9 * (offset[0] + 1) + 3 * (offset[1] + 1) + offset[2] + 1


def moved(offset, axis, step):
    return tuple(offset[a] + (step if a == axis else 0) for a in range(3))


CENTRE = (0, 0, 0)
OFFSETS = [(dx, dy, dz) for dx in (-1, 0, 1) for dy in (-1, 0, 1) for dz in (-1, 0, 1)]
ALONG = [o for o in OFFSETS if o[:2] == (0, 0) and o[2] != 0]
FACES = [o for o in OFFSETS if o[2] == 0 and abs(o[0]) + abs(o[1]) == 1]
CORNERS = [o for o in OFFSETS if o[2] == 0 and o[0] != 0 and o[1] != 0]
ENDS = [o for o in OFFSETS if o[2] != 0 and o[:2] != (0, 0)]


class Exchange:
    def __init__(self, grid, boundary, ghosts, send_sems, recv_sems):
        self.grid, self.boundary, self.ghosts = grid, boundary, ghosts
        self.send_sems, self.recv_sems = send_sems, recv_sems

    def copy(self, offset, axis, step):
        slot = number(moved(offset, axis, -step))
        return pltpu.make_async_remote_copy(
            src_ref=self.boundary if offset == CENTRE else self.ghosts.at[number(offset)],
            dst_ref=self.ghosts.at[slot],
            send_sem=self.send_sems.at[slot],
            recv_sem=self.recv_sems.at[slot],
            device_id=self.grid.target(axis, step),
            device_id_type=MESH,
        )

    def on_chip(self, step):
        return lax.rem(self.grid.place[2], 2) == (0 if step == 1 else 1)

    def last_hops(self, offset):
        dx, dy, dz = offset
        if dz == 0:
            if dx != 0 and dy != 0:
                return [(1 if dx == dy else 0, None)]
            return [(0 if dx != 0 else 1, None)]
        if (dx != 0) == (dy != 0):
            return [(2, None)]
        near = self.on_chip(dz)
        return [(2, near), (0 if dx != 0 else 1, jnp.logical_not(near))]

    def hops_from(self, offset):
        found = []
        for axis in range(3):
            if offset[axis] != 0:
                continue
            for step in (-1, 1):
                dx, dy, dz = reached = moved(offset, axis, -step)
                there = self.grid.inside(axis, step)
                if offset != CENTRE:
                    there = jnp.logical_and(there, self.grid.present(offset))
                if dz != 0 and (dx != 0) != (dy != 0):
                    near = self.on_chip(step if axis == 2 else dz)
                    there = jnp.logical_and(there, near if axis == 2 else jnp.logical_not(near))
                elif axis not in [a for a, _ in self.last_hops(reached)]:
                    continue
                found.append((axis, step, there))
        return found

    def forward(self, offset):
        for axis, step, there in self.hops_from(offset):

            @pl.when(there)
            def _():
                self.copy(offset, axis, step).start()

    def arrive(self, offset):
        for axis, condition in self.last_hops(offset):
            there = self.grid.present(offset)
            if condition is not None:
                there = jnp.logical_and(there, condition)

            @pl.when(there)
            def _():
                self.copy(moved(offset, axis, -offset[axis]), axis, -offset[axis]).wait_recv()

    def relay(self, offsets):
        for offset in offsets:
            self.arrive(offset)
            self.forward(offset)

    def finish_sends(self):
        for offset in [CENTRE] + ALONG + FACES + CORNERS:
            for axis, step, there in self.hops_from(offset):

                @pl.when(there)
                def _():
                    self.copy(offset, axis, step).wait_send()


class EdgeLayers:
    def __init__(self, rows, slots, refs, scratch):
        self.edge_ids, self.floor = refs["edge_ids"], refs["floor"]
        self.refs = refs
        self.rows, self.slots = rows, slots
        self.edges = slots * ROWS
        self.pairs, self.buffers, self.receive, self.summed, self.raw, self.square, self.weight = scratch
        self.width = self.receive.shape[1]

    def prepare(self, table_ref):
        refs = self.refs
        wide = refs["edge_out"][...].astype(F32)
        self.weight[...] = (wide - jnp.mean(wide, axis=1, keepdims=True)).astype(BF16)

        @pl.loop(0, self.rows // NODE_ROWS, unroll=3)
        def _(i):
            here = pl.ds(pl.multiple_of(i * NODE_ROWS, NODE_ROWS), NODE_ROWS)
            self.summed[here, :] = jnp.zeros((NODE_ROWS, self.width), F32)
            self.receive[here, :] = (
                jnp.dot(table_ref[here, :], refs["receive_weight"][...], preferred_element_type=F32)
                + refs["edge_bias"][...]
            )

    def gather(self, into, block, start, stop):
        first = pl.multiple_of(block * ROWS, ROWS)
        for e in range(start, stop):
            k, r = divmod(e, ROWS)
            if r % GROUP == 0:
                ids = self.edge_ids.at[k, pl.ds(first + r, GROUP)]
            into[pl.ds(2 * e, 2), :] = self.pairs[pl.ds(ids[r % GROUP], 2), :]

    def first_half(self, source, first, chunk, shift):
        per_chunk = CHUNK // ROWS
        own = self.receive[pl.ds(first, ROWS), :]
        left = source[pl.ds(2 * chunk * CHUNK, CHUNK, stride=2), :].reshape(per_chunk, ROWS, HALF)
        right = source[pl.ds(2 * chunk * CHUNK + 1, CHUNK, stride=2), :].reshape(per_chunk, ROWS, HALF)
        left = jnp.maximum(left + own[:, :HALF][None], 0.0).reshape(CHUNK, HALF).astype(BF16)
        right = jnp.maximum(right + own[:, HALF:][None], 0.0).reshape(CHUNK, HALF).astype(BF16)
        active = jnp.concatenate([left, right], axis=1)
        centred = jnp.dot(active, self.weight[...], preferred_element_type=F32) + shift
        total = jnp.sum(
            centred[:, :HALF] * centred[:, :HALF] + centred[:, HALF:] * centred[:, HALF:], axis=1, keepdims=True
        )
        here = pl.ds(chunk * CHUNK, CHUNK)
        self.raw[here, :] = centred
        self.square[here, :] = jnp.broadcast_to(total, (CHUNK, HALF))

    def second_half(self, floor, chunk, sums):
        left, right = sums
        per_chunk = CHUNK // ROWS
        for k in range(chunk * per_chunk, (chunk + 1) * per_chunk):
            here = pl.ds(k * ROWS, ROWS)
            scale = lax.rsqrt(self.square[here, :] * (1.0 / self.width) + floor[:, k : k + 1])
            left = left + self.raw[here, :HALF] * scale
            right = right + self.raw[here, HALF:] * scale
        return left, right

    def one_block(self, block, parity, last_block):
        chunks = self.edges // CHUNK
        first = pl.multiple_of(block * ROWS, ROWS)
        following = jnp.minimum(block + 1, last_block)
        edge_shift = self.refs["edge_shift"]
        shift = edge_shift[...] - jnp.mean(edge_shift[...], axis=1, keepdims=True)
        floor = self.floor[pl.ds(first, ROWS), :]
        sums = (jnp.zeros((ROWS, HALF), F32), jnp.zeros((ROWS, HALF), F32))
        for chunk in range(chunks + LAG):
            if chunk < chunks:
                self.gather(self.buffers[1 - parity], following, chunk * CHUNK, (chunk + 1) * CHUNK)
                self.first_half(self.buffers[parity], first, chunk, shift)
            if chunk >= LAG:
                sums = self.second_half(floor, chunk - LAG, sums)
        self.summed[pl.ds(first, ROWS), :HALF] = sums[0]
        self.summed[pl.ds(first, ROWS), HALF:] = sums[1]


def node_layers(refs, table_ref, summed, here):
    own = table_ref[here, :]
    message = (summed[here, :] * refs["edge_gain"][...]).astype(BF16)
    hidden = (
        jnp.dot(own, refs["node_self"][...], preferred_element_type=F32)
        + jnp.dot(message, refs["node_message"][...], preferred_element_type=F32)
        + refs["node_bias"][...]
    )
    hidden = jnp.maximum(hidden, 0.0).astype(BF16)
    node_raw = jnp.dot(hidden, refs["node_out"][...], preferred_element_type=F32) + refs["node_shift"][...]
    return own.astype(F32) + layer_norm(node_raw, refs["node_gain"][...])


def step_refs(t, edge_ids, floor, weights):
    edge_in, edge_bias, edge_out, edge_shift, edge_gain, node_in, node_bias, node_out, node_shift, node_gain = weights
    row = pl.ds(t, 1)
    return {
        "edge_ids": edge_ids,
        "floor": floor,
        "receive_weight": edge_in.at[t, 0],
        "edge_bias": edge_bias.at[row],
        "edge_out": edge_out.at[t],
        "edge_shift": edge_shift.at[row],
        "edge_gain": edge_gain.at[row],
        "node_self": node_in.at[t, 0],
        "node_message": node_in.at[t, 1],
        "node_bias": node_bias.at[row],
        "node_out": node_out.at[t],
        "node_shift": node_shift.at[row],
        "node_gain": node_gain.at[row],
    }


def edge_scratch(rows, slots, senders, width):
    edges = slots * ROWS
    return [
        pltpu.VMEM((2 * senders, HALF), F32),
        pltpu.VMEM((2 * edges, HALF), F32),
        pltpu.VMEM((2 * edges, HALF), F32),
        pltpu.VMEM((rows, width), F32),
        pltpu.VMEM((rows, width), F32),
        pltpu.VMEM((edges, width), F32),
        pltpu.VMEM((edges, HALF), F32),
        pltpu.VMEM((width, width), BF16),
    ]


def unpack_scratch(scratch):
    pairs, even, odd, receive, summed, raw, square, weight = scratch
    return pairs, (even, odd), receive, summed, raw, square, weight


def spread_block(pairs, first_row, block_ref):
    @pl.loop(0, block_ref.shape[0] // 128)
    def _(piece):
        start = pl.multiple_of(piece * 128, 128)
        store_split(pairs, first_row + start, block_ref[pl.ds(start, 128), :].astype(F32))


def first_step_kernel(slots, blocks, marks, *args):
    latent_ref, arrived_ref, digits, halo_lanes, halo_ids = args[:5]
    weights = args[5:15]
    renewed_ref, next_projected, next_ghosts, edge_lanes, floor_ref, place_ref, count_ref = args[15:22]
    scratch = unpack_scratch(args[22:30])
    (
        ghosts,
        boundary_ref,
        next_boundary,
        original,
        ordered,
        places,
        table_ref,
        order_lanes,
        edge_ids,
        order_ids,
        send_a,
        recv_a,
        send_b,
        recv_b,
        id_sems,
    ) = args[30:]
    pairs, summed = scratch[0], scratch[3]
    local_rows, width = latent_ref.shape
    arrivals = arrived_ref.shape[0]
    rows = local_rows + arrivals
    boundary_rows = boundary_ref.shape[0]
    refs = step_refs(0, edge_ids, floor_ref, weights)
    send_weight, next_weight = weights[0].at[0, 1], weights[0].at[1, 1]
    grid = Grid()
    now = Exchange(grid, boundary_ref, ghosts, send_a, recv_a)
    later = Exchange(grid, next_boundary, next_ghosts, send_b, recv_b)
    layers = EdgeLayers(rows, slots, refs, scratch)
    grid.greet()

    def sources(take):
        @pl.loop(0, local_rows // NODE_ROWS)
        def _(i):
            first = pl.multiple_of(i * NODE_ROWS, NODE_ROWS)
            take(first, latent_ref[pl.ds(first, NODE_ROWS), :])

        for first in range(0, arrivals, NODE_ROWS):
            take(local_rows + first, arrived_ref[pl.ds(first, NODE_ROWS), :width])

    sources(lambda first, values: store_split(original, first, values.astype(F32)))
    copy_rows(original, halo_ids, ordered, boundary_rows)
    for first in range(0, boundary_rows, NODE_ROWS):
        values = load_split(ordered, first, NODE_ROWS).astype(BF16)
        boundary_ref[pl.ds(first, NODE_ROWS), :] = project(values, send_weight[...])
    now.forward(CENTRE)
    sources(lambda first, values: store_split(pairs, first, project(values, send_weight[...]).astype(F32)))
    now.relay(ALONG)
    find_places(digits, halo_lanes, places, place_ref, count_ref)

    def spread(offset):
        spread_block(pairs, rows + number(offset) * boundary_rows, ghosts.at[number(offset)])

    def spread_all(offsets):
        for offset in offsets:

            @pl.when(grid.present(offset))
            def _():
                spread(offset)

    now.relay(FACES)
    apply_places(pairs.shape[0] // 2, digits, places, edge_lanes, floor_ref, order_lanes)
    fetch_edges = pltpu.make_async_copy(edge_lanes, edge_ids, id_sems.at[0])
    fetch_order = pltpu.make_async_copy(order_lanes, order_ids, id_sems.at[1])
    fetch_edges.start()
    fetch_order.start()
    now.relay(CORNERS)
    spread_all(ALONG)
    spread_all(FACES)
    fetch_edges.wait()
    fetch_order.wait()
    copy_rows(original, order_ids.at[0], ordered, rows)

    @pl.loop(0, rows // NODE_ROWS)
    def _(i):
        first = pl.multiple_of(i * NODE_ROWS, NODE_ROWS)
        table_ref[pl.ds(first, NODE_ROWS), :] = load_split(ordered, first, NODE_ROWS).astype(BF16)

    layers.prepare(table_ref)
    spread_all(CORNERS)
    for offset in ENDS:
        now.arrive(offset)
        spread_all([offset])

    layers.gather(layers.buffers[0], 0, 0, layers.edges)

    def renew(first, count):
        here = pl.ds(first, count)
        renewed = node_layers(refs, table_ref, summed, here).astype(BF16)
        renewed_ref[here, :] = renewed
        projected = project(renewed, next_weight[...])
        next_projected[here, :] = projected
        return projected

    @pl.loop(0, blocks // 2)
    def _(pair):
        @pl.when(pair == marks[0])
        def _():
            next_boundary[...] = renew(0, boundary_rows)
            later.forward(CENTRE)

        for mark, offsets in zip(marks[1:], (ALONG, FACES, CORNERS)):

            @pl.when(pair == mark)
            def _():
                later.relay(offsets)

        for parity in range(2):
            block = 2 * pair + parity

            @pl.when(block < blocks + grid.place[0])
            def _():
                layers.one_block(block, parity, blocks - 1)

    part = even_part(rows - boundary_rows)

    @pl.loop(0, (rows - boundary_rows) // part)
    def _(i):
        renew(pl.multiple_of(boundary_rows + i * part, HALF), part)

    for offset in ENDS:
        later.arrive(offset)

    now.finish_sends()
    later.finish_sends()


def first_step(blocks, latent, arrived, digits, halo_rows, weights):
    local_rows, width = latent.shape
    rows = local_rows + arrived.shape[0]
    slots = digits.shape[0] // 2 - SPARE
    count = halo_rows.shape[0]
    first_pair = count // ROWS // 2
    rest = blocks // 2 - first_pair
    marks = (first_pair, first_pair + rest * 4 // 26, first_pair + rest * 6 // 26, first_pair + rest * 10 // 26)
    return pl.pallas_call(
        functools.partial(first_step_kernel, slots, blocks, marks),
        out_shape=(
            jax.ShapeDtypeStruct((rows, width), BF16),
            jax.ShapeDtypeStruct((rows, width), BF16),
            jax.ShapeDtypeStruct((27, count, width), BF16),
            jax.ShapeDtypeStruct((slots, rows), jnp.int32),
            jax.ShapeDtypeStruct((rows, HALF), F32),
            jax.ShapeDtypeStruct((1, rows), jnp.int32),
            jax.ShapeDtypeStruct((1,), jnp.int32),
        ),
        in_specs=[VMEM] * 4 + [SMEM] + [VMEM] * 10,
        out_specs=(VMEM, VMEM, ANYWHERE, VMEM, VMEM, VMEM, SMEM),
        scratch_shapes=edge_scratch(rows, slots, rows + 27 * count, width)
        + [
            pltpu.VMEM((27, count, width), BF16),
            pltpu.VMEM((count, width), BF16),
            pltpu.VMEM((count, width), BF16),
            pltpu.VMEM((2 * rows, HALF), F32),
            pltpu.VMEM((2 * rows, HALF), F32),
            pltpu.VMEM((rows, HALF), F32),
            pltpu.VMEM((rows, width), BF16),
            pltpu.VMEM((1, rows), jnp.int32),
            pltpu.SMEM((slots, rows), jnp.int32),
            pltpu.SMEM((1, rows), jnp.int32),
        ]
        + [pltpu.SemaphoreType.DMA((27,))] * 4
        + [pltpu.SemaphoreType.DMA((2,))],
        compiler_params=pltpu.CompilerParams(
            collective_id=0, has_side_effects=True, vmem_limit_bytes=VMEM_BYTES
        ),
        name="first_step",
    )(latent, arrived, digits, halo_rows[None, :], halo_rows, *weights)


def last_step_kernel(slots, *args):
    edge_ids, floor_ref, table_ref, projected_ref, ghosts = args[:5]
    place_ids, count_ref, live_count, leave_lanes, arrived_ref = args[5:10]
    weights = args[10:20]
    updated_ref = args[20]
    scratch = unpack_scratch(args[21:29])
    staged, ordered, sems = args[29:]
    refs = step_refs(1, edge_ids, floor_ref, weights)
    pairs, summed = scratch[0], scratch[3]
    rows, width = table_ref.shape
    local_rows = rows - arrived_ref.shape[0]
    ghost_blocks, ghost_rows = ghosts.shape[0], ghosts.shape[1]
    centre = ghost_blocks // 2
    layers = EdgeLayers(rows, slots, refs, scratch)

    def fetch(block):
        return pltpu.make_async_copy(ghosts.at[block], staged.at[block], sems.at[block])

    for block in range(ghost_blocks):
        if block != centre:
            fetch(block).start()
    layers.prepare(table_ref)

    @pl.loop(0, rows // NODE_ROWS)
    def _(i):
        first = pl.multiple_of(i * NODE_ROWS, NODE_ROWS)
        store_split(ordered, first, projected_ref[pl.ds(first, NODE_ROWS), :].astype(F32))

    copy_rows(ordered, place_ids.at[0], pairs, rows)

    @pl.loop(0, ghost_blocks)
    def _(block):
        @pl.when(block != centre)
        def _():
            fetch(block).wait()
            spread_block(pairs, pl.multiple_of(rows + block * ghost_rows, ghost_rows), staged.at[block])

    blocks = (count_ref[0] + ROWS - 1) // ROWS
    layers.gather(layers.buffers[0], 0, 0, layers.edges)

    @pl.loop(0, (blocks + 1) // 2)
    def _(pair):
        for parity in range(2):
            block = 2 * pair + parity

            @pl.when(block < blocks)
            def _():
                layers.one_block(block, parity, rows // ROWS - 1)

    part = even_part(rows)

    @pl.loop(0, rows // part)
    def _(i):
        first = pl.multiple_of(i * part, HALF)
        renewed = node_layers(refs, table_ref, summed, pl.ds(first, part))
        store_split(ordered, first, renewed)

    copy_rows(ordered, place_ids.at[0], pairs, rows)

    @pl.loop(0, local_rows // NODE_ROWS)
    def _(i):
        first = pl.multiple_of(i * NODE_ROWS, NODE_ROWS)
        row_ids = lax.broadcasted_iota(jnp.int32, (NODE_ROWS, leave_lanes.shape[1]), 0) + first
        leaves = jnp.max((row_ids == leave_lanes[...]).astype(F32), axis=1, keepdims=True)
        living = jnp.where(row_ids[:, :1] < live_count[0], 1.0 - leaves, 0.0)
        updated_ref[pl.ds(first, NODE_ROWS), :] = (load_split(pairs, first, NODE_ROWS) * living).astype(BF16)

    for first in range(0, rows - local_rows, NODE_ROWS):
        living = arrived_ref[pl.ds(first, NODE_ROWS), width : width + 1].astype(F32)
        updated_ref[pl.ds(local_rows + first, NODE_ROWS), :] = (
            load_split(pairs, local_rows + first, NODE_ROWS) * living
        ).astype(BF16)


def last_step(edge_ids, floor, table, projected, ghosts, place_ids, count, live_count, leave_rows, arrived, weights):
    rows, width = table.shape
    slots = edge_ids.shape[0]
    return pl.pallas_call(
        functools.partial(last_step_kernel, slots),
        out_shape=jax.ShapeDtypeStruct((rows, width), BF16),
        in_specs=[SMEM, VMEM, VMEM, VMEM, ANYWHERE, SMEM, SMEM, SMEM] + [VMEM] * 12,
        out_specs=VMEM,
        scratch_shapes=edge_scratch(rows, slots, rows + ghosts.shape[0] * ghosts.shape[1], width)
        + [
            pltpu.VMEM(ghosts.shape, BF16),
            pltpu.VMEM((2 * rows, HALF), F32),
            pltpu.SemaphoreType.DMA((ghosts.shape[0],)),
        ],
        compiler_params=pltpu.CompilerParams(vmem_limit_bytes=VMEM_BYTES),
        name="last_step",
    )(
        edge_ids,
        floor,
        table,
        projected,
        ghosts,
        place_ids,
        count,
        live_count,
        leave_rows[None, :],
        arrived,
        *weights,
    )


def pick_rows(source_rows, row_ids):
    selector = (
        row_ids[:, None] == jnp.arange(source_rows.shape[0], dtype=jnp.int32)[None, :]
    ).astype(source_rows.dtype)
    return jnp.dot(selector, source_rows, preferred_element_type=F32).astype(source_rows.dtype)


def local(
    latent,
    live_count,
    leave_rows,
    leave_target,
    halo_rows,
    neighbours,
    edge_in,
    edge_bias,
    edge_out,
    edge_shift,
    edge_gain,
    node_in,
    node_bias,
    node_out,
    node_shift,
    node_gain,
):
    axes = ("gx", "gy", "gz")
    devices = lax.axis_size(axes)
    local_rows, width = latent.shape
    table_rows, slots = neighbours.shape
    slots_total = table_rows - local_rows
    capacity = slots_total // devices
    leaving = leave_rows.shape[0]
    target_domain = leave_target[:, 0]
    entry = jnp.arange(leaving, dtype=jnp.int32)
    earlier = entry[None, :] < entry[:, None]
    same_target = target_domain[:, None] == target_domain[None, :]
    row_rank = jnp.sum(jnp.logical_and(same_target, earlier).astype(jnp.int32), axis=1)
    position = target_domain * capacity + row_rank
    moving = pick_rows(latent, leave_rows)
    moving = jnp.concatenate([moving, jnp.ones((leaving, HALF), BF16)], axis=1)
    placement = jnp.arange(slots_total, dtype=jnp.int32)[:, None] == position[None, :]
    outgoing = jnp.dot(placement.astype(BF16), moving, preferred_element_type=F32).astype(BF16)
    arrived = lax.all_to_all(
        outgoing.reshape(devices, capacity, width + HALF), axes, split_axis=0, concat_axis=0, tiled=True
    ).reshape(slots_total, width + HALF)
    weights = (
        edge_in,
        edge_bias,
        edge_out,
        edge_shift,
        edge_gain,
        node_in,
        node_bias,
        node_out,
        node_shift,
        node_gain,
    )
    blocks = (local_rows - leaving + slots_total) // ROWS
    table, projected, ghosts, edge_ids, floor, place_ids, count = first_step(
        blocks, latent, arrived, digits_of(neighbours), halo_rows, weights
    )
    return last_step(
        edge_ids, floor, table, projected, ghosts, place_ids, count, live_count, leave_rows, arrived, weights
    )


def solution(mesh):
    rows = P(("gx", "gy", "gz"))
    in_specs = (rows,) * 6 + (P(),) * 10
    return jax.shard_map(local, mesh=mesh, in_specs=in_specs, out_specs=rows, check_vma=False)
```

```python
import functools

import jax
import jax.numpy as jnp
from jax import lax
from jax.experimental import pallas as pl
from jax.experimental.pallas import tpu as pltpu
from jax.sharding import PartitionSpec as P

EPS = 1e-05
F32 = jnp.float32
BF16 = jnp.bfloat16
HALF = 128
ROWS = 32
CHUNK = 256
LAG = 2
GROUP = 8
NODE_ROWS = 256
SPARE = 8
AXES = ("gx", "gy", "gz")
MESH = pl.DeviceIdType.MESH
VMEM_BYTES = 58 * 2**20
VMEM = pl.BlockSpec(memory_space=pltpu.VMEM)
SMEM = pl.BlockSpec(memory_space=pltpu.SMEM)
ANYWHERE = pl.BlockSpec(memory_space=pl.ANY)


def even_part(count, most=1024):
    parts = -(-count // most)
    while count % (parts * HALF):
        parts += 1
    return count // parts


def layer_norm(values, feature_gain):
    average = jnp.mean(values, axis=-1, keepdims=True)
    centred = values - average
    spread = jnp.mean(centred * centred, axis=-1, keepdims=True)
    return centred * lax.rsqrt(spread + EPS) * feature_gain


def store_split(pairs, first_row, values):
    count = values.shape[0]
    pairs[pl.ds(2 * first_row, count, stride=2), :] = values[:, :HALF]
    pairs[pl.ds(2 * first_row + 1, count, stride=2), :] = values[:, HALF:]


def load_split(pairs, first_row, count):
    left = pairs[pl.ds(2 * first_row, count, stride=2), :]
    right = pairs[pl.ds(2 * first_row + 1, count, stride=2), :]
    return jnp.concatenate([left, right], axis=1)


def project(rows, weight):
    return jnp.dot(rows, weight, preferred_element_type=F32).astype(BF16)


def copy_rows(source, ids, into, count):
    @pl.loop(0, count // 64)
    def _(block):
        for g in range(64 // GROUP):
            some = ids.at[pl.ds(block * 64 + g * GROUP, GROUP)]
            for e in range(GROUP):
                place = pl.multiple_of(2 * (block * 64 + g * GROUP + e), 2)
                into[pl.ds(place, 2), :] = source[pl.ds(2 * some[e], 2), :]


def find_places(digits, halo_lanes, places, place_ref, count_ref):
    rows = digits.shape[1]
    half_rows = digits.shape[0] // 2
    slots = half_rows - SPARE
    boundary = halo_lanes.shape[1]
    n = NODE_ROWS
    lower = (
        lax.broadcasted_iota(jnp.int32, (n, n), 0) > lax.broadcasted_iota(jnp.int32, (n, n), 1)
    ).astype(BF16)
    lane = lax.broadcasted_iota(jnp.int32, (n, boundary), 1).astype(F32)

    def one_chunk(c, carry):
        used, spare = carry
        first = pl.multiple_of(c * n, n)
        here = pl.ds(first, n)
        largest = jnp.max(
            digits[pl.ds(0, slots), here].astype(F32) + digits[pl.ds(half_rows, slots), here].astype(F32),
            axis=0,
            keepdims=True,
        )
        active = jnp.transpose(jnp.broadcast_to(largest, (HALF, n))) > 0.0
        row_ids = lax.broadcasted_iota(jnp.int32, (n, boundary), 0) + first
        same = (row_ids == halo_lanes[...]).astype(F32)
        listed = jnp.sum(same, axis=1, keepdims=True) > 0.0
        position = jnp.sum(same * lane, axis=1, keepdims=True)
        others = jnp.where(listed, 0.0, jnp.where(active, 1.0, 0.0))
        idle = jnp.where(listed, 0.0, jnp.where(active, 0.0, 1.0))
        before = jnp.dot(lower, others.astype(BF16), preferred_element_type=F32) + used
        behind = jnp.dot(lower, idle.astype(BF16), preferred_element_type=F32) + spare
        place = jnp.where(others > 0.0, boundary + before, rows - 1 - behind)
        place = jnp.where(listed, position, place)
        places[here, :] = place
        place_ref[:, here] = jnp.transpose(place)[:1].astype(jnp.int32)
        return used + jnp.sum(others[:, :1]), spare + jnp.sum(idle[:, :1])

    used, _ = lax.fori_loop(0, rows // n, one_chunk, (jnp.float32(0.0), jnp.float32(0.0)), unroll=3)
    count_ref[0] = used.astype(jnp.int32) + boundary


def apply_places(senders, digits, places, edge_ids, floor_ref, order_ref):
    rows = digits.shape[1]
    half_rows = digits.shape[0] // 2
    slots = half_rows - SPARE
    n = NODE_ROWS

    @pl.loop(0, rows // n, unroll=3)
    def _(c):
        first = pl.multiple_of(c * n, n)
        lanes = lax.broadcasted_iota(jnp.int32, (n, HALF), 1).astype(F32)
        picked = jnp.zeros((2 * half_rows, n), F32)
        for part in range(rows // n):
            here = places[pl.ds(part * n, n), :]
            halves = [
                jnp.where(here == lanes + (first + half * HALF).astype(F32), 1.0, 0.0).astype(BF16)
                for half in range(n // HALF)
            ]
            chosen = jnp.concatenate(halves, axis=1)
            picked = picked + jnp.dot(digits[:, pl.ds(part * n, n)], chosen, preferred_element_type=F32)
        value = picked[:half_rows] * 128.0 + picked[half_rows:]
        here = pl.ds(first, n)
        edge_ids[:, here] = 2 * jnp.clip((value[:slots] - 1.0).astype(jnp.int32), 0, senders - 1)
        order_ref[:, here] = jnp.clip(value[slots : slots + 1].astype(jnp.int32), 0, rows - 1)
        floor = jnp.where(value > 0.5, EPS, jnp.inf).astype(F32)
        floor_ref[here, :] = jnp.transpose(jnp.concatenate([floor] * (HALF // half_rows), axis=0))


def digits_of(neighbours):
    rows, slots = neighbours.shape
    ids = jnp.concatenate(
        [neighbours.T + 1, jnp.arange(rows, dtype=jnp.int32)[None], jnp.zeros((SPARE - 1, rows), jnp.int32)]
    )
    return jnp.concatenate([ids // 128, ids % 128]).astype(BF16)


class Grid:
    def __init__(self):
        self.place = [lax.axis_index(a) for a in AXES]
        self.sizes = [lax.axis_size(a) for a in AXES]

    def inside(self, axis, step):
        return jnp.logical_and(self.place[axis] + step >= 0, self.place[axis] + step < self.sizes[axis])

    def target(self, axis, step):
        return tuple(self.place[a] + (step if a == axis else 0) for a in range(3))

    def present(self, offset):
        found = None
        for a in range(3):
            if offset[a] != 0:
                here = self.inside(a, offset[a])
                found = here if found is None else jnp.logical_and(found, here)
        return found

    def greet(self):
        barrier = pltpu.get_barrier_semaphore()
        friends = jnp.int32(0)
        for axis in range(3):
            for step in (-1, 1):
                friends = friends + self.inside(axis, step).astype(jnp.int32)

                @pl.when(self.inside(axis, step))
                def _():
                    pl.semaphore_signal(barrier, inc=1, device_id=self.target(axis, step), device_id_type=MESH)

        pl.semaphore_wait(barrier, friends)


def number(offset):
    return 9 * (offset[0] + 1) + 3 * (offset[1] + 1) + offset[2] + 1


def moved(offset, axis, step):
    return tuple(offset[a] + (step if a == axis else 0) for a in range(3))


CENTRE = (0, 0, 0)
OFFSETS = [(dx, dy, dz) for dx in (-1, 0, 1) for dy in (-1, 0, 1) for dz in (-1, 0, 1)]
ALONG = [o for o in OFFSETS if o[:2] == (0, 0) and o[2] != 0]
FACES = [o for o in OFFSETS if o[2] == 0 and abs(o[0]) + abs(o[1]) == 1]
CORNERS = [o for o in OFFSETS if o[2] == 0 and o[0] != 0 and o[1] != 0]
ENDS = [o for n in (1, 2) for o in OFFSETS if o[2] != 0 and abs(o[0]) + abs(o[1]) == n]


class Exchange:
    def __init__(self, grid, boundary, ghosts, send_sems, recv_sems):
        self.grid, self.boundary, self.ghosts = grid, boundary, ghosts
        self.send_sems, self.recv_sems = send_sems, recv_sems

    def copy(self, offset, axis, step):
        slot = number(moved(offset, axis, -step))
        return pltpu.make_async_remote_copy(
            src_ref=self.boundary if offset == CENTRE else self.ghosts.at[number(offset)],
            dst_ref=self.ghosts.at[slot],
            send_sem=self.send_sems.at[slot],
            recv_sem=self.recv_sems.at[slot],
            device_id=self.grid.target(axis, step),
            device_id_type=MESH,
        )

    def on_chip(self, step):
        return lax.rem(self.grid.place[2], 2) == (0 if step == 1 else 1)

    def last_hops(self, offset):
        dx, dy, dz = offset
        if dz == 0:
            if dx != 0 and dy != 0:
                return [(1 if dx == dy else 0, None)]
            return [(0 if dx != 0 else 1, None)]
        if (dx != 0) == (dy != 0):
            return [(2, None)]
        near = self.on_chip(dz)
        return [(2, near), (0 if dx != 0 else 1, jnp.logical_not(near))]

    def hops_from(self, offset):
        found = []
        for axis in range(3):
            if offset[axis] != 0:
                continue
            for step in (-1, 1):
                dx, dy, dz = reached = moved(offset, axis, -step)
                there = self.grid.inside(axis, step)
                if offset != CENTRE:
                    there = jnp.logical_and(there, self.grid.present(offset))
                if dz != 0 and (dx != 0) != (dy != 0):
                    near = self.on_chip(step if axis == 2 else dz)
                    there = jnp.logical_and(there, near if axis == 2 else jnp.logical_not(near))
                elif axis not in [a for a, _ in self.last_hops(reached)]:
                    continue
                found.append((axis, step, there))
        return found

    def forward(self, offset):
        for axis, step, there in self.hops_from(offset):

            @pl.when(there)
            def _():
                self.copy(offset, axis, step).start()

    def arrive(self, offset):
        for axis, condition in self.last_hops(offset):
            there = self.grid.present(offset)
            if condition is not None:
                there = jnp.logical_and(there, condition)

            @pl.when(there)
            def _():
                self.copy(moved(offset, axis, -offset[axis]), axis, -offset[axis]).wait_recv()

    def relay(self, offsets):
        for offset in offsets:
            self.arrive(offset)
            self.forward(offset)

    def finish_sends(self):
        for offset in [CENTRE] + ALONG + FACES + CORNERS:
            for axis, step, there in self.hops_from(offset):

                @pl.when(there)
                def _():
                    self.copy(offset, axis, step).wait_send()


class EdgeLayers:
    def __init__(self, rows, slots, refs, scratch):
        self.edge_ids, self.floor = refs["edge_ids"], refs["floor"]
        self.refs = refs
        self.rows, self.slots = rows, slots
        self.edges = slots * ROWS
        self.pairs, self.buffers, self.receive, self.summed, self.raw, self.square, self.weight = scratch
        self.width = self.receive.shape[1]

    def prepare(self, table_ref):
        refs = self.refs
        wide = refs["edge_out"][...].astype(F32)
        self.weight[...] = (wide - jnp.mean(wide, axis=1, keepdims=True)).astype(BF16)

        @pl.loop(0, self.rows // NODE_ROWS, unroll=3)
        def _(i):
            here = pl.ds(pl.multiple_of(i * NODE_ROWS, NODE_ROWS), NODE_ROWS)
            self.summed[here, :] = jnp.zeros((NODE_ROWS, self.width), F32)
            self.receive[here, :] = (
                jnp.dot(table_ref[here, :], refs["receive_weight"][...], preferred_element_type=F32)
                + refs["edge_bias"][...]
            )

    def gather(self, into, block, start, stop):
        first = pl.multiple_of(block * ROWS, ROWS)
        for e in range(start, stop):
            k, r = divmod(e, ROWS)
            if r % GROUP == 0:
                ids = self.edge_ids.at[k, pl.ds(first + r, GROUP)]
            into[pl.ds(2 * e, 2), :] = self.pairs[pl.ds(ids[r % GROUP], 2), :]

    def first_half(self, source, first, chunk, shift):
        per_chunk = CHUNK // ROWS
        own = self.receive[pl.ds(first, ROWS), :]
        left = source[pl.ds(2 * chunk * CHUNK, CHUNK, stride=2), :].reshape(per_chunk, ROWS, HALF)
        right = source[pl.ds(2 * chunk * CHUNK + 1, CHUNK, stride=2), :].reshape(per_chunk, ROWS, HALF)
        left = jnp.maximum(left + own[:, :HALF][None], 0.0).reshape(CHUNK, HALF).astype(BF16)
        right = jnp.maximum(right + own[:, HALF:][None], 0.0).reshape(CHUNK, HALF).astype(BF16)
        active = jnp.concatenate([left, right], axis=1)
        centred = jnp.dot(active, self.weight[...], preferred_element_type=F32) + shift
        total = jnp.sum(
            centred[:, :HALF] * centred[:, :HALF] + centred[:, HALF:] * centred[:, HALF:], axis=1, keepdims=True
        )
        here = pl.ds(chunk * CHUNK, CHUNK)
        self.raw[here, :] = centred
        self.square[here, :] = jnp.broadcast_to(total, (CHUNK, HALF))

    def second_half(self, floor, chunk, sums):
        left, right = sums
        per_chunk = CHUNK // ROWS
        for k in range(chunk * per_chunk, (chunk + 1) * per_chunk):
            here = pl.ds(k * ROWS, ROWS)
            scale = lax.rsqrt(self.square[here, :] * (1.0 / self.width) + floor[:, k : k + 1])
            left = left + self.raw[here, :HALF] * scale
            right = right + self.raw[here, HALF:] * scale
        return left, right

    def one_block(self, block, parity, last_block):
        chunks = self.edges // CHUNK
        first = pl.multiple_of(block * ROWS, ROWS)
        following = jnp.minimum(block + 1, last_block)
        edge_shift = self.refs["edge_shift"]
        shift = edge_shift[...] - jnp.mean(edge_shift[...], axis=1, keepdims=True)
        floor = self.floor[pl.ds(first, ROWS), :]
        sums = (jnp.zeros((ROWS, HALF), F32), jnp.zeros((ROWS, HALF), F32))
        for chunk in range(chunks + LAG):
            if chunk < chunks:
                self.gather(self.buffers[1 - parity], following, chunk * CHUNK, (chunk + 1) * CHUNK)
                self.first_half(self.buffers[parity], first, chunk, shift)
            if chunk >= LAG:
                sums = self.second_half(floor, chunk - LAG, sums)
        self.summed[pl.ds(first, ROWS), :HALF] = sums[0]
        self.summed[pl.ds(first, ROWS), HALF:] = sums[1]


def node_layers(refs, table_ref, summed, here):
    own = table_ref[here, :]
    message = (summed[here, :] * refs["edge_gain"][...]).astype(BF16)
    hidden = (
        jnp.dot(own, refs["node_self"][...], preferred_element_type=F32)
        + jnp.dot(message, refs["node_message"][...], preferred_element_type=F32)
        + refs["node_bias"][...]
    )
    hidden = jnp.maximum(hidden, 0.0).astype(BF16)
    node_raw = jnp.dot(hidden, refs["node_out"][...], preferred_element_type=F32) + refs["node_shift"][...]
    return own.astype(F32) + layer_norm(node_raw, refs["node_gain"][...])


def step_refs(t, edge_ids, floor, weights):
    edge_in, edge_bias, edge_out, edge_shift, edge_gain, node_in, node_bias, node_out, node_shift, node_gain = weights
    row = pl.ds(t, 1)
    return {
        "edge_ids": edge_ids,
        "floor": floor,
        "receive_weight": edge_in.at[t, 0],
        "edge_bias": edge_bias.at[row],
        "edge_out": edge_out.at[t],
        "edge_shift": edge_shift.at[row],
        "edge_gain": edge_gain.at[row],
        "node_self": node_in.at[t, 0],
        "node_message": node_in.at[t, 1],
        "node_bias": node_bias.at[row],
        "node_out": node_out.at[t],
        "node_shift": node_shift.at[row],
        "node_gain": node_gain.at[row],
    }


def edge_scratch(rows, slots, senders, width):
    edges = slots * ROWS
    return [
        pltpu.VMEM((2 * senders, HALF), F32),
        pltpu.VMEM((2 * edges, HALF), F32),
        pltpu.VMEM((2 * edges, HALF), F32),
        pltpu.VMEM((rows, width), F32),
        pltpu.VMEM((rows, width), F32),
        pltpu.VMEM((edges, width), F32),
        pltpu.VMEM((edges, HALF), F32),
        pltpu.VMEM((width, width), BF16),
    ]


def unpack_scratch(scratch):
    pairs, even, odd, receive, summed, raw, square, weight = scratch
    return pairs, (even, odd), receive, summed, raw, square, weight


def spread_block(pairs, first_row, block_ref):
    @pl.loop(0, block_ref.shape[0] // 128)
    def _(piece):
        start = pl.multiple_of(piece * 128, 128)
        store_split(pairs, first_row + start, block_ref[pl.ds(start, 128), :].astype(F32))


def first_step_kernel(slots, blocks, marks, *args):
    latent_ref, arrived_ref, digits, halo_lanes, halo_ids = args[:5]
    weights = args[5:15]
    renewed_ref, next_projected, next_ghosts, edge_lanes, floor_ref, place_ref, count_ref = args[15:22]
    scratch = unpack_scratch(args[22:30])
    (
        ghosts,
        boundary_ref,
        next_boundary,
        original,
        ordered,
        places,
        table_ref,
        order_lanes,
        edge_ids,
        order_ids,
        send_a,
        recv_a,
        send_b,
        recv_b,
        id_sems,
    ) = args[30:]
    pairs, summed = scratch[0], scratch[3]
    local_rows, width = latent_ref.shape
    arrivals = arrived_ref.shape[0]
    rows = local_rows + arrivals
    boundary_rows = boundary_ref.shape[0]
    refs = step_refs(0, edge_ids, floor_ref, weights)
    send_weight, next_weight = weights[0].at[0, 1], weights[0].at[1, 1]
    grid = Grid()
    now = Exchange(grid, boundary_ref, ghosts, send_a, recv_a)
    later = Exchange(grid, next_boundary, next_ghosts, send_b, recv_b)
    layers = EdgeLayers(rows, slots, refs, scratch)
    grid.greet()

    def sources(take):
        @pl.loop(0, local_rows // NODE_ROWS)
        def _(i):
            first = pl.multiple_of(i * NODE_ROWS, NODE_ROWS)
            take(first, latent_ref[pl.ds(first, NODE_ROWS), :])

        for first in range(0, arrivals, NODE_ROWS):
            take(local_rows + first, arrived_ref[pl.ds(first, NODE_ROWS), :width])

    sources(lambda first, values: store_split(original, first, values.astype(F32)))
    copy_rows(original, halo_ids, ordered, boundary_rows)
    for first in range(0, boundary_rows, NODE_ROWS):
        values = load_split(ordered, first, NODE_ROWS).astype(BF16)
        boundary_ref[pl.ds(first, NODE_ROWS), :] = project(values, send_weight[...])
    now.forward(CENTRE)
    sources(lambda first, values: store_split(pairs, first, project(values, send_weight[...]).astype(F32)))
    find_places(digits, halo_lanes, places, place_ref, count_ref)

    def spread(offset):
        spread_block(pairs, rows + number(offset) * boundary_rows, ghosts.at[number(offset)])

    def spread_all(offsets):
        for offset in offsets:

            @pl.when(grid.present(offset))
            def _():
                spread(offset)

    now.relay(FACES)
    now.relay(ALONG)
    apply_places(pairs.shape[0] // 2, digits, places, edge_lanes, floor_ref, order_lanes)
    fetch_edges = pltpu.make_async_copy(edge_lanes, edge_ids, id_sems.at[0])
    fetch_order = pltpu.make_async_copy(order_lanes, order_ids, id_sems.at[1])
    fetch_edges.start()
    fetch_order.start()
    now.relay(CORNERS)
    spread_all(ALONG)
    spread_all(FACES)
    fetch_edges.wait()
    fetch_order.wait()
    copy_rows(original, order_ids.at[0], ordered, rows)

    @pl.loop(0, rows // NODE_ROWS)
    def _(i):
        first = pl.multiple_of(i * NODE_ROWS, NODE_ROWS)
        table_ref[pl.ds(first, NODE_ROWS), :] = load_split(ordered, first, NODE_ROWS).astype(BF16)

    layers.prepare(table_ref)
    spread_all(CORNERS)
    for offset in ENDS:
        now.arrive(offset)
        spread_all([offset])

    layers.gather(layers.buffers[0], 0, 0, layers.edges)

    def renew(first, count):
        here = pl.ds(first, count)
        renewed = node_layers(refs, table_ref, summed, here).astype(BF16)
        renewed_ref[here, :] = renewed
        projected = project(renewed, next_weight[...])
        next_projected[here, :] = projected
        return projected

    @pl.loop(0, blocks // 2)
    def _(pair):
        @pl.when(pair == marks[0])
        def _():
            next_boundary[...] = renew(0, boundary_rows)
            later.forward(CENTRE)

        for mark, offsets in zip(marks[1:], (FACES, ALONG, CORNERS)):

            @pl.when(pair == mark)
            def _():
                later.relay(offsets)

        for parity in range(2):
            block = 2 * pair + parity

            @pl.when(block < blocks + grid.place[0])
            def _():
                layers.one_block(block, parity, blocks - 1)

    part = even_part(rows - boundary_rows)

    @pl.loop(0, (rows - boundary_rows) // part)
    def _(i):
        renew(pl.multiple_of(boundary_rows + i * part, HALF), part)

    for offset in ENDS:
        later.arrive(offset)

    now.finish_sends()
    later.finish_sends()


def first_step(blocks, latent, arrived, digits, halo_rows, weights):
    local_rows, width = latent.shape
    rows = local_rows + arrived.shape[0]
    slots = digits.shape[0] // 2 - SPARE
    count = halo_rows.shape[0]
    first_pair = count // ROWS // 2
    rest = blocks // 2 - first_pair
    marks = (first_pair, first_pair + rest * 6 // 26, first_pair + rest * 7 // 26, first_pair + rest * 13 // 26)
    return pl.pallas_call(
        functools.partial(first_step_kernel, slots, blocks, marks),
        out_shape=(
            jax.ShapeDtypeStruct((rows, width), BF16),
            jax.ShapeDtypeStruct((rows, width), BF16),
            jax.ShapeDtypeStruct((27, count, width), BF16),
            jax.ShapeDtypeStruct((slots, rows), jnp.int32),
            jax.ShapeDtypeStruct((rows, HALF), F32),
            jax.ShapeDtypeStruct((1, rows), jnp.int32),
            jax.ShapeDtypeStruct((1,), jnp.int32),
        ),
        in_specs=[VMEM] * 4 + [SMEM] + [VMEM] * 10,
        out_specs=(VMEM, VMEM, ANYWHERE, VMEM, VMEM, VMEM, SMEM),
        scratch_shapes=edge_scratch(rows, slots, rows + 27 * count, width)
        + [
            pltpu.VMEM((27, count, width), BF16),
            pltpu.VMEM((count, width), BF16),
            pltpu.VMEM((count, width), BF16),
            pltpu.VMEM((2 * rows, HALF), F32),
            pltpu.VMEM((2 * rows, HALF), F32),
            pltpu.VMEM((rows, HALF), F32),
            pltpu.VMEM((rows, width), BF16),
            pltpu.VMEM((1, rows), jnp.int32),
            pltpu.SMEM((slots, rows), jnp.int32),
            pltpu.SMEM((1, rows), jnp.int32),
        ]
        + [pltpu.SemaphoreType.DMA((27,))] * 4
        + [pltpu.SemaphoreType.DMA((2,))],
        compiler_params=pltpu.CompilerParams(
            collective_id=0, has_side_effects=True, vmem_limit_bytes=VMEM_BYTES
        ),
        name="first_step",
    )(latent, arrived, digits, halo_rows[None, :], halo_rows, *weights)


def last_step_kernel(slots, *args):
    edge_ids, floor_ref, table_ref, projected_ref, ghosts = args[:5]
    place_ids, count_ref, live_count, leave_lanes, arrived_ref = args[5:10]
    weights = args[10:20]
    updated_ref = args[20]
    scratch = unpack_scratch(args[21:29])
    staged, ordered, sems = args[29:]
    refs = step_refs(1, edge_ids, floor_ref, weights)
    pairs, summed = scratch[0], scratch[3]
    rows, width = table_ref.shape
    local_rows = rows - arrived_ref.shape[0]
    ghost_blocks, ghost_rows = ghosts.shape[0], ghosts.shape[1]
    centre = ghost_blocks // 2
    layers = EdgeLayers(rows, slots, refs, scratch)

    def fetch(block):
        return pltpu.make_async_copy(ghosts.at[block], staged.at[block], sems.at[block])

    for block in range(ghost_blocks):
        if block != centre:
            fetch(block).start()
    layers.prepare(table_ref)

    @pl.loop(0, rows // NODE_ROWS)
    def _(i):
        first = pl.multiple_of(i * NODE_ROWS, NODE_ROWS)
        store_split(ordered, first, projected_ref[pl.ds(first, NODE_ROWS), :].astype(F32))

    copy_rows(ordered, place_ids.at[0], pairs, rows)

    @pl.loop(0, ghost_blocks)
    def _(block):
        @pl.when(block != centre)
        def _():
            fetch(block).wait()
            spread_block(pairs, pl.multiple_of(rows + block * ghost_rows, ghost_rows), staged.at[block])

    blocks = (count_ref[0] + ROWS - 1) // ROWS
    layers.gather(layers.buffers[0], 0, 0, layers.edges)

    @pl.loop(0, (blocks + 1) // 2)
    def _(pair):
        for parity in range(2):
            block = 2 * pair + parity

            @pl.when(block < blocks)
            def _():
                layers.one_block(block, parity, rows // ROWS - 1)

    part = even_part(rows)

    @pl.loop(0, rows // part)
    def _(i):
        first = pl.multiple_of(i * part, HALF)
        renewed = node_layers(refs, table_ref, summed, pl.ds(first, part))
        store_split(ordered, first, renewed)

    copy_rows(ordered, place_ids.at[0], pairs, rows)

    @pl.loop(0, local_rows // NODE_ROWS)
    def _(i):
        first = pl.multiple_of(i * NODE_ROWS, NODE_ROWS)
        row_ids = lax.broadcasted_iota(jnp.int32, (NODE_ROWS, leave_lanes.shape[1]), 0) + first
        leaves = jnp.max((row_ids == leave_lanes[...]).astype(F32), axis=1, keepdims=True)
        living = jnp.where(row_ids[:, :1] < live_count[0], 1.0 - leaves, 0.0)
        updated_ref[pl.ds(first, NODE_ROWS), :] = (load_split(pairs, first, NODE_ROWS) * living).astype(BF16)

    for first in range(0, rows - local_rows, NODE_ROWS):
        living = arrived_ref[pl.ds(first, NODE_ROWS), width : width + 1].astype(F32)
        updated_ref[pl.ds(local_rows + first, NODE_ROWS), :] = (
            load_split(pairs, local_rows + first, NODE_ROWS) * living
        ).astype(BF16)


def last_step(edge_ids, floor, table, projected, ghosts, place_ids, count, live_count, leave_rows, arrived, weights):
    rows, width = table.shape
    slots = edge_ids.shape[0]
    return pl.pallas_call(
        functools.partial(last_step_kernel, slots),
        out_shape=jax.ShapeDtypeStruct((rows, width), BF16),
        in_specs=[SMEM, VMEM, VMEM, VMEM, ANYWHERE, SMEM, SMEM, SMEM] + [VMEM] * 12,
        out_specs=VMEM,
        scratch_shapes=edge_scratch(rows, slots, rows + ghosts.shape[0] * ghosts.shape[1], width)
        + [
            pltpu.VMEM(ghosts.shape, BF16),
            pltpu.VMEM((2 * rows, HALF), F32),
            pltpu.SemaphoreType.DMA((ghosts.shape[0],)),
        ],
        compiler_params=pltpu.CompilerParams(vmem_limit_bytes=VMEM_BYTES),
        name="last_step",
    )(
        edge_ids,
        floor,
        table,
        projected,
        ghosts,
        place_ids,
        count,
        live_count,
        leave_rows[None, :],
        arrived,
        *weights,
    )


def pick_rows(source_rows, row_ids):
    selector = (
        row_ids[:, None] == jnp.arange(source_rows.shape[0], dtype=jnp.int32)[None, :]
    ).astype(source_rows.dtype)
    return jnp.dot(selector, source_rows, preferred_element_type=F32).astype(source_rows.dtype)


def local(
    latent,
    live_count,
    leave_rows,
    leave_target,
    halo_rows,
    neighbours,
    edge_in,
    edge_bias,
    edge_out,
    edge_shift,
    edge_gain,
    node_in,
    node_bias,
    node_out,
    node_shift,
    node_gain,
):
    axes = ("gx", "gy", "gz")
    devices = lax.axis_size(axes)
    local_rows, width = latent.shape
    table_rows, slots = neighbours.shape
    slots_total = table_rows - local_rows
    capacity = slots_total // devices
    leaving = leave_rows.shape[0]
    target_domain = leave_target[:, 0]
    entry = jnp.arange(leaving, dtype=jnp.int32)
    earlier = entry[None, :] < entry[:, None]
    same_target = target_domain[:, None] == target_domain[None, :]
    row_rank = jnp.sum(jnp.logical_and(same_target, earlier).astype(jnp.int32), axis=1)
    position = target_domain * capacity + row_rank
    moving = pick_rows(latent, leave_rows)
    moving = jnp.concatenate([moving, jnp.ones((leaving, HALF), BF16)], axis=1)
    placement = jnp.arange(slots_total, dtype=jnp.int32)[:, None] == position[None, :]
    outgoing = jnp.dot(placement.astype(BF16), moving, preferred_element_type=F32).astype(BF16)
    arrived = lax.all_to_all(
        outgoing.reshape(devices, capacity, width + HALF), axes, split_axis=0, concat_axis=0, tiled=True
    ).reshape(slots_total, width + HALF)
    weights = (
        edge_in,
        edge_bias,
        edge_out,
        edge_shift,
        edge_gain,
        node_in,
        node_bias,
        node_out,
        node_shift,
        node_gain,
    )
    blocks = (local_rows - leaving + slots_total) // ROWS
    table, projected, ghosts, edge_ids, floor, place_ids, count = first_step(
        blocks, latent, arrived, digits_of(neighbours), halo_rows, weights
    )
    return last_step(
        edge_ids, floor, table, projected, ghosts, place_ids, count, live_count, leave_rows, arrived, weights
    )


def solution(mesh):
    rows = P(("gx", "gy", "gz"))
    in_specs = (rows,) * 6 + (P(),) * 10
    return jax.shard_map(local, mesh=mesh, in_specs=in_specs, out_specs=rows, check_vma=False)
```

```python
import functools

import jax
import jax.numpy as jnp
from jax import lax
from jax.experimental import pallas as pl
from jax.experimental.pallas import tpu as pltpu
from jax.sharding import PartitionSpec as P

EPS = 1e-05
F32 = jnp.float32
BF16 = jnp.bfloat16
HALF = 128
ROWS = 32
CHUNK = 256
LAG = 2
GROUP = 8
NODE_ROWS = 256
SPARE = 8
AXES = ("gx", "gy", "gz")
MESH = pl.DeviceIdType.MESH
VMEM_BYTES = 58 * 2**20
VMEM = pl.BlockSpec(memory_space=pltpu.VMEM)
SMEM = pl.BlockSpec(memory_space=pltpu.SMEM)
ANYWHERE = pl.BlockSpec(memory_space=pl.ANY)


def even_part(count, most=1024):
    parts = -(-count // most)
    while count % (parts * HALF):
        parts += 1
    return count // parts


def layer_norm(values, feature_gain):
    average = jnp.mean(values, axis=-1, keepdims=True)
    centred = values - average
    spread = jnp.mean(centred * centred, axis=-1, keepdims=True)
    return centred * lax.rsqrt(spread + EPS) * feature_gain


def store_split(pairs, first_row, values):
    count = values.shape[0]
    pairs[pl.ds(2 * first_row, count, stride=2), :] = values[:, :HALF]
    pairs[pl.ds(2 * first_row + 1, count, stride=2), :] = values[:, HALF:]


def load_split(pairs, first_row, count):
    left = pairs[pl.ds(2 * first_row, count, stride=2), :]
    right = pairs[pl.ds(2 * first_row + 1, count, stride=2), :]
    return jnp.concatenate([left, right], axis=1)


def project(rows, weight):
    return jnp.dot(rows, weight, preferred_element_type=F32).astype(BF16)


def copy_rows(source, ids, into, count):
    @pl.loop(0, count // 64)
    def _(block):
        for g in range(64 // GROUP):
            some = ids.at[pl.ds(block * 64 + g * GROUP, GROUP)]
            for e in range(GROUP):
                place = pl.multiple_of(2 * (block * 64 + g * GROUP + e), 2)
                into[pl.ds(place, 2), :] = source[pl.ds(2 * some[e], 2), :]


def find_places(digits, halo_lanes, places, place_ref, count_ref):
    rows = digits.shape[1]
    half_rows = digits.shape[0] // 2
    slots = half_rows - SPARE
    boundary = halo_lanes.shape[1]
    n = NODE_ROWS
    lower = (
        lax.broadcasted_iota(jnp.int32, (n, n), 0) > lax.broadcasted_iota(jnp.int32, (n, n), 1)
    ).astype(BF16)
    lane = lax.broadcasted_iota(jnp.int32, (n, boundary), 1).astype(F32)

    def one_chunk(c, carry):
        used, spare = carry
        first = pl.multiple_of(c * n, n)
        here = pl.ds(first, n)
        largest = jnp.max(
            digits[pl.ds(0, slots), here].astype(F32) + digits[pl.ds(half_rows, slots), here].astype(F32),
            axis=0,
            keepdims=True,
        )
        active = jnp.transpose(jnp.broadcast_to(largest, (HALF, n))) > 0.0
        row_ids = lax.broadcasted_iota(jnp.int32, (n, boundary), 0) + first
        same = (row_ids == halo_lanes[...]).astype(F32)
        listed = jnp.sum(same, axis=1, keepdims=True) > 0.0
        position = jnp.sum(same * lane, axis=1, keepdims=True)
        others = jnp.where(listed, 0.0, jnp.where(active, 1.0, 0.0))
        idle = jnp.where(listed, 0.0, jnp.where(active, 0.0, 1.0))
        before = jnp.dot(lower, others.astype(BF16), preferred_element_type=F32) + used
        behind = jnp.dot(lower, idle.astype(BF16), preferred_element_type=F32) + spare
        place = jnp.where(others > 0.0, boundary + before, rows - 1 - behind)
        place = jnp.where(listed, position, place)
        places[here, :] = place
        place_ref[:, here] = jnp.transpose(place)[:1].astype(jnp.int32)
        return used + jnp.sum(others[:, :1]), spare + jnp.sum(idle[:, :1])

    used, _ = lax.fori_loop(0, rows // n, one_chunk, (jnp.float32(0.0), jnp.float32(0.0)), unroll=3)
    count_ref[0] = used.astype(jnp.int32) + boundary


def apply_places(senders, digits, places, edge_ids, floor_ref, order_ref):
    rows = digits.shape[1]
    half_rows = digits.shape[0] // 2
    slots = half_rows - SPARE
    n = NODE_ROWS

    @pl.loop(0, rows // n, unroll=3)
    def _(c):
        first = pl.multiple_of(c * n, n)
        lanes = lax.broadcasted_iota(jnp.int32, (n, HALF), 1).astype(F32)
        picked = jnp.zeros((2 * half_rows, n), F32)
        for part in range(rows // n):
            here = places[pl.ds(part * n, n), :]
            halves = [
                jnp.where(here == lanes + (first + half * HALF).astype(F32), 1.0, 0.0).astype(BF16)
                for half in range(n // HALF)
            ]
            chosen = jnp.concatenate(halves, axis=1)
            picked = picked + jnp.dot(digits[:, pl.ds(part * n, n)], chosen, preferred_element_type=F32)
        value = picked[:half_rows] * 128.0 + picked[half_rows:]
        here = pl.ds(first, n)
        edge_ids[:, here] = 2 * jnp.clip((value[:slots] - 1.0).astype(jnp.int32), 0, senders - 1)
        order_ref[:, here] = jnp.clip(value[slots : slots + 1].astype(jnp.int32), 0, rows - 1)
        floor = jnp.where(value > 0.5, EPS, jnp.inf).astype(F32)
        floor_ref[here, :] = jnp.transpose(jnp.concatenate([floor] * (HALF // half_rows), axis=0))


def digits_of(neighbours):
    rows, slots = neighbours.shape
    ids = jnp.concatenate(
        [neighbours.T + 1, jnp.arange(rows, dtype=jnp.int32)[None], jnp.zeros((SPARE - 1, rows), jnp.int32)]
    )
    return jnp.concatenate([ids // 128, ids % 128]).astype(BF16)


class Grid:
    def __init__(self):
        self.place = [lax.axis_index(a) for a in AXES]
        self.sizes = [lax.axis_size(a) for a in AXES]

    def inside(self, axis, step):
        return jnp.logical_and(self.place[axis] + step >= 0, self.place[axis] + step < self.sizes[axis])

    def target(self, axis, step):
        return tuple(self.place[a] + (step if a == axis else 0) for a in range(3))

    def present(self, offset):
        found = None
        for a in range(3):
            if offset[a] != 0:
                here = self.inside(a, offset[a])
                found = here if found is None else jnp.logical_and(found, here)
        return found

    def greet(self):
        barrier = pltpu.get_barrier_semaphore()
        friends = jnp.int32(0)
        for axis in range(3):
            for step in (-1, 1):
                friends = friends + self.inside(axis, step).astype(jnp.int32)

                @pl.when(self.inside(axis, step))
                def _():
                    pl.semaphore_signal(barrier, inc=1, device_id=self.target(axis, step), device_id_type=MESH)

        pl.semaphore_wait(barrier, friends)


def number(offset):
    return 9 * (offset[0] + 1) + 3 * (offset[1] + 1) + offset[2] + 1


def moved(offset, axis, step):
    return tuple(offset[a] + (step if a == axis else 0) for a in range(3))


CENTRE = (0, 0, 0)
OFFSETS = [(dx, dy, dz) for dx in (-1, 0, 1) for dy in (-1, 0, 1) for dz in (-1, 0, 1)]
ALONG = [o for o in OFFSETS if o[:2] == (0, 0) and o[2] != 0]
FACES = [o for o in OFFSETS if o[2] == 0 and abs(o[0]) + abs(o[1]) == 1]
CORNERS = [o for o in OFFSETS if o[2] == 0 and o[0] != 0 and o[1] != 0]
ENDS = [o for n in (1, 2) for o in OFFSETS if o[2] != 0 and abs(o[0]) + abs(o[1]) == n]


class Exchange:
    def __init__(self, grid, boundary, ghosts, send_sems, recv_sems):
        self.grid, self.boundary, self.ghosts = grid, boundary, ghosts
        self.send_sems, self.recv_sems = send_sems, recv_sems

    def copy(self, offset, axis, step):
        slot = number(moved(offset, axis, -step))
        return pltpu.make_async_remote_copy(
            src_ref=self.boundary if offset == CENTRE else self.ghosts.at[number(offset)],
            dst_ref=self.ghosts.at[slot],
            send_sem=self.send_sems.at[slot],
            recv_sem=self.recv_sems.at[slot],
            device_id=self.grid.target(axis, step),
            device_id_type=MESH,
        )

    def on_chip(self, step):
        return lax.rem(self.grid.place[2], 2) == (0 if step == 1 else 1)

    def last_hops(self, offset):
        dx, dy, dz = offset
        if dz == 0:
            if dx != 0 and dy != 0:
                return [(1 if dx == dy else 0, None)]
            return [(0 if dx != 0 else 1, None)]
        if (dx != 0) == (dy != 0):
            return [(2, None)]
        near = self.on_chip(dz)
        return [(2, near), (0 if dx != 0 else 1, jnp.logical_not(near))]

    def hops_from(self, offset):
        found = []
        for axis in range(3):
            if offset[axis] != 0:
                continue
            for step in (-1, 1):
                dx, dy, dz = reached = moved(offset, axis, -step)
                there = self.grid.inside(axis, step)
                if offset != CENTRE:
                    there = jnp.logical_and(there, self.grid.present(offset))
                if dz != 0 and (dx != 0) != (dy != 0):
                    near = self.on_chip(step if axis == 2 else dz)
                    there = jnp.logical_and(there, near if axis == 2 else jnp.logical_not(near))
                elif axis not in [a for a, _ in self.last_hops(reached)]:
                    continue
                found.append((axis, step, there))
        return found

    def forward(self, offset):
        for axis, step, there in self.hops_from(offset):

            @pl.when(there)
            def _():
                self.copy(offset, axis, step).start()

    def arrive(self, offset):
        for axis, condition in self.last_hops(offset):
            there = self.grid.present(offset)
            if condition is not None:
                there = jnp.logical_and(there, condition)

            @pl.when(there)
            def _():
                self.copy(moved(offset, axis, -offset[axis]), axis, -offset[axis]).wait_recv()

    def relay(self, offsets):
        for offset in offsets:
            self.arrive(offset)
            self.forward(offset)

    def finish_sends(self):
        for offset in [CENTRE] + ALONG + FACES + CORNERS:
            for axis, step, there in self.hops_from(offset):

                @pl.when(there)
                def _():
                    self.copy(offset, axis, step).wait_send()


class EdgeLayers:
    def __init__(self, rows, slots, refs, scratch):
        self.edge_ids, self.floor = refs["edge_ids"], refs["floor"]
        self.refs = refs
        self.rows, self.slots = rows, slots
        self.edges = slots * ROWS
        self.pairs, self.buffers, self.receive, self.summed, self.raw, self.square, self.weight = scratch
        self.width = self.receive.shape[1]

    def prepare(self, table_ref):
        refs = self.refs
        wide = refs["edge_out"][...].astype(F32)
        self.weight[...] = (wide - jnp.mean(wide, axis=1, keepdims=True)).astype(BF16)

        @pl.loop(0, self.rows // NODE_ROWS, unroll=3)
        def _(i):
            here = pl.ds(pl.multiple_of(i * NODE_ROWS, NODE_ROWS), NODE_ROWS)
            self.summed[here, :] = jnp.zeros((NODE_ROWS, self.width), F32)
            self.receive[here, :] = (
                jnp.dot(table_ref[here, :], refs["receive_weight"][...], preferred_element_type=F32)
                + refs["edge_bias"][...]
            )

    def gather(self, into, block, start, stop):
        first = pl.multiple_of(block * ROWS, ROWS)
        for e in range(start, stop):
            k, r = divmod(e, ROWS)
            if r % GROUP == 0:
                ids = self.edge_ids.at[k, pl.ds(first + r, GROUP)]
            into[pl.ds(2 * e, 2), :] = self.pairs[pl.ds(ids[r % GROUP], 2), :]

    def first_half(self, source, first, chunk, shift):
        per_chunk = CHUNK // ROWS
        own = self.receive[pl.ds(first, ROWS), :]
        left = source[pl.ds(2 * chunk * CHUNK, CHUNK, stride=2), :].reshape(per_chunk, ROWS, HALF)
        right = source[pl.ds(2 * chunk * CHUNK + 1, CHUNK, stride=2), :].reshape(per_chunk, ROWS, HALF)
        left = jnp.maximum(left + own[:, :HALF][None], 0.0).reshape(CHUNK, HALF).astype(BF16)
        right = jnp.maximum(right + own[:, HALF:][None], 0.0).reshape(CHUNK, HALF).astype(BF16)
        active = jnp.concatenate([left, right], axis=1)
        centred = jnp.dot(active, self.weight[...], preferred_element_type=F32) + shift
        total = jnp.sum(
            centred[:, :HALF] * centred[:, :HALF] + centred[:, HALF:] * centred[:, HALF:], axis=1, keepdims=True
        )
        here = pl.ds(chunk * CHUNK, CHUNK)
        self.raw[here, :] = centred
        self.square[here, :] = jnp.broadcast_to(total, (CHUNK, HALF))

    def second_half(self, floor, chunk, sums):
        left, right = sums
        per_chunk = CHUNK // ROWS
        for k in range(chunk * per_chunk, (chunk + 1) * per_chunk):
            here = pl.ds(k * ROWS, ROWS)
            scale = lax.rsqrt(self.square[here, :] * (1.0 / self.width) + floor[:, k : k + 1])
            left = left + self.raw[here, :HALF] * scale
            right = right + self.raw[here, HALF:] * scale
        return left, right

    def one_block(self, block, parity, last_block):
        chunks = self.edges // CHUNK
        first = pl.multiple_of(block * ROWS, ROWS)
        following = jnp.minimum(block + 1, last_block)
        edge_shift = self.refs["edge_shift"]
        shift = edge_shift[...] - jnp.mean(edge_shift[...], axis=1, keepdims=True)
        floor = self.floor[pl.ds(first, ROWS), :]
        sums = (jnp.zeros((ROWS, HALF), F32), jnp.zeros((ROWS, HALF), F32))
        for chunk in range(chunks + LAG):
            if chunk < chunks:
                self.gather(self.buffers[1 - parity], following, chunk * CHUNK, (chunk + 1) * CHUNK)
                self.first_half(self.buffers[parity], first, chunk, shift)
            if chunk >= LAG:
                sums = self.second_half(floor, chunk - LAG, sums)
        self.summed[pl.ds(first, ROWS), :HALF] = sums[0]
        self.summed[pl.ds(first, ROWS), HALF:] = sums[1]


def node_layers(refs, table_ref, summed, here):
    own = table_ref[here, :]
    message = (summed[here, :] * refs["edge_gain"][...]).astype(BF16)
    hidden = (
        jnp.dot(own, refs["node_self"][...], preferred_element_type=F32)
        + jnp.dot(message, refs["node_message"][...], preferred_element_type=F32)
        + refs["node_bias"][...]
    )
    hidden = jnp.maximum(hidden, 0.0).astype(BF16)
    node_raw = jnp.dot(hidden, refs["node_out"][...], preferred_element_type=F32) + refs["node_shift"][...]
    return own.astype(F32) + layer_norm(node_raw, refs["node_gain"][...])


def step_refs(t, edge_ids, floor, weights):
    edge_in, edge_bias, edge_out, edge_shift, edge_gain, node_in, node_bias, node_out, node_shift, node_gain = weights
    row = pl.ds(t, 1)
    return {
        "edge_ids": edge_ids,
        "floor": floor,
        "receive_weight": edge_in.at[t, 0],
        "edge_bias": edge_bias.at[row],
        "edge_out": edge_out.at[t],
        "edge_shift": edge_shift.at[row],
        "edge_gain": edge_gain.at[row],
        "node_self": node_in.at[t, 0],
        "node_message": node_in.at[t, 1],
        "node_bias": node_bias.at[row],
        "node_out": node_out.at[t],
        "node_shift": node_shift.at[row],
        "node_gain": node_gain.at[row],
    }


def edge_scratch(rows, slots, senders, width):
    edges = slots * ROWS
    return [
        pltpu.VMEM((2 * senders, HALF), F32),
        pltpu.VMEM((2 * edges, HALF), F32),
        pltpu.VMEM((2 * edges, HALF), F32),
        pltpu.VMEM((rows, width), F32),
        pltpu.VMEM((rows, width), F32),
        pltpu.VMEM((edges, width), F32),
        pltpu.VMEM((edges, HALF), F32),
        pltpu.VMEM((width, width), BF16),
    ]


def unpack_scratch(scratch):
    pairs, even, odd, receive, summed, raw, square, weight = scratch
    return pairs, (even, odd), receive, summed, raw, square, weight


def spread_block(pairs, first_row, block_ref):
    @pl.loop(0, block_ref.shape[0] // 128)
    def _(piece):
        start = pl.multiple_of(piece * 128, 128)
        store_split(pairs, first_row + start, block_ref[pl.ds(start, 128), :].astype(F32))


def first_step_kernel(slots, blocks, marks, *args):
    latent_ref, arrived_ref, digits, halo_lanes, halo_ids = args[:5]
    weights = args[5:15]
    renewed_ref, next_projected, next_ghosts, edge_lanes, floor_ref, place_ref, count_ref = args[15:22]
    scratch = unpack_scratch(args[22:30])
    (
        ghosts,
        boundary_ref,
        next_boundary,
        original,
        ordered,
        places,
        table_ref,
        order_lanes,
        edge_ids,
        order_ids,
        send_a,
        recv_a,
        send_b,
        recv_b,
        id_sems,
    ) = args[30:]
    pairs, summed = scratch[0], scratch[3]
    local_rows, width = latent_ref.shape
    arrivals = arrived_ref.shape[0]
    rows = local_rows + arrivals
    boundary_rows = boundary_ref.shape[0]
    refs = step_refs(0, edge_ids, floor_ref, weights)
    send_weight, next_weight = weights[0].at[0, 1], weights[0].at[1, 1]
    grid = Grid()
    now = Exchange(grid, boundary_ref, ghosts, send_a, recv_a)
    later = Exchange(grid, next_boundary, next_ghosts, send_b, recv_b)
    layers = EdgeLayers(rows, slots, refs, scratch)
    grid.greet()

    def sources(take):
        @pl.loop(0, local_rows // NODE_ROWS)
        def _(i):
            first = pl.multiple_of(i * NODE_ROWS, NODE_ROWS)
            take(first, latent_ref[pl.ds(first, NODE_ROWS), :])

        for first in range(0, arrivals, NODE_ROWS):
            take(local_rows + first, arrived_ref[pl.ds(first, NODE_ROWS), :width])

    sources(lambda first, values: store_split(original, first, values.astype(F32)))
    copy_rows(original, halo_ids, ordered, boundary_rows)
    for first in range(0, boundary_rows, NODE_ROWS):
        values = load_split(ordered, first, NODE_ROWS).astype(BF16)
        boundary_ref[pl.ds(first, NODE_ROWS), :] = project(values, send_weight[...])
    now.forward(CENTRE)
    sources(lambda first, values: store_split(pairs, first, project(values, send_weight[...]).astype(F32)))
    find_places(digits, halo_lanes, places, place_ref, count_ref)

    def spread(offset):
        spread_block(pairs, rows + number(offset) * boundary_rows, ghosts.at[number(offset)])

    def spread_all(offsets):
        for offset in offsets:

            @pl.when(grid.present(offset))
            def _():
                spread(offset)

    now.relay(FACES)
    now.relay(ALONG)
    apply_places(pairs.shape[0] // 2, digits, places, edge_lanes, floor_ref, order_lanes)
    fetch_edges = pltpu.make_async_copy(edge_lanes, edge_ids, id_sems.at[0])
    fetch_order = pltpu.make_async_copy(order_lanes, order_ids, id_sems.at[1])
    fetch_edges.start()
    fetch_order.start()
    now.relay(CORNERS)
    spread_all(ALONG)
    spread_all(FACES)
    fetch_edges.wait()
    fetch_order.wait()
    copy_rows(original, order_ids.at[0], ordered, rows)

    @pl.loop(0, rows // NODE_ROWS)
    def _(i):
        first = pl.multiple_of(i * NODE_ROWS, NODE_ROWS)
        table_ref[pl.ds(first, NODE_ROWS), :] = load_split(ordered, first, NODE_ROWS).astype(BF16)

    layers.prepare(table_ref)
    spread_all(CORNERS)
    for offset in ENDS:
        now.arrive(offset)
        spread_all([offset])

    layers.gather(layers.buffers[0], 0, 0, layers.edges)

    def renew(first, count):
        here = pl.ds(first, count)
        renewed = node_layers(refs, table_ref, summed, here).astype(BF16)
        renewed_ref[here, :] = renewed
        projected = project(renewed, next_weight[...])
        next_projected[here, :] = projected
        return projected

    @pl.loop(0, blocks // 2)
    def _(pair):
        @pl.when(pair == marks[0])
        def _():
            next_boundary[...] = renew(0, boundary_rows)
            later.forward(CENTRE)

        for mark, offsets in zip(marks[1:], (FACES, ALONG, CORNERS)):

            @pl.when(pair == mark)
            def _():
                later.relay(offsets)

        for parity in range(2):
            block = 2 * pair + parity

            @pl.when(block < blocks + grid.place[0])
            def _():
                layers.one_block(block, parity, blocks - 1)

    part = even_part(rows - boundary_rows)

    @pl.loop(0, (rows - boundary_rows) // part)
    def _(i):
        renew(pl.multiple_of(boundary_rows + i * part, HALF), part)

    for offset in ENDS:
        later.arrive(offset)

    now.finish_sends()
    later.finish_sends()


def first_step(blocks, latent, arrived, digits, halo_rows, weights):
    local_rows, width = latent.shape
    rows = local_rows + arrived.shape[0]
    slots = digits.shape[0] // 2 - SPARE
    count = halo_rows.shape[0]
    first_pair = count // ROWS // 2
    rest = blocks // 2 - first_pair
    marks = (first_pair, first_pair + rest * 8 // 26, first_pair + rest * 9 // 26, first_pair + rest * 15 // 26)
    return pl.pallas_call(
        functools.partial(first_step_kernel, slots, blocks, marks),
        out_shape=(
            jax.ShapeDtypeStruct((rows, width), BF16),
            jax.ShapeDtypeStruct((rows, width), BF16),
            jax.ShapeDtypeStruct((27, count, width), BF16),
            jax.ShapeDtypeStruct((slots, rows), jnp.int32),
            jax.ShapeDtypeStruct((rows, HALF), F32),
            jax.ShapeDtypeStruct((1, rows), jnp.int32),
            jax.ShapeDtypeStruct((1,), jnp.int32),
        ),
        in_specs=[VMEM] * 4 + [SMEM] + [VMEM] * 10,
        out_specs=(VMEM, VMEM, ANYWHERE, VMEM, VMEM, VMEM, SMEM),
        scratch_shapes=edge_scratch(rows, slots, rows + 27 * count, width)
        + [
            pltpu.VMEM((27, count, width), BF16),
            pltpu.VMEM((count, width), BF16),
            pltpu.VMEM((count, width), BF16),
            pltpu.VMEM((2 * rows, HALF), F32),
            pltpu.VMEM((2 * rows, HALF), F32),
            pltpu.VMEM((rows, HALF), F32),
            pltpu.VMEM((rows, width), BF16),
            pltpu.VMEM((1, rows), jnp.int32),
            pltpu.SMEM((slots, rows), jnp.int32),
            pltpu.SMEM((1, rows), jnp.int32),
        ]
        + [pltpu.SemaphoreType.DMA((27,))] * 4
        + [pltpu.SemaphoreType.DMA((2,))],
        compiler_params=pltpu.CompilerParams(
            collective_id=0, has_side_effects=True, vmem_limit_bytes=VMEM_BYTES
        ),
        name="first_step",
    )(latent, arrived, digits, halo_rows[None, :], halo_rows, *weights)


def last_step_kernel(slots, *args):
    edge_ids, floor_ref, table_ref, projected_ref, ghosts = args[:5]
    place_ids, count_ref, live_count, leave_lanes, arrived_ref = args[5:10]
    weights = args[10:20]
    updated_ref = args[20]
    scratch = unpack_scratch(args[21:29])
    staged, ordered, sems = args[29:]
    refs = step_refs(1, edge_ids, floor_ref, weights)
    pairs, summed = scratch[0], scratch[3]
    rows, width = table_ref.shape
    local_rows = rows - arrived_ref.shape[0]
    ghost_blocks, ghost_rows = ghosts.shape[0], ghosts.shape[1]
    centre = ghost_blocks // 2
    layers = EdgeLayers(rows, slots, refs, scratch)

    def fetch(block):
        return pltpu.make_async_copy(ghosts.at[block], staged.at[block], sems.at[block])

    for block in range(ghost_blocks):
        if block != centre:
            fetch(block).start()
    layers.prepare(table_ref)

    @pl.loop(0, rows // NODE_ROWS)
    def _(i):
        first = pl.multiple_of(i * NODE_ROWS, NODE_ROWS)
        store_split(ordered, first, projected_ref[pl.ds(first, NODE_ROWS), :].astype(F32))

    copy_rows(ordered, place_ids.at[0], pairs, rows)

    @pl.loop(0, ghost_blocks)
    def _(block):
        @pl.when(block != centre)
        def _():
            fetch(block).wait()
            spread_block(pairs, pl.multiple_of(rows + block * ghost_rows, ghost_rows), staged.at[block])

    blocks = (count_ref[0] + ROWS - 1) // ROWS
    layers.gather(layers.buffers[0], 0, 0, layers.edges)

    @pl.loop(0, (blocks + 1) // 2)
    def _(pair):
        for parity in range(2):
            block = 2 * pair + parity

            @pl.when(block < blocks)
            def _():
                layers.one_block(block, parity, rows // ROWS - 1)

    part = even_part(rows)

    @pl.loop(0, rows // part)
    def _(i):
        first = pl.multiple_of(i * part, HALF)
        renewed = node_layers(refs, table_ref, summed, pl.ds(first, part))
        store_split(ordered, first, renewed)

    copy_rows(ordered, place_ids.at[0], pairs, rows)

    @pl.loop(0, local_rows // NODE_ROWS)
    def _(i):
        first = pl.multiple_of(i * NODE_ROWS, NODE_ROWS)
        row_ids = lax.broadcasted_iota(jnp.int32, (NODE_ROWS, leave_lanes.shape[1]), 0) + first
        leaves = jnp.max((row_ids == leave_lanes[...]).astype(F32), axis=1, keepdims=True)
        living = jnp.where(row_ids[:, :1] < live_count[0], 1.0 - leaves, 0.0)
        updated_ref[pl.ds(first, NODE_ROWS), :] = (load_split(pairs, first, NODE_ROWS) * living).astype(BF16)

    for first in range(0, rows - local_rows, NODE_ROWS):
        living = arrived_ref[pl.ds(first, NODE_ROWS), width : width + 1].astype(F32)
        updated_ref[pl.ds(local_rows + first, NODE_ROWS), :] = (
            load_split(pairs, local_rows + first, NODE_ROWS) * living
        ).astype(BF16)


def last_step(edge_ids, floor, table, projected, ghosts, place_ids, count, live_count, leave_rows, arrived, weights):
    rows, width = table.shape
    slots = edge_ids.shape[0]
    return pl.pallas_call(
        functools.partial(last_step_kernel, slots),
        out_shape=jax.ShapeDtypeStruct((rows, width), BF16),
        in_specs=[SMEM, VMEM, VMEM, VMEM, ANYWHERE, SMEM, SMEM, SMEM] + [VMEM] * 12,
        out_specs=VMEM,
        scratch_shapes=edge_scratch(rows, slots, rows + ghosts.shape[0] * ghosts.shape[1], width)
        + [
            pltpu.VMEM(ghosts.shape, BF16),
            pltpu.VMEM((2 * rows, HALF), F32),
            pltpu.SemaphoreType.DMA((ghosts.shape[0],)),
        ],
        compiler_params=pltpu.CompilerParams(vmem_limit_bytes=VMEM_BYTES),
        name="last_step",
    )(
        edge_ids,
        floor,
        table,
        projected,
        ghosts,
        place_ids,
        count,
        live_count,
        leave_rows[None, :],
        arrived,
        *weights,
    )


def pick_rows(source_rows, row_ids):
    selector = (
        row_ids[:, None] == jnp.arange(source_rows.shape[0], dtype=jnp.int32)[None, :]
    ).astype(source_rows.dtype)
    return jnp.dot(selector, source_rows, preferred_element_type=F32).astype(source_rows.dtype)


def local(
    latent,
    live_count,
    leave_rows,
    leave_target,
    halo_rows,
    neighbours,
    edge_in,
    edge_bias,
    edge_out,
    edge_shift,
    edge_gain,
    node_in,
    node_bias,
    node_out,
    node_shift,
    node_gain,
):
    axes = ("gx", "gy", "gz")
    devices = lax.axis_size(axes)
    local_rows, width = latent.shape
    table_rows, slots = neighbours.shape
    slots_total = table_rows - local_rows
    capacity = slots_total // devices
    leaving = leave_rows.shape[0]
    target_domain = leave_target[:, 0]
    entry = jnp.arange(leaving, dtype=jnp.int32)
    earlier = entry[None, :] < entry[:, None]
    same_target = target_domain[:, None] == target_domain[None, :]
    row_rank = jnp.sum(jnp.logical_and(same_target, earlier).astype(jnp.int32), axis=1)
    position = target_domain * capacity + row_rank
    moving = pick_rows(latent, leave_rows)
    moving = jnp.concatenate([moving, jnp.ones((leaving, HALF), BF16)], axis=1)
    placement = jnp.arange(slots_total, dtype=jnp.int32)[:, None] == position[None, :]
    outgoing = jnp.dot(placement.astype(BF16), moving, preferred_element_type=F32).astype(BF16)
    arrived = lax.all_to_all(
        outgoing.reshape(devices, capacity, width + HALF), axes, split_axis=0, concat_axis=0, tiled=True
    ).reshape(slots_total, width + HALF)
    weights = (
        edge_in,
        edge_bias,
        edge_out,
        edge_shift,
        edge_gain,
        node_in,
        node_bias,
        node_out,
        node_shift,
        node_gain,
    )
    blocks = (local_rows - leaving + slots_total) // ROWS
    table, projected, ghosts, edge_ids, floor, place_ids, count = first_step(
        blocks, latent, arrived, digits_of(neighbours), halo_rows, weights
    )
    return last_step(
        edge_ids, floor, table, projected, ghosts, place_ids, count, live_count, leave_rows, arrived, weights
    )


def solution(mesh):
    rows = P(("gx", "gy", "gz"))
    in_specs = (rows,) * 6 + (P(),) * 10
    return jax.shard_map(local, mesh=mesh, in_specs=in_specs, out_specs=rows, check_vma=False)
```
